512 devices in a mesh: agg: 64 (over x, z, core), grp: 8 (over y).
Axes of the slice: x: 4, y: 8, z: 8, core: 2. Of those that a mesh axis runs over, the one named last changes fastest.
Arguments:
- pressure_rhs: float32 [512, 128, 512], P('agg', 'grp'), may hold values from -6 to 6
- cell_shift: float32 [512, 128, 512], P('agg', 'grp'), may hold values from 0.05 to 3
- fluid_mask: int32 [512, 128, 512], P('agg', 'grp'), may hold values 0 or 1
- coarse_shift: float32 [128, 32, 128], P('agg', 'grp'), may hold values from 0.05 to 3
- coarse_inverse: float32 [4096, 4096], P('agg', 'grp'), may hold values from -0.2 to 1.7
Outputs:
- pressure: float32 [512, 128, 512], P('agg', 'grp')
The draws below stay inside these ranges and needn't reach their ends.
All inputs are finite; a program needn't handle non-finite values. No bound on the sum of `fluid_mask` on one device may be relied on, other than what follows from the above.
Results may differ from the reference program's by a relative error of at most 0.00018.
Values sent between devices are 32-bit elements; how exact they have to be, the bound alone decides.
No kernel may reach another device: no remote copies, remote signals or barrier semaphores. Data moves between devices by JAX's collectives and lax.ppermute only.
A program may use at most 64 MiB of HBM per device.

```python
import math
import jax
import jax.numpy as jnp
from jax import lax

CZ = 512
NX = 512
NY = 128
NX1 = 128
NY1 = 32
NZ1 = 128
NCO = 4096


def draw_coarse_inverse(key, part):
    key_off, key_diag = jax.random.split(jax.random.fold_in(key, 11))
    offdiag = jax.random.normal(key_off, (NCO, NCO), jnp.float32) * (0.5 / NCO ** 0.5)
    offdiag = jnp.clip(offdiag, -0.15, 0.15)
    diagonal = jax.random.uniform(key_diag, (NCO,), jnp.float32, 0.5, 1.5)
    rows = lax.broadcasted_iota(jnp.int32, (NCO, NCO), 0)
    columns = lax.broadcasted_iota(jnp.int32, (NCO, NCO), 1)
    return jnp.where(rows == columns, diagonal[None, :], offdiag)


def place_ends(array, rng, low, largest):
    place = [jax.random.randint(jax.random.fold_in(rng, axis), (), 0, length) for axis, length in enumerate(array.shape)]
    main_axis = array.shape.index(max(array.shape))
    next_to = place[:main_axis] + [(place[main_axis] + 1) % array.shape[main_axis]] + place[main_axis + 1:]
    return array.at[tuple(place)].set(low).at[tuple(next_to)].set(largest)


def level_of(own_key, shape, shards, smallest, largest):
    factor_of = 1.0
    for axis_at, parts in shards:
        heights = jax.random.uniform(jax.random.fold_in(jax.random.fold_in(own_key, 6), axis_at), (parts,), jnp.float32, smallest / len(shards), largest / len(shards))
        factor_of = factor_of * jnp.repeat(jnp.exp(heights), shape[axis_at] // parts).reshape((-1,) + (1,) * (len(shape) - 1 - axis_at))
    return factor_of


def noise(key, shape, deviation, reach, shards=(), dtype=jnp.bfloat16):
    entries = jax.random.normal(key, shape, jnp.float32) * deviation
    if len(shards) > 0:
        entries = level_of(key, shape, shards, -0.22, 0.18) * entries
    return jnp.clip(entries, min=-reach, max=reach).astype(dtype)


def setup_inputs(seed: int = 0) -> dict:
    splits = jax.random.split(jax.random.key(seed), 6)
    return {
        "pressure_rhs": noise(splits[0], (NX, NY, CZ), 1.0, 6.0, ((0, 64), (1, 8)), jnp.float32),
        "cell_shift": jnp.clip(jnp.exp(math.log(3.0) - 4.0943445 * jax.random.uniform(splits[1], (NX, NY, CZ), jnp.float32) ** level_of(splits[1], (NX, NY, CZ), ((0, 64), (1, 8)), -0.2, 0.2)), 0.05, 3.0),
        "fluid_mask": place_ends((jax.random.randint(splits[2], (NX, NY, CZ), 0, 8) < 7).astype(jnp.int32), jax.random.fold_in(splits[2], 1), 0, 1),
        "coarse_shift": jnp.clip(jnp.exp(math.log(3.0) - 4.0943445 * jax.random.uniform(splits[3], (NX1, NY1, NZ1), jnp.float32) ** level_of(splits[3], (NX1, NY1, NZ1), ((0, 64), (1, 8)), -0.2, 0.2)), 0.05, 3.0),
        "coarse_inverse": draw_coarse_inverse(jax.random.fold_in(splits[5], 71), 0),
    }


first_weight = 0.5735
second_weight = 1.9751


def neighbours(field):
    padded = jnp.pad(field, 1)
    total = padded[2:, 1:-1, 1:-1] + padded[:-2, 1:-1, 1:-1]
    total = total + padded[1:-1, 2:, 1:-1] + padded[1:-1, :-2, 1:-1]
    return total + padded[1:-1, 1:-1, 2:] + padded[1:-1, 1:-1, :-2]


def restrict(field):
    a, b, c = field.shape
    return field.reshape(a // 4, 4, b // 4, 4, c // 4, 4).sum(axis=(1, 3, 5))


def prolong(field):
    a, b, c = field.shape
    wide = jnp.broadcast_to(field[:, None, :, None, :, None], (a, 4, b, 4, c, 4))
    return wide.reshape(a * 4, b * 4, c * 4)


def reference(pressure_rhs, cell_shift, fluid_mask, coarse_shift, coarse_inverse):
    fluid = fluid_mask.astype(jnp.float32)
    diag = 6.0 + cell_shift
    cdiag = 6.0 + coarse_shift

    def fine_apply(field):
        return diag * field - fluid * neighbours(field * fluid)

    def coarse_apply(field):
        return cdiag * field - neighbours(field)

    pre = first_weight * pressure_rhs / diag
    pre = pre + second_weight * (pressure_rhs - fine_apply(pre)) / diag
    agg_rhs = restrict(pressure_rhs - fine_apply(pre))
    agg_fix = first_weight * agg_rhs / cdiag
    agg_fix = agg_fix + second_weight * (agg_rhs - coarse_apply(agg_fix)) / cdiag
    agg_residual = agg_rhs - coarse_apply(agg_fix)
    line_rhs = agg_residual.sum(axis=0).reshape(-1)
    line_fix = jnp.dot(coarse_inverse, line_rhs, precision=lax.Precision.HIGHEST)
    agg_fix = agg_fix + line_fix.reshape(agg_residual.shape[1:])[None]
    mid = pre + prolong(agg_fix)
    mid = mid + first_weight * (pressure_rhs - fine_apply(mid)) / diag
    return mid + second_weight * (pressure_rhs - fine_apply(mid)) / diag
```

```python
import functools
import jax
import jax.numpy as jnp
import numpy as np
from jax import lax
from jax.experimental import pallas as pl
from jax.experimental.pallas import tpu as pltpu
from jax.sharding import Mesh, PartitionSpec as P

c1 = 0.5735
c2 = 1.9751
alpha = c1 + c2 - c1 * c2
beta = c1 * c2
AGG = ("x", "zhi", "zlo", "core")

VM = pl.BlockSpec(memory_space=pltpu.VMEM)
SM = pl.BlockSpec(memory_space=pltpu.SMEM)
HIGH = lax.Precision.HIGHEST

ROWS = (
    [("w", 1, p) for p in range(-2, 10)]
    + [("w", 2, p) for p in range(-1, 9)]
    + [("w", 3, p) for p in range(0, 8)]
    + [("g", 1, p) for p in range(-1, 9)]
    + [("g", 2, p) for p in range(0, 8)]
)


def shape(*dims):
    return jax.ShapeDtypeStruct(dims, jnp.float32)


def call(body, outs, scratch=()):
    return pl.pallas_call(
        body,
        out_shape=outs,
        scratch_shapes=list(scratch),
        compiler_params=pltpu.CompilerParams(vmem_limit_bytes=40 * 1024 * 1024),
    )


def plane_rows(field, p):
    base = {"w": 0, "g": 3}[field]
    if p < 0:
        return "lo", (base + p + (3 if field == "w" else 2)) * 16
    return "hi", (base + p - 8) * 16


def k1(rhs, shift, mask, cshift, w, g, h, up, down):
    for p in range(8):
        gp = mask[p].astype(jnp.float32) / (6.0 + shift[p])
        wp = rhs[p] * gp
        w[p] = wp
        g[p] = gp
        if p >= 5:
            up[(p - 5) * 16:(p - 4) * 16] = wp
        if p >= 6:
            up[(p - 3) * 16:(p - 2) * 16] = gp
        if p < 3:
            down[p * 16:(p + 1) * 16] = wp
        if p < 2:
            down[(p + 3) * 16:(p + 4) * 16] = gp
    h[...] = jnp.zeros((2, 8, 128), jnp.float32)
    for x in range(2):
        h[x, 2:6, :] = 1.0 / (6.0 + cshift[x])
    up[80:88, 0:128] = h[1]
    down[80:88, 0:128] = h[0]
    up[80:88, 128:512] = jnp.zeros((8, 384), jnp.float32)
    down[80:88, 128:512] = jnp.zeros((8, 384), jnp.float32)


def k2(w, g, lo, hi, h, up, down):
    own = {"w": w, "g": g}
    sides = {"lo": lo, "hi": hi}
    for k, (field, d, p) in enumerate(ROWS):
        for out, row in ((up, 16 - d), (down, d - 1)):
            if 0 <= p < 8:
                out[k:k + 1] = own[field][p, row:row + 1, :]
            else:
                side, base = plane_rows(field, p)
                out[k:k + 1] = sides[side][base + row:base + row + 1, :]
    for out in (up, down):
        out[48:56, 0:128] = h[0]
        out[48:56, 128:256] = h[1]
        out[48:56, 256:512] = jnp.zeros((8, 256), jnp.float32)


def fine_sum(ref, p, first, last):
    c = ref[p]
    total = ref[p - 1] + ref[p + 1]
    total = total + pltpu.roll(c, 1, 0) + pltpu.roll(c, 31, 0)
    total = total + jnp.where(first, 0.0, pltpu.roll(c, 1, 1))
    return total + jnp.where(last, 0.0, pltpu.roll(c, 511, 1))


def edges(dims):
    lane = lax.broadcasted_iota(jnp.int32, dims, 1)
    return lane == 0, lane == dims[1] - 1


def line_sides(c, first, last):
    total = jnp.where(first, 0.0, pltpu.roll(c, 1, 1))
    return total + jnp.where(last, 0.0, pltpu.roll(c, 127, 1))


def column_sides(c):
    return pltpu.roll(c, 1, 0) + pltpu.roll(c, 7, 0)


def k3(w, g, xlo, xhi, ylo, yhi, h, rhs, W, G, F, u, L, V):
    sides = {"lo": xlo, "hi": xhi}
    own = {"w": w, "g": g}
    wide = {"w": W, "g": G}
    zero = jnp.zeros((8, 512), jnp.float32)
    for field in ("w", "g"):
        for i in range(14):
            p = i - 3
            out = wide[field]
            out[i, 0:8, :] = zero
            out[i, 24:32, :] = zero
            if 0 <= p < 8:
                out[i, 8:24, :] = own[field][p]
            elif field == "g" and (p < -2 or p > 9):
                out[i, 8:16, :] = zero
                out[i, 16:24, :] = zero
            else:
                side, base = plane_rows(field, p)
                out[i, 8:24, :] = sides[side][base:base + 16, :]
    for k, (field, d, p) in enumerate(ROWS):
        wide[field][p + 3, 8 - d:9 - d, :] = ylo[k:k + 1]
        wide[field][p + 3, 23 + d:24 + d, :] = yhi[k:k + 1]
    first, last = edges((32, 512))
    for i in range(1, 13):
        wi = W[i]
        fp = alpha * wi + (beta * G[i]) * fine_sum(W, i, first, last)
        F[i] = fp
        V[i] = fp - beta * wi
    sums = []
    for x in range(2):
        total = None
        for p in range(4 * x, 4 * x + 4):
            s = fine_sum(V, p + 3, first, last)[8:24]
            r = (1.0 - alpha) * rhs[p] + jnp.where(g[p] > 0.0, s, 0.0)
            total = r if total is None else total + r
        sums.append(total)
    both = jnp.concatenate(sums, axis=0)
    cell = lax.broadcasted_iota(jnp.int32, (512, 128), 0)
    agg = lax.broadcasted_iota(jnp.int32, (512, 128), 1)
    thin = jnp.dot(both, (cell // 4 == agg).astype(jnp.float32), precision=HIGH)
    row = lax.broadcasted_iota(jnp.int32, (16, 32), 0)
    col = lax.broadcasted_iota(jnp.int32, (16, 32), 1)
    x_of, y_of = row // 8, row % 8 - 2
    take = (col // 16 == x_of) & ((col % 16) // 4 == y_of) & (y_of >= 0) & (y_of < 4)
    tiles = jnp.dot(take.astype(jnp.float32), thin, precision=HIGH)
    r = (tiles[0:8], tiles[8:16])
    four = lax.broadcasted_iota(jnp.int32, (8, 128), 0)
    first, last = edges((8, 128))
    lo, hi = xlo[80:88, 0:128], xhi[80:88, 0:128]
    hx = (lo + h[1], h[0] + hi)
    us, hs = [], []
    for x in range(2):
        us.append(r[x] * h[x])
        below = pltpu.roll(ylo[48:56, 128 * x:128 * x + 128], 4, 0)
        above = pltpu.roll(yhi[48:56, 128 * x:128 * x + 128], 4, 0)
        hs.append(h[x] + jnp.where(four == 1, below, 0.0) + jnp.where(four == 6, above, 0.0))
        u[x] = us[x]
    q = jnp.zeros((8, 128), jnp.float32)
    flat = []
    for x in range(2):
        side = line_sides(us[x], first, last) + column_sides(us[x])
        q = q + (alpha - beta) * us[x] + beta * (hx[x] * us[x] + hs[x] * side)
        flat.append((alpha - beta) * us[x] + beta * hs[x] * (us[1 - x] + side))
    total = 2.0 * q + line_sides(q, first, last) + column_sides(q) + (1.0 - alpha) * (r[0] + r[1])
    total = total - jnp.where(jnp.broadcast_to(lo[2:3], (8, 128)) > 0.0, 0.0, flat[0])
    total = total - jnp.where(jnp.broadcast_to(hi[2:3], (8, 128)) > 0.0, 0.0, flat[1])
    for i in range(64):
        L[i] = total


def k4(lines, inv, lo, hi, out):
    s = lines[0]
    for i in range(1, 64):
        s = s + lines[i]
    parts = []
    for i in range(8):
        t = jnp.zeros((8, 128), jnp.float32)
        for k in range(8):
            if k < 2:
                c = lo[10 + 8 * k + i]
            elif k < 6:
                c = inv[8 * i:8 * i + 8, 128 * (k - 2):128 * (k - 1)]
            else:
                c = hi[10 + 8 * (k - 6) + i]
            t = t + c * s[k:k + 1]
        parts.append(t)
    parts.append(jnp.zeros((64, 128), jnp.float32))
    table = jnp.concatenate(parts, axis=0)
    out[...] = lax.dot_general(
        jnp.ones((8, 128), jnp.float32), table, (((1,), (1,)), ((), ())), precision=HIGH
    )


def k5(place, blocks, out):
    b = blocks[...]
    row = lax.broadcasted_iota(jnp.int32, (8, 128), 0)
    after = jnp.where(row == 7, 0.0, pltpu.roll(b, 7, 0))
    before = jnp.where(row == 0, 0.0, pltpu.roll(b, 1, 0))
    z = b + pltpu.roll(jnp.where(place[0] == 0, after, before), 64, 1)
    for i in range(8):
        out[8 * i:8 * i + 8] = z


def k6(terms, W, G, F, u, h, xlo, xhi, ylo, yhi, rhs, shift, out, U0, U1):
    rows = [jnp.sum(terms[8 * j:8 * j + 8], axis=0, keepdims=True) for j in range(8)]
    m = jnp.concatenate(rows, axis=0)
    rolled = pltpu.roll(m, 64, 1)
    low = lax.broadcasted_iota(jnp.int32, (1, 128), 1) < 64
    fix = [jnp.zeros((1, 128), jnp.float32), jnp.where(low, rolled[6:7], m[7:8])]
    for j in range(4):
        fix.append(jnp.where(low, m[2 * j:2 * j + 1], rolled[2 * j + 1:2 * j + 2]))
    fix += [jnp.where(low, rolled[0:1], m[1:2]), jnp.zeros((1, 128), jnp.float32)]
    fix = jnp.concatenate(fix, axis=0)
    four = lax.broadcasted_iota(jnp.int32, (8, 128), 0)
    first, last = edges((8, 128))

    def tile(own, k):
        below = pltpu.roll(ylo[k], 4, 0)
        above = pltpu.roll(yhi[k], 4, 0)
        return own + jnp.where(four < 2, below, jnp.where(four > 5, above, 0.0))

    us = [tile(xlo[0], 2), tile(xlo[1], 3), tile(u[0], 0), tile(u[1], 1), tile(xhi[0], 4), tile(xhi[1], 5)]
    hs = [tile(xlo[2], 8), tile(h[0], 6), tile(h[1], 7), tile(xhi[2], 9)]
    es = []
    for x in range(4):
        c = us[x + 1]
        s = us[x] + us[x + 2] + line_sides(c, first, last) + column_sides(c)
        es.append(alpha * c + beta * hs[x] * s + fix)
    cell = lax.broadcasted_iota(jnp.int32, (128, 512), 1)
    agg = lax.broadcasted_iota(jnp.int32, (128, 512), 0)
    z = jnp.dot(jnp.concatenate(es, axis=0), (cell // 4 == agg).astype(jnp.float32), precision=HIGH)
    upper = lax.broadcasted_iota(jnp.int32, (8, 512), 0) < 4
    pro = []
    for x in range(4):
        parts = []
        for t in range(4):
            k = 8 * x + 2 * t
            a = jnp.broadcast_to(z[k:k + 1], (8, 512))
            b = jnp.broadcast_to(z[k + 1:k + 2], (8, 512))
            parts.append(jnp.where(upper, a, b))
        pro.append(jnp.concatenate(parts, axis=0))
    for i in range(1, 13):
        U0[i] = F[i] + jnp.where(G[i] > 0.0, pro[(i + 1) // 4], 0.0)
    first, last = edges((32, 512))
    for i in range(2, 12):
        s = G[i] * fine_sum(U0, i, first, last)
        U1[i] = (1.0 - c1) * U0[i] + c1 * (W[i] + s)
    for p in range(8):
        i = p + 3
        rho = rhs[p] / (6.0 + shift[p])
        gp = G[i, 8:24, :]
        solid = (1.0 - c1) * (alpha * rho + pro[(i + 1) // 4][8:24]) + c1 * rho
        mid = jnp.where(gp > 0.0, U1[i, 8:24, :], solid)
        s = gp * fine_sum(U1, i, first, last)[8:24]
        out[p] = (1.0 - c2) * mid + c2 * (rho + s)


def along(up, down, axis):
    count = lax.axis_size(axis)
    lo = lax.ppermute(up, axis, [(i, i + 1) for i in range(count - 1)])
    hi = lax.ppermute(down, axis, [(i + 1, i) for i in range(count - 1)])
    return lo, hi


def shards(rhs, shift, mask, cshift, inverse):
    field = shape(8, 16, 512)
    side = shape(88, 512)
    with jax.named_scope("weights"):
        w, g, h, up, down = call(k1, [field, field, shape(2, 8, 128), side, side])(rhs, shift, mask, cshift)
    xlo, xhi = along(up, down, AGG)
    with jax.named_scope("edges"):
        up, down = call(k2, [shape(56, 512)] * 2)(w, g, xlo, xhi, h)
    ylo, yhi = along(up, down, "grp")
    wide = shape(14, 32, 512)
    with jax.named_scope("presmooth"):
        W, G, F, u, lines = call(
            k3, [wide, wide, wide, shape(2, 8, 128), shape(64, 8, 128)],
            [pltpu.VMEM((14, 32, 512), jnp.float32)],
        )(w, g, xlo, xhi, ylo, yhi, h, rhs)
    lines = lax.all_to_all(lines, AGG, 0, 0)
    ulo, uhi = along(jnp.concatenate([u, h[1:2]]), jnp.concatenate([u, h[0:1]]), AGG)
    ext = [u, ulo[:2], uhi[:2], h, ulo[2:], uhi[2:]]
    blocks = [inverse[:, 128 * k:128 * k + 128].reshape(8, 8, 128) for k in range(4)]
    vlo, vhi = along(jnp.concatenate(ext + blocks[2:]), jnp.concatenate(ext + blocks[:2]), "grp")
    with jax.named_scope("line_product"):
        part = call(k4, shape(8, 128))(lines, inverse, vlo, vhi)
    part = lax.all_to_all(part.reshape(8, 1, 128), ("x", "zhi"), 0, 0).reshape(8, 128)
    place = lax.axis_index("zlo").astype(jnp.int32).reshape(1)
    with jax.named_scope("line_terms"):
        terms = pl.pallas_call(k5, out_shape=shape(64, 128), in_specs=[SM, VM])(place, part)
    terms = lax.all_to_all(terms.reshape(64, 1, 128), ("zlo", "core", "grp"), 0, 0).reshape(64, 128)
    scratch = [pltpu.VMEM((14, 32, 512), jnp.float32)] * 2
    with jax.named_scope("postsmooth"):
        return call(k6, field, scratch)(terms, W, G, F, u, h, ulo, uhi, vlo, vhi, rhs, shift)


def solution(mesh):
    finer = Mesh(mesh.devices.reshape(4, 2, 4, 2, 8), AGG + ("grp",))
    cells = P(AGG, "grp", None)
    return jax.shard_map(
        shards, mesh=finer, in_specs=(cells, cells, cells, cells, P(AGG, "grp")), out_specs=cells,
        check_vma=False,
    )
```

```python
import jax
import jax.numpy as jnp
from jax import lax
from jax.experimental import pallas as pl
from jax.experimental.pallas import tpu as pltpu
from jax.sharding import Mesh, PartitionSpec as P

c1 = 0.5735
c2 = 1.9751
alpha = c1 + c2 - c1 * c2
beta = c1 * c2
AGG = ("x", "zhi", "zlo", "core")
ROW = ("x", "zhi", "zlo", "grp")

VM = pl.BlockSpec(memory_space=pltpu.VMEM)
SM = pl.BlockSpec(memory_space=pltpu.SMEM)
HB = pl.BlockSpec(memory_space=pl.ANY)
HIGH = lax.Precision.HIGHEST

NEAR = (
    [("w", 1, p) for p in range(-1, 9)]
    + [("w", 2, p) for p in range(0, 8)]
    + [("g", 1, p) for p in range(0, 8)]
)
FAR = (
    [("w", 1, p) for p in (-2, 9)]
    + [("w", 2, p) for p in (-1, 8)]
    + [("w", 3, p) for p in range(0, 8)]
    + [("g", 1, p) for p in (-1, 8)]
    + [("g", 2, p) for p in range(0, 8)]
)
PLANES = {
    ("w", -2): ("lo", 0, 0), ("w", -1): ("lo", 0, 16), ("g", -1): ("lo", 0, 32),
    ("w", 8): ("hi", 0, 0), ("w", 9): ("hi", 0, 16), ("g", 8): ("hi", 0, 32),
    ("w", -3): ("lo", 1, 0), ("g", -2): ("lo", 1, 16),
    ("w", 10): ("hi", 1, 0), ("g", 9): ("hi", 1, 16),
}


def shape(*dims):
    return jax.ShapeDtypeStruct(dims, jnp.float32)


def call(body, outs, scratch=(), specs=None, mib=8, flops=0):
    extra = {} if specs is None else {"in_specs": specs}
    return pl.pallas_call(
        body,
        out_shape=outs,
        scratch_shapes=list(scratch),
        compiler_params=pltpu.CompilerParams(vmem_limit_bytes=mib * 1024 * 1024),
        cost_estimate=pl.CostEstimate(flops=flops, bytes_accessed=flops // 2, transcendentals=0),
        **extra,
    )


def k1(rhs_at, shift_at, mask_at, cshift_at, w, g, rho, h, up, down, rhs, shift, mask, cshift, sems):
    pairs = ((rhs_at, rhs), (shift_at, shift), (mask_at, mask), (cshift_at, cshift))
    copies = [pltpu.make_async_copy(a, b, sems.at[i]) for i, (a, b) in enumerate(pairs)]
    for c in copies:
        c.start()
    h[...] = jnp.zeros((2, 8, 128), jnp.float32)
    for c in copies:
        c.wait()
    for x in range(2):
        h[x, 2:6, :] = 1.0 / (6.0 + cshift[x])
    for p in range(8):
        inv = 1.0 / (6.0 + shift[p])
        f = mask[p].astype(jnp.float32)
        q = rhs[p] * inv
        wp, gp = f * q, f * inv
        w[p], g[p], rho[p] = wp, gp, q
        if p >= 6:
            up[(p - 6) * 16:(p - 5) * 16] = wp
        if p == 7:
            up[32:48] = gp
        if p < 2:
            down[p * 16:(p + 1) * 16] = wp
        if p == 0:
            down[32:48] = gp
    for out, x in ((up, 1), (down, 0)):
        out[48:56, 0:128] = h[x]
        out[48:56, 128:512] = jnp.zeros((8, 384), jnp.float32)


def plane(own, sides, field, p):
    if 0 <= p < 8:
        return lambda a, b: own[field][p, a:b, :]
    side, which, base = PLANES[field, p]
    ref = sides[side][which]
    return lambda a, b: ref[base + a:base + b, :]


def pack_rows(rows, own, sides, up, down):
    for k, (field, d, p) in enumerate(rows):
        read = plane(own, sides, field, p)
        up[k:k + 1] = read(16 - d, 17 - d)
        down[k:k + 1] = read(d - 1, d)


def k2(w, g, lo, hi, h, inverse, up, down):
    pack_rows(NEAR, {"w": w, "g": g}, {"lo": (lo,), "hi": (hi,)}, up, down)
    for out, first in ((up, 256), (down, 0)):
        out[26:32] = jnp.zeros((6, 512), jnp.float32)
        for x in range(2):
            out[26:30, 128 * x:128 * x + 128] = h[x, 2:6, :]
        for half in range(2):
            out[32:64, 256 * half:256 * half + 256] = inverse[32 * half:32 * half + 32, first:first + 256]


def fine_sum(ref, p, first, last):
    c = ref[p]
    total = ref[p - 1] + ref[p + 1]
    total = total + pltpu.roll(c, 1, 0) + pltpu.roll(c, 31, 0)
    total = total + jnp.where(first, 0.0, pltpu.roll(c, 1, 1))
    return total + jnp.where(last, 0.0, pltpu.roll(c, 511, 1))


def edges(dims):
    lane = lax.broadcasted_iota(jnp.int32, dims, 1)
    return lane == 0, lane == dims[1] - 1


def line_sides(c, first, last):
    total = jnp.where(first, 0.0, pltpu.roll(c, 1, 1))
    return total + jnp.where(last, 0.0, pltpu.roll(c, 127, 1))


def column_sides(c):
    return pltpu.roll(c, 1, 0) + pltpu.roll(c, 7, 0)


def fill(wide, own, sides, messages):
    zero = jnp.zeros((8, 512), jnp.float32)
    for field in ("w", "g"):
        out = wide[field]
        for i in range(14):
            p = i - 3
            out[i, 0:8, :] = zero
            out[i, 24:32, :] = zero
            known = 0 <= p < 8 or ((field, p) in PLANES and PLANES[field, p][1] < len(sides["lo"]))
            if known:
                out[i, 8:24, :] = plane(own, sides, field, p)(0, 16)
            else:
                out[i, 8:16, :] = zero
                out[i, 16:24, :] = zero
    for rows, lo, hi in messages:
        for k, (field, d, p) in enumerate(rows):
            wide[field][p + 3, 8 - d:9 - d, :] = lo[k:k + 1]
            wide[field][p + 3, 23 + d:24 + d, :] = hi[k:k + 1]


def k3(w, g, xlo, xhi, ylo, yhi, h, rhs, inverse, L, CE, u, up, down, W, G, V):
    own = {"w": w, "g": g}
    fill({"w": W, "g": G}, own, {"lo": (xlo,), "hi": (xhi,)}, [(NEAR, ylo, yhi)])
    first, last = edges((32, 512))
    for i in range(2, 12):
        V[i] = (alpha - beta) * W[i] + (beta * G[i]) * fine_sum(W, i, first, last)
    sums = []
    for x in range(2):
        total = None
        for p in range(4 * x, 4 * x + 4):
            s = fine_sum(V, p + 3, first, last)[8:24]
            r = (1.0 - alpha) * rhs[p] + jnp.where(g[p] > 0.0, s, 0.0)
            total = r if total is None else total + r
        sums.append(total)
    both = jnp.concatenate(sums, axis=0)
    cell = lax.broadcasted_iota(jnp.int32, (512, 128), 0)
    agg = lax.broadcasted_iota(jnp.int32, (512, 128), 1)
    thin = jnp.dot(both, (cell // 4 == agg).astype(jnp.float32), precision=HIGH)
    row = lax.broadcasted_iota(jnp.int32, (16, 32), 0)
    col = lax.broadcasted_iota(jnp.int32, (16, 32), 1)
    x_of, y_of = row // 8, row % 8 - 2
    take = (col // 16 == x_of) & ((col % 16) // 4 == y_of) & (y_of >= 0) & (y_of < 4)
    tiles = jnp.dot(take.astype(jnp.float32), thin, precision=HIGH)
    r = (tiles[0:8], tiles[8:16])
    four = lax.broadcasted_iota(jnp.int32, (8, 128), 0)
    first, last = edges((8, 128))
    lo, hi = xlo[48:56, 0:128], xhi[48:56, 0:128]
    hx = (lo + h[1], h[0] + hi)
    us, hs = [], []
    for x in range(2):
        us.append(r[x] * h[x])
        below = jnp.broadcast_to(ylo[29:30, 128 * x:128 * x + 128], (8, 128))
        above = jnp.broadcast_to(yhi[26:27, 128 * x:128 * x + 128], (8, 128))
        hs.append(jnp.where(four == 1, below, jnp.where(four == 6, above, h[x])))
        u[x] = us[x]
    q = jnp.zeros((8, 128), jnp.float32)
    flat = []
    for x in range(2):
        side = line_sides(us[x], first, last) + column_sides(us[x])
        q = q + (alpha - beta) * us[x] + beta * (hx[x] * us[x] + hs[x] * side)
        flat.append((alpha - beta) * us[x] + beta * hs[x] * (us[1 - x] + side))
    total = 2.0 * q + line_sides(q, first, last) + column_sides(q) + (1.0 - alpha) * (r[0] + r[1])
    total = total - jnp.where(jnp.broadcast_to(lo[2:3], (8, 128)) > 0.0, 0.0, flat[0])
    total = total - jnp.where(jnp.broadcast_to(hi[2:3], (8, 128)) > 0.0, 0.0, flat[1])
    for i in range(64):
        L[i] = total
    CE[:, 256:768] = inverse[...]
    for half in range(2):
        rows, lanes = slice(32 * half, 32 * half + 32), slice(256 * half, 256 * half + 256)
        CE[rows, 0:256] = ylo[32:64, lanes]
        CE[rows, 768:1024] = yhi[32:64, lanes]
    for out, p, q, x in ((up, 5, 6, 1), (down, 2, 1, 0)):
        out[0:16] = w[p]
        out[16:32] = g[q]
        out[32:40, 0:128] = us[0]
        out[32:40, 128:256] = us[1]
        out[32:40, 256:384] = h[x]
        out[32:40, 384:512] = jnp.zeros((8, 128), jnp.float32)


def k4(w, g, lo, hi, u, h, flo, fhi, up, down):
    own = {"w": w, "g": g}
    pack_rows(FAR, own, {"lo": (lo,), "hi": (hi,)}, up, down)
    tiles = [u[0], u[1], h[0], h[1]]
    tiles += [flo[32:40, 128 * k:128 * k + 128] for k in range(4)]
    tiles += [fhi[32:40, 128 * k:128 * k + 128] for k in range(4)]
    for out in (up, down):
        out[22:24] = jnp.zeros((2, 512), jnp.float32)
        for k, t in enumerate(tiles):
            row, lane = 24 + 8 * (k // 4), 128 * (k % 4)
            out[row:row + 8, lane:lane + 128] = t


def k5(place, lines, own, mate, out):
    s = lines[0]
    for i in range(1, 64):
        s = s + lines[i]
    tables = []
    for ref in (own, mate):
        t = ref[:, 0:128] * s[0:1]
        for k in range(1, 8):
            t = t + ref[:, 128 * k:128 * k + 128] * s[k:k + 1]
        tables.append(t)
    even = place[0] == 0
    table = jnp.concatenate([jnp.where(even, *tables), jnp.where(even, *tables[::-1])], axis=0)
    y = lax.dot_general(
        jnp.ones((8, 128), jnp.float32), table, (((1,), (1,)), ((), ())), precision=HIGH
    )
    for i in range(32):
        out[8 * i:8 * i + 8] = y


def prolong_lines(z, upper, k):
    parts = []
    for t in range(4):
        a = jnp.broadcast_to(z[k + 2 * t:k + 2 * t + 1], (8, 512))
        b = jnp.broadcast_to(z[k + 2 * t + 1:k + 2 * t + 2], (8, 512))
        parts.append(jnp.where(upper, a, b))
    return jnp.concatenate(parts, axis=0)


def spread(tiles):
    cell = lax.broadcasted_iota(jnp.int32, (128, 512), 1)
    agg = lax.broadcasted_iota(jnp.int32, (128, 512), 0)
    z = jnp.dot(tiles, (cell // 4 == agg).astype(jnp.float32), precision=HIGH)
    upper = lax.broadcasted_iota(jnp.int32, (8, 512), 0) < 4
    return [prolong_lines(z, upper, k) for k in range(0, tiles.shape[0], 8)]


def k6(w, g, xlo, xhi, ylo, yhi, flo, fhi, vlo, vhi, u, h, rho, W, G, U, solid):
    own = {"w": w, "g": g}
    fill({"w": W, "g": G}, own, {"lo": (xlo, flo), "hi": (xhi, fhi)}, [(NEAR, ylo, yhi), (FAR, vlo, vhi)])
    four = lax.broadcasted_iota(jnp.int32, (8, 128), 0)
    first, last = edges((8, 128))

    def tile(mine, k):
        row, lane = 24 + 8 * (k // 4), 128 * (k % 4)
        below = pltpu.roll(vlo[row:row + 8, lane:lane + 128], 4, 0)
        above = pltpu.roll(vhi[row:row + 8, lane:lane + 128], 4, 0)
        return jnp.where(four < 2, below, jnp.where(four > 5, above, mine))

    far = [[ref[32:40, 128 * k:128 * k + 128] for k in range(3)] for ref in (flo, fhi)]
    us = [tile(far[0][0], 4), tile(far[0][1], 5), tile(u[0], 0), tile(u[1], 1), tile(far[1][0], 8), tile(far[1][1], 9)]
    hs = [tile(far[0][2], 6), tile(h[0], 2), tile(h[1], 3), tile(far[1][2], 10)]
    es = []
    for x in range(4):
        c = us[x + 1]
        s = us[x] + us[x + 2] + line_sides(c, first, last) + column_sides(c)
        es.append(alpha * c + beta * hs[x] * s)
    pro = spread(jnp.concatenate(es, axis=0))
    first, last = edges((32, 512))
    for i in range(1, 13):
        fp = alpha * W[i] + (beta * G[i]) * fine_sum(W, i, first, last)
        U[i] = fp + jnp.where(G[i] > 0.0, pro[(i + 1) // 4], 0.0)
    for p in range(8):
        solid[p] = ((1.0 - c1) * alpha + c1) * rho[p] + (1.0 - c1) * pro[p // 4 + 1][8:24]


def k7(place, terms, W, G, U, solid, rho, out, U0, U1):
    grp = place[1]
    rows = [jnp.zeros((1, 128), jnp.float32)]
    for j in range(-1, 5):
        k = jnp.clip(4 * grp + j, 0, 31)
        rows.append(jnp.sum(terms[pl.ds(pl.multiple_of(8 * k, 8), 8), :], axis=0, keepdims=True))
    rows.append(jnp.zeros((1, 128), jnp.float32))
    pro = spread(jnp.concatenate(rows, axis=0))[0]
    for i in range(1, 13):
        U0[i] = U[i] + jnp.where(G[i] > 0.0, pro, 0.0)
    first, last = edges((32, 512))
    for i in range(2, 12):
        U1[i] = (1.0 - c1) * U0[i] + c1 * (W[i] + G[i] * fine_sum(U0, i, first, last))
    for p in range(8):
        i = p + 3
        gp = G[i, 8:24, :]
        mid = jnp.where(gp > 0.0, U1[i, 8:24, :], solid[p] + (1.0 - c1) * pro[8:24])
        s = gp * fine_sum(U1, i, first, last)[8:24]
        out[p] = (1.0 - c2) * mid + c2 * (rho[p] + s)


def along(up, down, axis):
    count = lax.axis_size(axis)
    lo = lax.ppermute(up, axis, [(i, i + 1) for i in range(count - 1)])
    hi = lax.ppermute(down, axis, [(i + 1, i) for i in range(count - 1)])
    return lo, hi


def shards(rhs, shift, mask, cshift, inverse):
    field, wide, coarse = shape(8, 16, 512), shape(14, 32, 512), shape(2, 8, 128)
    wide_at = pltpu.VMEM((14, 32, 512), jnp.float32)
    place = jnp.stack([lax.axis_index("core"), lax.axis_index("grp")]).astype(jnp.int32)
    fetched = [pltpu.VMEM(a.shape, a.dtype) for a in (rhs, shift, mask, cshift)]
    with jax.named_scope("weights"):
        w, g, rho, h, up, down = call(
            k1, [field, field, field, coarse, shape(56, 512), shape(56, 512)],
            fetched + [pltpu.SemaphoreType.DMA((4,))], [HB] * 4, mib=44,
        )(rhs, shift, mask, cshift)
    xlo, xhi = along(up, down, AGG)
    with jax.named_scope("near_rows"):
        up, down = call(k2, [shape(64, 512)] * 2)(w, g, xlo, xhi, h, inverse)
    ylo, yhi = along(up, down, "grp")
    with jax.named_scope("residual"):
        lines, table, u, up, down = call(
            k3, [shape(64, 8, 128), shape(64, 1024), coarse, shape(40, 512), shape(40, 512)],
            [wide_at] * 3,
        )(w, g, xlo, xhi, ylo, yhi, h, rhs, inverse)
    lines = lax.all_to_all(lines, AGG, 0, 0)
    mate = lax.ppermute(table, "core", [(0, 1), (1, 0)])
    flo, fhi = along(up, down, AGG)
    with jax.named_scope("line_product"):
        part = call(k5, shape(256, 128), specs=[SM, VM, VM, VM])(place, lines, table, mate)
    terms = lax.all_to_all(part.reshape(256, 1, 128), ROW, 0, 0).reshape(256, 128)
    with jax.named_scope("far_rows"):
        up, down = call(k4, [shape(48, 512)] * 2, flops=200000)(w, g, xlo, xhi, u, h, flo, fhi)
    vlo, vhi = along(up, down, "grp")
    with jax.named_scope("presmooth"):
        W, G, U, solid = call(k6, [wide, wide, wide, field], flops=4000000)(
            w, g, xlo, xhi, ylo, yhi, flo, fhi, vlo, vhi, u, h, rho
        )
    with jax.named_scope("postsmooth"):
        return call(k7, field, [wide_at] * 2, [SM] + [VM] * 6)(place, terms, W, G, U, solid, rho)


def solution(mesh):
    finer = Mesh(mesh.devices.reshape(4, 2, 4, 2, 8), AGG + ("grp",))
    cells = P(AGG, "grp", None)
    return jax.shard_map(
        shards, mesh=finer, in_specs=(cells, cells, cells, cells, P(AGG, "grp")), out_specs=cells,
        check_vma=False,
    )
```

```python
import jax
import jax.numpy as jnp
from jax import lax
from jax.experimental import pallas as pl
from jax.experimental.pallas import tpu as pltpu
from jax.sharding import Mesh, PartitionSpec as P

c1 = 0.5735
c2 = 1.9751
alpha = c1 + c2 - c1 * c2
beta = c1 * c2
AGG = ("x", "zhi", "zlo", "core")
ROW = ("x", "zhi", "zlo", "grp")

VM = pl.BlockSpec(memory_space=pltpu.VMEM)
SM = pl.BlockSpec(memory_space=pltpu.SMEM)
HIGH = lax.Precision.HIGHEST

NEAR = (
    [("w", 1, p) for p in range(-1, 9)]
    + [("w", 2, p) for p in range(0, 8)]
    + [("g", 1, p) for p in range(0, 8)]
)
FAR = (
    [("w", 1, p) for p in (-2, 9)]
    + [("w", 2, p) for p in (-1, 8)]
    + [("w", 3, p) for p in range(0, 8)]
    + [("g", 1, p) for p in (-1, 8)]
    + [("g", 2, p) for p in range(0, 8)]
)
PLANES = {
    ("w", -2): ("lo", 0, 0), ("w", -1): ("lo", 0, 16), ("g", -1): ("lo", 0, 32),
    ("w", 8): ("hi", 0, 0), ("w", 9): ("hi", 0, 16), ("g", 8): ("hi", 0, 32),
    ("w", -3): ("lo", 1, 0), ("g", -2): ("lo", 1, 16),
    ("w", 10): ("hi", 1, 0), ("g", 9): ("hi", 1, 16),
}


def shape(*dims):
    return jax.ShapeDtypeStruct(dims, jnp.float32)


def call(body, outs, scratch=(), specs=None, mib=8, flops=0):
    extra = {} if specs is None else {"in_specs": specs}
    return pl.pallas_call(
        body,
        out_shape=outs,
        scratch_shapes=list(scratch),
        compiler_params=pltpu.CompilerParams(vmem_limit_bytes=mib * 1024 * 1024),
        cost_estimate=pl.CostEstimate(flops=flops, bytes_accessed=flops // 2, transcendentals=0),
        **extra,
    )


class Pick:
    def __init__(self, flag, yes, no):
        self.flag, self.yes, self.no = flag, yes, no

    def __getitem__(self, at):
        return jnp.where(self.flag, self.yes[at], self.no[at])


class Post:
    def __init__(self, even, s0, s1):
        self.even, self.s0, self.s1 = even, s0, s1

    def put(self, at, up, down):
        self.s0[at] = jnp.where(self.even, up, down)
        self.s1[at] = jnp.where(self.even, down, up)

    def both(self, at, value):
        self.s0[at] = value
        self.s1[at] = value


def received(even, r0, r1):
    return Pick(even, r1, r0), Pick(even, r0, r1)


def k1(place, w, g, cshift, h, s0, s1):
    post = Post(place[0] == 0, s0, s1)
    h[...] = jnp.zeros((2, 8, 128), jnp.float32)
    for x in range(2):
        h[x, 2:6, :] = 1.0 / (6.0 + cshift[x])
    rows = lambda k: (slice(16 * k, 16 * k + 16), slice(None))
    post.put(rows(0), w[6], w[0])
    post.put(rows(1), w[7], w[1])
    post.put(rows(2), g[7], g[0])
    post.put((slice(48, 56), slice(0, 128)), h[1], h[0])
    post.both((slice(48, 56), slice(128, 512)), jnp.zeros((8, 384), jnp.float32))


def plane(own, sides, field, p):
    if 0 <= p < 8:
        return lambda a, b: own[field][p, a:b, :]
    side, which, base = PLANES[field, p]
    ref = sides[side][which]
    return lambda a, b: ref[base + a:base + b, :]


def pack_rows(rows, own, sides, post):
    for k, (field, d, p) in enumerate(rows):
        read = plane(own, sides, field, p)
        post.put((slice(k, k + 1), slice(None)), read(16 - d, 17 - d), read(d - 1, d))


def k2(place, w, g, x0, x1, h, inverse, s0, s1):
    lo, hi = received(place[0] == 0, x0, x1)
    post = Post(lax.rem(place[1], 2) == 0, s0, s1)
    pack_rows(NEAR, {"w": w, "g": g}, {"lo": (lo,), "hi": (hi,)}, post)
    post.both((slice(26, 32), slice(None)), jnp.zeros((6, 512), jnp.float32))
    for x in range(2):
        post.both((slice(26, 30), slice(128 * x, 128 * x + 128)), h[x, 2:6, :])
    for half in range(2):
        piece = inverse[32 * half:32 * half + 32, :]
        at = (slice(32, 64), slice(256 * half, 256 * half + 256))
        post.put(at, piece[:, 256:512], piece[:, 0:256])


def fine_sum(ref, p, first, last):
    c = ref[p]
    total = ref[p - 1] + ref[p + 1]
    total = total + pltpu.roll(c, 1, 0) + pltpu.roll(c, 31, 0)
    total = total + jnp.where(first, 0.0, pltpu.roll(c, 1, 1))
    return total + jnp.where(last, 0.0, pltpu.roll(c, 511, 1))


def edges(dims):
    lane = lax.broadcasted_iota(jnp.int32, dims, 1)
    return lane == 0, lane == dims[1] - 1


def line_sides(c, first, last):
    total = jnp.where(first, 0.0, pltpu.roll(c, 1, 1))
    return total + jnp.where(last, 0.0, pltpu.roll(c, 127, 1))


def column_sides(c):
    return pltpu.roll(c, 1, 0) + pltpu.roll(c, 7, 0)


def fill(wide, own, sides, messages):
    zero = jnp.zeros((8, 512), jnp.float32)
    for field in ("w", "g"):
        out = wide[field]
        for i in range(14):
            p = i - 3
            out[i, 0:8, :] = zero
            out[i, 24:32, :] = zero
            known = 0 <= p < 8 or ((field, p) in PLANES and PLANES[field, p][1] < len(sides["lo"]))
            if known:
                out[i, 8:24, :] = plane(own, sides, field, p)(0, 16)
            else:
                out[i, 8:16, :] = zero
                out[i, 16:24, :] = zero
    for rows, lo, hi in messages:
        for k, (field, d, p) in enumerate(rows):
            wide[field][p + 3, 8 - d:9 - d, :] = lo[k:k + 1]
            wide[field][p + 3, 23 + d:24 + d, :] = hi[k:k + 1]


def k3(place, w, g, x0, x1, y0, y1, h, rhs, inverse, L, CE, u, s0, s1, W, G, V):
    even = place[0] == 0
    xlo, xhi = received(even, x0, x1)
    ylo, yhi = received(lax.rem(place[1], 2) == 0, y0, y1)
    post = Post(even, s0, s1)
    own = {"w": w, "g": g}
    fill({"w": W, "g": G}, own, {"lo": (xlo,), "hi": (xhi,)}, [(NEAR, ylo, yhi)])
    first, last = edges((32, 512))
    for i in range(2, 12):
        V[i] = (alpha - beta) * W[i] + (beta * G[i]) * fine_sum(W, i, first, last)
    sums = []
    for x in range(2):
        total = None
        for p in range(4 * x, 4 * x + 4):
            s = fine_sum(V, p + 3, first, last)[8:24]
            r = (1.0 - alpha) * rhs[p] + jnp.where(g[p] > 0.0, s, 0.0)
            total = r if total is None else total + r
        sums.append(total)
    both = jnp.concatenate(sums, axis=0)
    cell = lax.broadcasted_iota(jnp.int32, (512, 128), 0)
    agg = lax.broadcasted_iota(jnp.int32, (512, 128), 1)
    thin = jnp.dot(both, (cell // 4 == agg).astype(jnp.float32), precision=HIGH)
    row = lax.broadcasted_iota(jnp.int32, (16, 32), 0)
    col = lax.broadcasted_iota(jnp.int32, (16, 32), 1)
    x_of, y_of = row // 8, row % 8 - 2
    take = (col // 16 == x_of) & ((col % 16) // 4 == y_of) & (y_of >= 0) & (y_of < 4)
    tiles = jnp.dot(take.astype(jnp.float32), thin, precision=HIGH)
    r = (tiles[0:8], tiles[8:16])
    four = lax.broadcasted_iota(jnp.int32, (8, 128), 0)
    first, last = edges((8, 128))
    lo, hi = xlo[48:56, 0:128], xhi[48:56, 0:128]
    hx = (lo + h[1], h[0] + hi)
    us, hs = [], []
    for x in range(2):
        us.append(r[x] * h[x])
        below = jnp.broadcast_to(ylo[29:30, 128 * x:128 * x + 128], (8, 128))
        above = jnp.broadcast_to(yhi[26:27, 128 * x:128 * x + 128], (8, 128))
        hs.append(jnp.where(four == 1, below, jnp.where(four == 6, above, h[x])))
        u[x] = us[x]
    q = jnp.zeros((8, 128), jnp.float32)
    flat = []
    for x in range(2):
        side = line_sides(us[x], first, last) + column_sides(us[x])
        q = q + (alpha - beta) * us[x] + beta * (hx[x] * us[x] + hs[x] * side)
        flat.append((alpha - beta) * us[x] + beta * hs[x] * (us[1 - x] + side))
    total = 2.0 * q + line_sides(q, first, last) + column_sides(q) + (1.0 - alpha) * (r[0] + r[1])
    total = total - jnp.where(jnp.broadcast_to(lo[2:3], (8, 128)) > 0.0, 0.0, flat[0])
    total = total - jnp.where(jnp.broadcast_to(hi[2:3], (8, 128)) > 0.0, 0.0, flat[1])
    for i in range(64):
        L[i] = total
    CE[:, 256:768] = inverse[...]
    for half in range(2):
        rows, lanes = slice(32 * half, 32 * half + 32), slice(256 * half, 256 * half + 256)
        CE[rows, 0:256] = ylo[32:64, lanes]
        CE[rows, 768:1024] = yhi[32:64, lanes]
    post.put((slice(0, 16), slice(None)), w[5], w[2])
    post.put((slice(16, 32), slice(None)), g[6], g[1])
    tiles = slice(32, 40)
    post.both((tiles, slice(0, 128)), us[0])
    post.both((tiles, slice(128, 256)), us[1])
    post.put((tiles, slice(256, 384)), h[1], h[0])
    post.both((tiles, slice(384, 512)), jnp.zeros((8, 128), jnp.float32))


def k4(place, w, g, x0, x1, u, h, f0, f1, s0, s1):
    even = place[0] == 0
    lo, hi = received(even, x0, x1)
    flo, fhi = received(even, f0, f1)
    post = Post(lax.rem(place[1], 2) == 0, s0, s1)
    pack_rows(FAR, {"w": w, "g": g}, {"lo": (lo,), "hi": (hi,)}, post)
    post.both((slice(22, 24), slice(None)), jnp.zeros((2, 512), jnp.float32))
    tiles = [u[0], u[1], h[0], h[1]]
    for ref in (flo, fhi):
        tiles += [ref[32:40, 128 * k:128 * k + 128] for k in range(4)]
    for k, t in enumerate(tiles):
        row, lane = 24 + 8 * (k // 4), 128 * (k % 4)
        post.both((slice(row, row + 8), slice(lane, lane + 128)), t)


def k5(place, lines, own, mate, out):
    s = lines[0]
    for i in range(1, 64):
        s = s + lines[i]
    tables = []
    for ref in (own, mate):
        t = ref[:, 0:128] * s[0:1]
        for k in range(1, 8):
            t = t + ref[:, 128 * k:128 * k + 128] * s[k:k + 1]
        tables.append(t)
    even = place[0] == 0
    table = jnp.concatenate([jnp.where(even, *tables), jnp.where(even, *tables[::-1])], axis=0)
    y = lax.dot_general(
        jnp.ones((8, 128), jnp.float32), table, (((1,), (1,)), ((), ())), precision=HIGH
    )
    for i in range(32):
        out[8 * i:8 * i + 8] = y


def prolong_lines(z, upper, k):
    parts = []
    for t in range(4):
        a = jnp.broadcast_to(z[k + 2 * t:k + 2 * t + 1], (8, 512))
        b = jnp.broadcast_to(z[k + 2 * t + 1:k + 2 * t + 2], (8, 512))
        parts.append(jnp.where(upper, a, b))
    return jnp.concatenate(parts, axis=0)


def spread(tiles):
    cell = lax.broadcasted_iota(jnp.int32, (128, 512), 1)
    agg = lax.broadcasted_iota(jnp.int32, (128, 512), 0)
    z = jnp.dot(tiles, (cell // 4 == agg).astype(jnp.float32), precision=HIGH)
    upper = lax.broadcasted_iota(jnp.int32, (8, 512), 0) < 4
    return [prolong_lines(z, upper, k) for k in range(0, tiles.shape[0], 8)]


def k6(place, terms, w, g, x0, x1, y0, y1, f0, f1, v0, v1, u, h, rho, out, W, G, U0, U1):
    even, row_even = place[0] == 0, lax.rem(place[1], 2) == 0
    xlo, xhi = received(even, x0, x1)
    flo, fhi = received(even, f0, f1)
    ylo, yhi = received(row_even, y0, y1)
    vlo, vhi = received(row_even, v0, v1)
    own = {"w": w, "g": g}
    fill({"w": W, "g": G}, own, {"lo": (xlo, flo), "hi": (xhi, fhi)}, [(NEAR, ylo, yhi), (FAR, vlo, vhi)])
    fix = [jnp.zeros((1, 128), jnp.float32)]
    for j in range(-1, 5):
        k = jnp.clip(4 * place[1] + j, 0, 31)
        fix.append(jnp.sum(terms[pl.ds(pl.multiple_of(8 * k, 8), 8), :], axis=0, keepdims=True))
    fix = jnp.concatenate(fix + [jnp.zeros((1, 128), jnp.float32)], axis=0)
    four = lax.broadcasted_iota(jnp.int32, (8, 128), 0)
    first, last = edges((8, 128))

    def tile(mine, k):
        row, lane = 24 + 8 * (k // 4), 128 * (k % 4)
        below = pltpu.roll(vlo[row:row + 8, lane:lane + 128], 4, 0)
        above = pltpu.roll(vhi[row:row + 8, lane:lane + 128], 4, 0)
        return jnp.where(four < 2, below, jnp.where(four > 5, above, mine))

    far = [[ref[32:40, 128 * k:128 * k + 128] for k in range(3)] for ref in (flo, fhi)]
    us = [tile(far[0][0], 4), tile(far[0][1], 5), tile(u[0], 0), tile(u[1], 1), tile(far[1][0], 8), tile(far[1][1], 9)]
    hs = [tile(far[0][2], 6), tile(h[0], 2), tile(h[1], 3), tile(far[1][2], 10)]
    es = []
    for x in range(4):
        c = us[x + 1]
        s = us[x] + us[x + 2] + line_sides(c, first, last) + column_sides(c)
        es.append(alpha * c + beta * hs[x] * s + fix)
    pro = spread(jnp.concatenate(es, axis=0))
    first, last = edges((32, 512))
    for i in range(1, 13):
        fp = alpha * W[i] + (beta * G[i]) * fine_sum(W, i, first, last)
        U0[i] = fp + jnp.where(G[i] > 0.0, pro[(i + 1) // 4], 0.0)
    for i in range(2, 12):
        U1[i] = (1.0 - c1) * U0[i] + c1 * (W[i] + G[i] * fine_sum(U0, i, first, last))
    for p in range(8):
        i = p + 3
        gp = G[i, 8:24, :]
        solid = ((1.0 - c1) * alpha + c1) * rho[p] + (1.0 - c1) * pro[p // 4 + 1][8:24]
        mid = jnp.where(gp > 0.0, U1[i, 8:24, :], solid)
        s = gp * fine_sum(U1, i, first, last)[8:24]
        out[p] = (1.0 - c2) * mid + c2 * (rho[p] + s)


def swaps(s0, s1, axis, order):
    count, sent, got = lax.axis_size(axis), (s0, s1), [None, None]
    for parity in order:
        pairs = []
        for i in range(parity, count - 1, 2):
            pairs += [(i, i + 1), (i + 1, i)]
        got[parity] = lax.ppermute(sent[parity], axis, pairs)
    return got


def shards(rhs, shift, mask, cshift, inverse):
    field, wide, coarse = shape(8, 16, 512), shape(14, 32, 512), shape(2, 8, 128)
    wide_at = pltpu.VMEM((14, 32, 512), jnp.float32)
    place = jnp.stack([lax.axis_index("core"), lax.axis_index("grp")]).astype(jnp.int32)

    def kernel(name, body, outs, scratch, *args, flops=0):
        with jax.named_scope(name):
            return call(body, outs, scratch, [SM] + [VM] * len(args), flops=flops)(place, *args)

    diag = 6.0 + shift
    fluid = mask.astype(jnp.float32)
    rho = rhs / diag
    g = fluid / diag
    w = fluid * rho
    h, s0, s1 = kernel("edges", k1, [coarse, shape(56, 512), shape(56, 512)], [], w, g, cshift)
    x0, x1 = swaps(s0, s1, AGG, (1, 0))
    s0, s1 = kernel("near_rows", k2, [shape(64, 512)] * 2, [], w, g, x0, x1, h, inverse)
    y0, y1 = swaps(s0, s1, "grp", (0, 1))
    lines, table, u, s0, s1 = kernel(
        "residual", k3, [shape(64, 8, 128), shape(64, 1024), coarse, shape(40, 512), shape(40, 512)],
        [wide_at] * 3, w, g, x0, x1, y0, y1, h, rhs, inverse,
    )
    lines = lax.all_to_all(lines, AGG, 0, 0)
    mate = lax.ppermute(table, "core", [(0, 1), (1, 0)])
    f0, f1 = swaps(s0, s1, AGG, (1, 0))
    lines, mate, f0, f1 = lax.optimization_barrier((lines, mate, f0, f1))
    part = kernel("line_product", k5, shape(256, 128), [], lines, table, mate)
    terms = lax.all_to_all(part.reshape(256, 1, 128), ROW, 0, 0).reshape(256, 128)
    s0, s1 = kernel("far_rows", k4, [shape(48, 512)] * 2, [], w, g, x0, x1, u, h, f0, f1, flops=200000)
    v0, v1 = swaps(s0, s1, "grp", (0, 1))
    return kernel(
        "postsmooth", k6, field, [wide_at] * 4,
        terms, w, g, x0, x1, y0, y1, f0, f1, v0, v1, u, h, rho,
    )


def solution(mesh):
    finer = Mesh(mesh.devices.reshape(4, 2, 4, 2, 8), AGG + ("grp",))
    cells = P(AGG, "grp", None)
    return jax.shard_map(
        shards, mesh=finer, in_specs=(cells, cells, cells, cells, P(AGG, "grp")), out_specs=cells,
        check_vma=False,
    )
```

```python
import jax
import jax.numpy as jnp
from jax import lax
from jax.experimental import pallas as pl
from jax.experimental.pallas import tpu as pltpu
from jax.sharding import Mesh, PartitionSpec as P

c1 = 0.5735
c2 = 1.9751
alpha = c1 + c2 - c1 * c2
beta = c1 * c2
AGG = ("x", "zhi", "zlo", "core")
ROW = ("x", "zhi", "zlo", "grp")

HIGH = lax.Precision.HIGHEST

NEAR = (
    [("w", 1, p) for p in range(-1, 9)]
    + [("w", 2, p) for p in range(0, 8)]
    + [("g", 1, p) for p in range(0, 8)]
)
FAR = (
    [("w", 1, p) for p in (-2, 9)]
    + [("w", 2, p) for p in (-1, 8)]
    + [("w", 3, p) for p in range(0, 8)]
    + [("g", 1, p) for p in (-1, 8)]
    + [("g", 2, p) for p in range(0, 8)]
)
PLANES = {
    ("w", -2): ("lo", 0, 0), ("w", -1): ("lo", 0, 16), ("g", -1): ("lo", 0, 32),
    ("w", 8): ("hi", 0, 0), ("w", 9): ("hi", 0, 16), ("g", 8): ("hi", 0, 32),
    ("w", -3): ("lo", 1, 0), ("g", -2): ("lo", 1, 16),
    ("w", 10): ("hi", 1, 0), ("g", 9): ("hi", 1, 16),
}


def shape(*dims):
    return jax.ShapeDtypeStruct(dims, jnp.float32)


def call(body, outs, scratch=(), mib=8, flops=0):
    return pl.pallas_call(
        body,
        out_shape=outs,
        scratch_shapes=list(scratch),
        compiler_params=pltpu.CompilerParams(vmem_limit_bytes=mib * 1024 * 1024),
        cost_estimate=pl.CostEstimate(flops=flops, bytes_accessed=flops // 2, transcendentals=0),
    )


class Pick:
    def __init__(self, flag, yes, no):
        self.flag, self.yes, self.no = flag, yes, no

    def __getitem__(self, at):
        return jnp.where(self.flag, self.yes[at], self.no[at])


class Post:
    def __init__(self, even, s0, s1):
        self.even, self.s0, self.s1 = even, s0, s1

    def put(self, at, up, down):
        self.s0[at] = jnp.where(self.even, up, down)
        self.s1[at] = jnp.where(self.even, down, up)

    def both(self, at, value):
        self.s0[at] = value
        self.s1[at] = value


def received(even, r0, r1):
    return Pick(even, r1, r0), Pick(even, r0, r1)


def k1(w, g, cshift, h, s1, s0):
    post = Post(lax.axis_index("core") == 0, s0, s1)
    h[...] = jnp.zeros((2, 8, 128), jnp.float32)
    for x in range(2):
        h[x, 2:6, :] = 1.0 / (6.0 + cshift[x])
    rows = lambda k: (slice(16 * k, 16 * k + 16), slice(None))
    post.put(rows(0), w[6], w[0])
    post.put(rows(1), w[7], w[1])
    post.put(rows(2), g[7], g[0])
    post.put((slice(48, 56), slice(0, 128)), h[1], h[0])
    post.both((slice(48, 56), slice(128, 512)), jnp.zeros((8, 384), jnp.float32))


def plane(own, sides, field, p):
    if 0 <= p < 8:
        return lambda a, b: own[field][p, a:b, :]
    side, which, base = PLANES[field, p]
    ref = sides[side][which]
    return lambda a, b: ref[base + a:base + b, :]


def pack_rows(rows, own, sides, post):
    for k, (field, d, p) in enumerate(rows):
        read = plane(own, sides, field, p)
        post.put((slice(k, k + 1), slice(None)), read(16 - d, 17 - d), read(d - 1, d))


def k2(w, g, x1, x0, h, inverse, s0, s1):
    lo, hi = received(lax.axis_index("core") == 0, x0, x1)
    post = Post(lax.rem(lax.axis_index("grp"), 2) == 0, s0, s1)
    pack_rows(NEAR, {"w": w, "g": g}, {"lo": (lo,), "hi": (hi,)}, post)
    post.both((slice(26, 32), slice(None)), jnp.zeros((6, 512), jnp.float32))
    for x in range(2):
        post.both((slice(26, 30), slice(128 * x, 128 * x + 128)), h[x, 2:6, :])
    for half in range(2):
        piece = inverse[32 * half:32 * half + 32, :]
        at = (slice(32, 64), slice(256 * half, 256 * half + 256))
        post.put(at, piece[:, 256:512], piece[:, 0:256])


def fine_sum(ref, p, first, last):
    c = ref[p]
    total = ref[p - 1] + ref[p + 1]
    total = total + pltpu.roll(c, 1, 0) + pltpu.roll(c, 31, 0)
    total = total + jnp.where(first, 0.0, pltpu.roll(c, 1, 1))
    return total + jnp.where(last, 0.0, pltpu.roll(c, 511, 1))


def edges(dims):
    lane = lax.broadcasted_iota(jnp.int32, dims, 1)
    return lane == 0, lane == dims[1] - 1


def line_sides(c, first, last):
    total = jnp.where(first, 0.0, pltpu.roll(c, 1, 1))
    return total + jnp.where(last, 0.0, pltpu.roll(c, 127, 1))


def column_sides(c):
    return pltpu.roll(c, 1, 0) + pltpu.roll(c, 7, 0)


def fill(wide, own, sides, messages):
    zero = jnp.zeros((8, 512), jnp.float32)
    for field in ("w", "g"):
        out = wide[field]
        for i in range(14):
            p = i - 3
            out[i, 0:8, :] = zero
            out[i, 24:32, :] = zero
            known = 0 <= p < 8 or ((field, p) in PLANES and PLANES[field, p][1] < len(sides["lo"]))
            if known:
                out[i, 8:24, :] = plane(own, sides, field, p)(0, 16)
            else:
                out[i, 8:16, :] = zero
                out[i, 16:24, :] = zero
    for rows, lo, hi in messages:
        for k, (field, d, p) in enumerate(rows):
            wide[field][p + 3, 8 - d:9 - d, :] = lo[k:k + 1]
            wide[field][p + 3, 23 + d:24 + d, :] = hi[k:k + 1]


def k3(w, g, x1, x0, y0, y1, h, rhs, inverse, L, CE, u, s1, s0, W, G, V):
    even = lax.axis_index("core") == 0
    xlo, xhi = received(even, x0, x1)
    ylo, yhi = received(lax.rem(lax.axis_index("grp"), 2) == 0, y0, y1)
    post = Post(even, s0, s1)
    own = {"w": w, "g": g}
    fill({"w": W, "g": G}, own, {"lo": (xlo,), "hi": (xhi,)}, [(NEAR, ylo, yhi)])
    first, last = edges((32, 512))
    for i in range(2, 12):
        V[i] = (alpha - beta) * W[i] + (beta * G[i]) * fine_sum(W, i, first, last)
    sums = []
    for x in range(2):
        total = None
        for p in range(4 * x, 4 * x + 4):
            s = fine_sum(V, p + 3, first, last)[8:24]
            r = (1.0 - alpha) * rhs[p] + jnp.where(g[p] > 0.0, s, 0.0)
            total = r if total is None else total + r
        sums.append(total)
    both = jnp.concatenate(sums, axis=0)
    cell = lax.broadcasted_iota(jnp.int32, (512, 128), 0)
    agg = lax.broadcasted_iota(jnp.int32, (512, 128), 1)
    thin = jnp.dot(both, (cell // 4 == agg).astype(jnp.float32), precision=HIGH)
    row = lax.broadcasted_iota(jnp.int32, (16, 32), 0)
    col = lax.broadcasted_iota(jnp.int32, (16, 32), 1)
    x_of, y_of = row // 8, row % 8 - 2
    take = (col // 16 == x_of) & ((col % 16) // 4 == y_of) & (y_of >= 0) & (y_of < 4)
    tiles = jnp.dot(take.astype(jnp.float32), thin, precision=HIGH)
    r = (tiles[0:8], tiles[8:16])
    four = lax.broadcasted_iota(jnp.int32, (8, 128), 0)
    first, last = edges((8, 128))
    lo, hi = xlo[48:56, 0:128], xhi[48:56, 0:128]
    hx = (lo + h[1], h[0] + hi)
    us, hs = [], []
    for x in range(2):
        us.append(r[x] * h[x])
        below = jnp.broadcast_to(ylo[29:30, 128 * x:128 * x + 128], (8, 128))
        above = jnp.broadcast_to(yhi[26:27, 128 * x:128 * x + 128], (8, 128))
        hs.append(jnp.where(four == 1, below, jnp.where(four == 6, above, h[x])))
        u[x] = us[x]
    q = jnp.zeros((8, 128), jnp.float32)
    flat = []
    for x in range(2):
        side = line_sides(us[x], first, last) + column_sides(us[x])
        q = q + (alpha - beta) * us[x] + beta * (hx[x] * us[x] + hs[x] * side)
        flat.append((alpha - beta) * us[x] + beta * hs[x] * (us[1 - x] + side))
    total = 2.0 * q + line_sides(q, first, last) + column_sides(q) + (1.0 - alpha) * (r[0] + r[1])
    total = total - jnp.where(jnp.broadcast_to(lo[2:3], (8, 128)) > 0.0, 0.0, flat[0])
    total = total - jnp.where(jnp.broadcast_to(hi[2:3], (8, 128)) > 0.0, 0.0, flat[1])
    for i in range(64):
        L[i] = total
    CE[:, 256:768] = inverse[...]
    for half in range(2):
        rows, lanes = slice(32 * half, 32 * half + 32), slice(256 * half, 256 * half + 256)
        CE[rows, 0:256] = ylo[32:64, lanes]
        CE[rows, 768:1024] = yhi[32:64, lanes]
    post.put((slice(0, 16), slice(None)), w[5], w[2])
    post.put((slice(16, 32), slice(None)), g[6], g[1])
    tiles = slice(32, 40)
    post.both((tiles, slice(0, 128)), us[0])
    post.both((tiles, slice(128, 256)), us[1])
    post.put((tiles, slice(256, 384)), h[1], h[0])
    post.both((tiles, slice(384, 512)), jnp.zeros((8, 128), jnp.float32))


def k4(w, g, x1, x0, u, h, f1, f0, s0, s1):
    even = lax.axis_index("core") == 0
    lo, hi = received(even, x0, x1)
    flo, fhi = received(even, f0, f1)
    post = Post(lax.rem(lax.axis_index("grp"), 2) == 0, s0, s1)
    pack_rows(FAR, {"w": w, "g": g}, {"lo": (lo,), "hi": (hi,)}, post)
    post.both((slice(22, 24), slice(None)), jnp.zeros((2, 512), jnp.float32))
    tiles = [u[0], u[1], h[0], h[1]]
    for ref in (flo, fhi):
        tiles += [ref[32:40, 128 * k:128 * k + 128] for k in range(4)]
    for k, t in enumerate(tiles):
        row, lane = 24 + 8 * (k // 4), 128 * (k % 4)
        post.both((slice(row, row + 8), slice(lane, lane + 128)), t)


def k5(lines, own, mate, out):
    s = lines[0]
    for i in range(1, 64):
        s = s + lines[i]
    tables = []
    for ref in (own, mate):
        t = ref[:, 0:128] * s[0:1]
        for k in range(1, 8):
            t = t + ref[:, 128 * k:128 * k + 128] * s[k:k + 1]
        tables.append(t)
    even = lax.axis_index("core") == 0
    table = jnp.concatenate([jnp.where(even, *tables), jnp.where(even, *tables[::-1])], axis=0)
    y = lax.dot_general(
        jnp.ones((8, 128), jnp.float32), table, (((1,), (1,)), ((), ())), precision=HIGH
    )
    for i in range(32):
        out[8 * i:8 * i + 8] = y


def prolong_lines(z, upper, k):
    parts = []
    for t in range(4):
        a = jnp.broadcast_to(z[k + 2 * t:k + 2 * t + 1], (8, 512))
        b = jnp.broadcast_to(z[k + 2 * t + 1:k + 2 * t + 2], (8, 512))
        parts.append(jnp.where(upper, a, b))
    return jnp.concatenate(parts, axis=0)


def spread(tiles):
    cell = lax.broadcasted_iota(jnp.int32, (128, 512), 1)
    agg = lax.broadcasted_iota(jnp.int32, (128, 512), 0)
    z = jnp.dot(tiles, (cell // 4 == agg).astype(jnp.float32), precision=HIGH)
    upper = lax.broadcasted_iota(jnp.int32, (8, 512), 0) < 4
    return [prolong_lines(z, upper, k) for k in range(0, tiles.shape[0], 8)]


def k6(terms, w, g, x0, x1, y0, y1, f0, f1, v0, v1, u, h, rho, out, W, G, U0, U1):
    even, row_even = lax.axis_index("core") == 0, lax.rem(lax.axis_index("grp"), 2) == 0
    xlo, xhi = received(even, x0, x1)
    flo, fhi = received(even, f0, f1)
    ylo, yhi = received(row_even, y0, y1)
    vlo, vhi = received(row_even, v0, v1)
    own = {"w": w, "g": g}
    fill({"w": W, "g": G}, own, {"lo": (xlo, flo), "hi": (xhi, fhi)}, [(NEAR, ylo, yhi), (FAR, vlo, vhi)])
    fix = [jnp.zeros((1, 128), jnp.float32)]
    for j in range(-1, 5):
        k = jnp.clip(4 * lax.axis_index("grp") + j, 0, 31)
        fix.append(jnp.sum(terms[pl.ds(pl.multiple_of(8 * k, 8), 8), :], axis=0, keepdims=True))
    fix = jnp.concatenate(fix + [jnp.zeros((1, 128), jnp.float32)], axis=0)
    four = lax.broadcasted_iota(jnp.int32, (8, 128), 0)
    first, last = edges((8, 128))

    def tile(mine, k):
        row, lane = 24 + 8 * (k // 4), 128 * (k % 4)
        below = pltpu.roll(vlo[row:row + 8, lane:lane + 128], 4, 0)
        above = pltpu.roll(vhi[row:row + 8, lane:lane + 128], 4, 0)
        return jnp.where(four < 2, below, jnp.where(four > 5, above, mine))

    far = [[ref[32:40, 128 * k:128 * k + 128] for k in range(3)] for ref in (flo, fhi)]
    us = [tile(far[0][0], 4), tile(far[0][1], 5), tile(u[0], 0), tile(u[1], 1), tile(far[1][0], 8), tile(far[1][1], 9)]
    hs = [tile(far[0][2], 6), tile(h[0], 2), tile(h[1], 3), tile(far[1][2], 10)]
    es = []
    for x in range(4):
        c = us[x + 1]
        s = us[x] + us[x + 2] + line_sides(c, first, last) + column_sides(c)
        es.append(alpha * c + beta * hs[x] * s + fix)
    pro = spread(jnp.concatenate(es, axis=0))
    first, last = edges((32, 512))
    for i in range(1, 13):
        fp = alpha * W[i] + (beta * G[i]) * fine_sum(W, i, first, last)
        U0[i] = fp + jnp.where(G[i] > 0.0, pro[(i + 1) // 4], 0.0)
    for i in range(2, 12):
        U1[i] = (1.0 - c1) * U0[i] + c1 * (W[i] + G[i] * fine_sum(U0, i, first, last))
    for p in range(8):
        i = p + 3
        gp = G[i, 8:24, :]
        solid = ((1.0 - c1) * alpha + c1) * rho[p] + (1.0 - c1) * pro[p // 4 + 1][8:24]
        mid = jnp.where(gp > 0.0, U1[i, 8:24, :], solid)
        s = gp * fine_sum(U1, i, first, last)[8:24]
        out[p] = (1.0 - c2) * mid + c2 * (rho[p] + s)


def swaps(s0, s1, axis, order):
    count, sent, got = lax.axis_size(axis), (s0, s1), [None, None]
    for parity in order:
        pairs = []
        for i in range(parity, count - 1, 2):
            pairs += [(i, i + 1), (i + 1, i)]
        got[parity] = lax.ppermute(sent[parity], axis, pairs)
    return got


def shards(rhs, shift, mask, cshift, inverse):
    field, wide, coarse = shape(8, 16, 512), shape(14, 32, 512), shape(2, 8, 128)
    wide_at = pltpu.VMEM((14, 32, 512), jnp.float32)

    def kernel(name, body, outs, scratch, *args, flops=0):
        with jax.named_scope(name):
            return call(body, outs, scratch, flops=flops)(*args)

    diag = 6.0 + shift
    fluid = mask.astype(jnp.float32)
    rho = rhs / diag
    g = fluid / diag
    w = fluid * rho
    h, s1, s0 = kernel("edges", k1, [coarse, shape(56, 512), shape(56, 512)], [], w, g, cshift)
    x0, x1 = swaps(s0, s1, AGG, (1, 0))
    s0, s1 = kernel("near_rows", k2, [shape(64, 512)] * 2, [], w, g, x1, x0, h, inverse)
    y0, y1 = swaps(s0, s1, "grp", (0, 1))
    lines, table, u, s1, s0 = kernel(
        "residual", k3, [shape(64, 8, 128), shape(64, 1024), coarse, shape(40, 512), shape(40, 512)],
        [wide_at] * 3, w, g, x1, x0, y0, y1, h, rhs, inverse,
    )
    lines = lax.all_to_all(lines, AGG, 0, 0)
    mate = lax.ppermute(table, "core", [(0, 1), (1, 0)])
    f0, f1 = swaps(s0, s1, AGG, (1, 0))
    lines, mate, f1, f0 = lax.optimization_barrier((lines, mate, f1, f0))
    part = kernel("line_product", k5, shape(256, 128), [], lines, table, mate)
    terms = lax.all_to_all(part.reshape(256, 1, 128), ROW, 0, 0).reshape(256, 128)
    s0, s1 = kernel("far_rows", k4, [shape(48, 512)] * 2, [], w, g, x1, x0, u, h, f1, f0, flops=200000)
    v0, v1 = swaps(s0, s1, "grp", (0, 1))
    return kernel(
        "postsmooth", k6, field, [wide_at] * 4,
        terms, w, g, x0, x1, y0, y1, f0, f1, v0, v1, u, h, rho,
    )


def solution(mesh):
    finer = Mesh(mesh.devices.reshape(4, 2, 4, 2, 8), AGG + ("grp",))
    cells = P(AGG, "grp", None)
    return jax.shard_map(
        shards, mesh=finer, in_specs=(cells, cells, cells, cells, P(AGG, "grp")), out_specs=cells,
        check_vma=False,
    )
```

```python
import jax
import jax.numpy as jnp
from jax import lax
from jax.experimental import pallas as pl
from jax.experimental.pallas import tpu as pltpu
from jax.sharding import Mesh, PartitionSpec as P

c1 = 0.5735
c2 = 1.9751
alpha = c1 + c2 - c1 * c2
beta = c1 * c2
AGG = ("x", "zhi", "zlo", "core")
ROW = ("x", "zhi", "zlo", "grp")


NEAR = (
    [("w", 1, p) for p in range(-1, 9)]
    + [("w", 2, p) for p in range(0, 8)]
    + [("g", 1, p) for p in range(0, 8)]
)
FAR = (
    [("w", 1, p) for p in (-2, 9)]
    + [("w", 2, p) for p in (-1, 8)]
    + [("w", 3, p) for p in range(0, 8)]
    + [("g", 1, p) for p in (-1, 8)]
    + [("g", 2, p) for p in range(0, 8)]
)
PLANES = {
    ("w", -2): ("lo", 0, 0, 0), ("w", -1): ("lo", 0, 16, 0), ("g", -1): ("lo", 0, 32, 0),
    ("w", 8): ("hi", 0, 0, 0), ("w", 9): ("hi", 0, 16, 0), ("g", 8): ("hi", 0, 32, 0),
    ("w", -3): ("lo", 1, 0, 0), ("g", -2): ("lo", 1, 0, 512),
    ("w", 10): ("hi", 1, 0, 0), ("g", 9): ("hi", 1, 0, 512),
}
TALL = 24
TOP = 4


def shape(*dims):
    return jax.ShapeDtypeStruct(dims, jnp.float32)


def call(body, outs, scratch=(), mib=8, flops=0, **extra):
    return pl.pallas_call(
        body,
        out_shape=outs,
        scratch_shapes=list(scratch),
        compiler_params=pltpu.CompilerParams(vmem_limit_bytes=mib * 1024 * 1024),
        cost_estimate=pl.CostEstimate(flops=flops, bytes_accessed=flops // 2, transcendentals=0),
        **extra,
    )


class Pick:
    def __init__(self, flag, yes, no):
        self.flag, self.yes, self.no = flag, yes, no

    def __getitem__(self, at):
        return jnp.where(self.flag, self.yes[at], self.no[at])


class Post:
    def __init__(self, even, s0, s1):
        self.even, self.s0, self.s1 = even, s0, s1

    def put(self, at, up, down):
        self.s0[at] = jnp.where(self.even, up, down)
        self.s1[at] = jnp.where(self.even, down, up)

    def both(self, at, value):
        self.s0[at] = value
        self.s1[at] = value


def received(even, r0, r1):
    return Pick(even, r1, r0), Pick(even, r0, r1)


def k1(w, g, cshift, h, s1, s0):
    post = Post(lax.axis_index("core") == 0, s0, s1)
    h[...] = jnp.zeros((2, 8, 128), jnp.float32)
    for x in range(2):
        h[x, 2:6, :] = 1.0 / (6.0 + cshift[x])
    rows = lambda k: (slice(16 * k, 16 * k + 16), slice(None))
    post.put(rows(0), w[6], w[0])
    post.put(rows(1), w[7], w[1])
    post.put(rows(2), g[7], g[0])
    post.put((slice(48, 56), slice(0, 128)), h[1], h[0])
    post.both((slice(48, 56), slice(128, 512)), jnp.zeros((8, 384), jnp.float32))


def plane(own, sides, field, p):
    if 0 <= p < 8:
        return lambda a, b: own[field][p, a:b, :]
    side, which, base, lane = PLANES[field, p]
    ref = sides[side][which]
    return lambda a, b: ref[base + a:base + b, lane:lane + 512]


def pack_rows(rows, own, sides, post):
    for k, (field, d, p) in enumerate(rows):
        read = plane(own, sides, field, p)
        post.put((slice(k, k + 1), slice(None)), read(16 - d, 17 - d), read(d - 1, d))


def k2(w, g, x1, x0, h, inverse, s0, s1):
    lo, hi = received(lax.axis_index("core") == 0, x0, x1)
    post = Post(lax.rem(lax.axis_index("grp"), 2) == 0, s0, s1)
    pack_rows(NEAR, {"w": w, "g": g}, {"lo": (lo,), "hi": (hi,)}, post)
    post.both((slice(26, 32), slice(None)), jnp.zeros((6, 512), jnp.float32))
    for x in range(2):
        post.both((slice(26, 30), slice(128 * x, 128 * x + 128)), h[x, 2:6, :])
    for half in range(2):
        piece = inverse[32 * half:32 * half + 32, :]
        at = (slice(32, 64), slice(256 * half, 256 * half + 256))
        post.put(at, piece[:, 256:512], piece[:, 0:256])


def fine_sum(ref, p, first, last):
    c = ref[p]
    total = ref[p - 1] + ref[p + 1]
    total = total + pltpu.roll(c, 1, 0) + pltpu.roll(c, TALL - 1, 0)
    total = total + jnp.where(first, 0.0, pltpu.roll(c, 1, 1))
    return total + jnp.where(last, 0.0, pltpu.roll(c, 511, 1))


def edges(dims):
    lane = lax.broadcasted_iota(jnp.int32, dims, 1)
    return lane == 0, lane == dims[1] - 1


def line_sides(c, first, last):
    total = jnp.where(first, 0.0, pltpu.roll(c, 1, 1))
    return total + jnp.where(last, 0.0, pltpu.roll(c, 127, 1))


def column_sides(c):
    return pltpu.roll(c, 1, 0) + pltpu.roll(c, 7, 0)


def fill(wide, own, sides, messages):
    zero = jnp.zeros((TOP, 512), jnp.float32)
    for field in ("w", "g"):
        out = wide[field]
        for i in range(14):
            p = i - 3
            out[i, 0:TOP, :] = zero
            out[i, TOP + 16:TALL, :] = zero
            known = 0 <= p < 8 or ((field, p) in PLANES and PLANES[field, p][1] < len(sides["lo"]))
            out[i, TOP:TOP + 16, :] = plane(own, sides, field, p)(0, 16) if known else jnp.zeros((16, 512), jnp.float32)
    for rows, lo, hi in messages:
        for k, (field, d, p) in enumerate(rows):
            wide[field][p + 3, TOP - d:TOP + 1 - d, :] = lo[k:k + 1]
            wide[field][p + 3, TOP + 15 + d:TOP + 16 + d, :] = hi[k:k + 1]


def exact_dot(x, chosen):
    rest, parts = x, []
    for _ in range(3):
        part = rest.astype(jnp.bfloat16)
        parts.append(part)
        rest = rest - part.astype(jnp.float32)
    y = jnp.dot(
        jnp.concatenate(parts, axis=0), chosen.astype(jnp.float32).astype(jnp.bfloat16),
        preferred_element_type=jnp.float32,
    )
    n = x.shape[0]
    return y[0:n] + (y[n:2 * n] + y[2 * n:3 * n])


def k3(w, g, x1, x0, y0, y1, h, rhs, inverse, L, T, u, s1, W, G, V):
    even = lax.axis_index("core") == 0
    xlo, xhi = received(even, x0, x1)
    ylo, yhi = received(lax.rem(lax.axis_index("grp"), 2) == 0, y0, y1)
    own = {"w": w, "g": g}
    fill({"w": W, "g": G}, own, {"lo": (xlo,), "hi": (xhi,)}, [(NEAR, ylo, yhi)])
    first, last = edges((TALL, 512))
    for i in range(2, 12):
        V[i] = (alpha - beta) * W[i] + (beta * G[i]) * fine_sum(W, i, first, last)
    sums = []
    for x in range(2):
        total, right = jnp.zeros((TALL, 512), jnp.float32), rhs[4 * x]
        for p in range(4 * x, 4 * x + 4):
            total = total + jnp.where(G[p + 3] > 0.0, fine_sum(V, p + 3, first, last), 0.0)
            right = right if p == 4 * x else right + rhs[p]
        sums.append(total[TOP:TOP + 16] + (1.0 - alpha) * right)
    cell = lax.broadcasted_iota(jnp.int32, (512, 128), 0)
    agg = lax.broadcasted_iota(jnp.int32, (512, 128), 1)
    thin = exact_dot(jnp.concatenate(sums, axis=0), cell // 4 == agg)
    thin = thin + pltpu.roll(thin, 31, 0)
    thin = thin + pltpu.roll(thin, 30, 0)
    two = jnp.zeros((2, 128), jnp.float32)
    r = [
        jnp.concatenate([two] + [thin[k:k + 1] for k in range(16 * x, 16 * x + 16, 4)] + [two], axis=0)
        for x in range(2)
    ]
    four = lax.broadcasted_iota(jnp.int32, (8, 128), 0)
    first, last = edges((8, 128))
    lo, hi = xlo[48:56, 0:128], xhi[48:56, 0:128]
    hx = (lo + h[1], h[0] + hi)
    us, hs = [], []
    for x in range(2):
        us.append(r[x] * h[x])
        below = jnp.broadcast_to(ylo[29:30, 128 * x:128 * x + 128], (8, 128))
        above = jnp.broadcast_to(yhi[26:27, 128 * x:128 * x + 128], (8, 128))
        hs.append(jnp.where(four == 1, below, jnp.where(four == 6, above, h[x])))
        u[x] = us[x]
    q = jnp.zeros((8, 128), jnp.float32)
    flat = []
    for x in range(2):
        side = line_sides(us[x], first, last) + column_sides(us[x])
        q = q + (alpha - beta) * us[x] + beta * (hx[x] * us[x] + hs[x] * side)
        flat.append((alpha - beta) * us[x] + beta * hs[x] * (us[1 - x] + side))
    total = 2.0 * q + line_sides(q, first, last) + column_sides(q) + (1.0 - alpha) * (r[0] + r[1])
    total = total - jnp.where(jnp.broadcast_to(lo[2:3], (8, 128)) > 0.0, 0.0, flat[0])
    total = total - jnp.where(jnp.broadcast_to(hi[2:3], (8, 128)) > 0.0, 0.0, flat[1])
    for i in range(64):
        L[i] = total
    T[0:64, 256:768] = inverse[...]
    for half in range(2):
        rows, lanes = slice(32 * half, 32 * half + 32), slice(256 * half, 256 * half + 256)
        T[rows, 0:256] = ylo[32:64, lanes]
        T[rows, 768:1024] = yhi[32:64, lanes]
    post = Post(even, T.at[64:88], s1)
    post.put((slice(0, 16), slice(0, 512)), w[5], w[2])
    post.put((slice(0, 16), slice(512, 1024)), g[6], g[1])
    tiles = slice(16, 24)
    post.both((tiles, slice(0, 128)), us[0])
    post.both((tiles, slice(128, 256)), us[1])
    post.put((tiles, slice(256, 384)), h[1], h[0])
    post.both((tiles, slice(384, 1024)), jnp.zeros((8, 640), jnp.float32))


def k4(w, g, x1, x0, u, h, f1, mate, s0, s1):
    even = lax.axis_index("core") == 0
    lo, hi = received(even, x0, x1)
    flo, fhi = received(even, mate.at[64:88], f1)
    post = Post(lax.rem(lax.axis_index("grp"), 2) == 0, s0, s1)
    pack_rows(FAR, {"w": w, "g": g}, {"lo": (lo,), "hi": (hi,)}, post)
    post.both((slice(22, 24), slice(None)), jnp.zeros((2, 512), jnp.float32))
    tiles = [u[0], u[1], h[0], h[1]]
    for ref in (flo, fhi):
        tiles += [ref[16:24, 128 * k:128 * k + 128] for k in range(4)]
    for k, t in enumerate(tiles):
        row, lane = 24 + 8 * (k // 4), 128 * (k % 4)
        post.both((slice(row, row + 8), slice(lane, lane + 128)), t)


def k5(lines, own, mate, out):
    s = [lines[i] for i in range(8)]
    for i in range(8, 64):
        s[i % 8] = s[i % 8] + lines[i]
    while len(s) > 1:
        s = [a + b for a, b in zip(s[::2], s[1::2])]
    s = s[0]
    tables = []
    for ref in (own, mate):
        t = ref[0:64, 0:128] * s[0:1]
        for k in range(1, 8):
            t = t + ref[0:64, 128 * k:128 * k + 128] * s[k:k + 1]
        tables.append(t)
    even = lax.axis_index("core") == 0
    table = jnp.concatenate([jnp.where(even, *tables), jnp.where(even, *tables[::-1])], axis=0)
    y = jnp.broadcast_to(jnp.sum(table.T, axis=0, keepdims=True), (8, 128))
    for i in range(32):
        out[8 * i:8 * i + 8] = y


def spread(tiles):
    cell = lax.broadcasted_iota(jnp.int32, (128, 512), 1)
    agg = lax.broadcasted_iota(jnp.int32, (128, 512), 0)
    z = exact_dot(tiles, cell // 4 == agg)
    upper = lax.broadcasted_iota(jnp.int32, (8, 512), 0) < 4
    planes = []
    for k in range(0, tiles.shape[0], 8):
        parts = []
        for t in range(k + 1, k + 7, 2):
            a = jnp.broadcast_to(z[t:t + 1], (8, 512))
            b = jnp.broadcast_to(z[t + 1:t + 2], (8, 512))
            parts.append(jnp.where(upper, a, b))
        planes.append(jnp.concatenate(parts, axis=0))
    return planes


def k6(terms, w, g, x0, x1, y0, y1, mate, f1, v0, v1, u, h, rho, out, W, G, R, U0, U1, O, sems):
    even, row_even = lax.axis_index("core") == 0, lax.rem(lax.axis_index("grp"), 2) == 0
    xlo, xhi = received(even, x0, x1)
    flo, fhi = received(even, mate.at[64:88], f1)
    ylo, yhi = received(row_even, y0, y1)
    vlo, vhi = received(row_even, v0, v1)
    own = {"w": w, "g": g}
    fill({"w": W, "g": G}, own, {"lo": (xlo, flo), "hi": (xhi, fhi)}, [(NEAR, ylo, yhi), (FAR, vlo, vhi)])
    fix = [jnp.zeros((1, 128), jnp.float32)]
    for j in range(-1, 5):
        k = jnp.clip(4 * lax.axis_index("grp") + j, 0, 31)
        fix.append(jnp.sum(terms[pl.ds(pl.multiple_of(8 * k, 8), 8), :], axis=0, keepdims=True))
    fix = jnp.concatenate(fix + [jnp.zeros((1, 128), jnp.float32)], axis=0)
    four = lax.broadcasted_iota(jnp.int32, (8, 128), 0)
    first, last = edges((8, 128))

    def tile(mine, k):
        row, lane = 24 + 8 * (k // 4), 128 * (k % 4)
        below = pltpu.roll(vlo[row:row + 8, lane:lane + 128], 4, 0)
        above = pltpu.roll(vhi[row:row + 8, lane:lane + 128], 4, 0)
        return jnp.where(four < 2, below, jnp.where(four > 5, above, mine))

    far = [[ref[16:24, 128 * k:128 * k + 128] for k in range(3)] for ref in (flo, fhi)]
    us = [tile(far[0][0], 4), tile(far[0][1], 5), tile(u[0], 0), tile(u[1], 1), tile(far[1][0], 8), tile(far[1][1], 9)]
    hs = [tile(far[0][2], 6), tile(h[0], 2), tile(h[1], 3), tile(far[1][2], 10)]
    es = []
    for x in range(4):
        c = us[x + 1]
        s = us[x] + us[x + 2] + line_sides(c, first, last) + column_sides(c)
        es.append(alpha * c + beta * hs[x] * s + fix)
    pro = spread(jnp.concatenate(es, axis=0))
    first, last = edges((TALL, 512))
    for p in range(8):
        R[p, 0:TOP, :] = jnp.zeros((TOP, 512), jnp.float32)
        R[p, TOP:TOP + 16, :] = rho[p]
        R[p, TOP + 16:TALL, :] = jnp.zeros((TOP, 512), jnp.float32)
    for i in range(1, 13):
        fp = alpha * W[i] + (beta * G[i]) * fine_sum(W, i, first, last)
        U0[i] = fp + jnp.where(G[i] > 0.0, pro[(i + 1) // 4], 0.0)
    for i in range(2, 12):
        U1[i] = (1.0 - c1) * U0[i] + c1 * (W[i] + G[i] * fine_sum(U0, i, first, last))
    copies = []
    for p in range(8):
        i = p + 3
        gp = G[i]
        solid = ((1.0 - c1) * alpha + c1) * R[p] + (1.0 - c1) * pro[p // 4 + 1]
        mid = jnp.where(gp > 0.0, U1[i], solid)
        new = (1.0 - c2) * mid + c2 * (R[p] + gp * fine_sum(U1, i, first, last))
        O[p] = new[TOP:TOP + 16]
        copies.append(pltpu.make_async_copy(O.at[p], out.at[p], sems.at[p]))
        copies[-1].start()
    for c in copies:
        c.wait()


def swaps(s0, s1, axis, order):
    count, sent, got = lax.axis_size(axis), (s0, s1), [None, None]
    for parity in order:
        pairs = []
        for i in range(parity, count - 1, 2):
            pairs += [(i, i + 1), (i + 1, i)]
        got[parity] = lax.ppermute(sent[parity], axis, pairs)
    return got


def shards(rhs, shift, mask, cshift, inverse):
    field, coarse = shape(8, 16, 512), shape(2, 8, 128)
    wide = pltpu.VMEM((14, TALL, 512), jnp.float32)

    def kernel(name, body, outs, scratch, *args, flops=0, **extra):
        with jax.named_scope(name):
            return call(body, outs, scratch, flops=flops, **extra)(*args)

    inv = 1.0 / (6.0 + shift)
    fluid = mask.astype(jnp.float32)
    rho = rhs * inv
    g = fluid * inv
    w = fluid * rho
    h, s1, s0 = kernel("edges", k1, [coarse, shape(56, 512), shape(56, 512)], [], w, g, cshift)
    x0, x1 = swaps(s0, s1, AGG, (1, 0))
    s0, s1 = kernel("near_rows", k2, [shape(64, 512)] * 2, [], w, g, x1, x0, h, inverse)
    y0, y1 = swaps(s0, s1, "grp", (0, 1))
    lines, table, u, s1 = kernel(
        "residual", k3, [shape(64, 8, 128), shape(88, 1024), coarse, shape(24, 1024)],
        [wide] * 3, w, g, x1, x0, y0, y1, h, rhs, inverse,
    )
    lines = lax.all_to_all(lines, AGG, 0, 0)
    mate, f1 = swaps(table, s1, AGG, (1, 0))
    lines, f1, mate = lax.optimization_barrier((lines, f1, mate))
    part = kernel("line_product", k5, shape(256, 128), [], lines, table, mate)
    terms = lax.all_to_all(part.reshape(256, 1, 128), ROW, 0, 0).reshape(256, 128)
    s0, s1 = kernel("far_rows", k4, [shape(48, 512)] * 2, [], w, g, x1, x0, u, h, f1, mate, flops=200000)
    v0, v1 = swaps(s0, s1, "grp", (0, 1))
    own = pltpu.VMEM((8, 16, 512), jnp.float32)
    return kernel(
        "postsmooth", k6, field,
        [wide, wide, pltpu.VMEM((8, TALL, 512), jnp.float32), wide, wide, own, pltpu.SemaphoreType.DMA((8,))],
        terms, w, g, x0, x1, y0, y1, mate, f1, v0, v1, u, h, rho,
        out_specs=pl.BlockSpec(memory_space=pl.ANY),
    )


def solution(mesh):
    finer = Mesh(mesh.devices.reshape(4, 2, 4, 2, 8), AGG + ("grp",))
    cells = P(AGG, "grp", None)
    return jax.shard_map(
        shards, mesh=finer, in_specs=(cells, cells, cells, cells, P(AGG, "grp")), out_specs=cells,
        check_vma=False,
    )
```

```python
import jax
import jax.numpy as jnp
from jax import lax
from jax.experimental import pallas as pl
from jax.experimental.pallas import tpu as pltpu
from jax.sharding import Mesh, PartitionSpec as P

c1 = 0.5735
c2 = 1.9751
alpha = c1 + c2 - c1 * c2
beta = c1 * c2
AGG = ("x", "zhi", "zlo", "core")
ROW = ("x", "zhi", "zlo", "grp")


NEAR = (
    [("w", 1, p) for p in range(-1, 9)]
    + [("w", 2, p) for p in range(0, 8)]
    + [("g", 1, p) for p in range(0, 8)]
)
FAR = (
    [("w", 1, p) for p in (-2, 9)]
    + [("w", 2, p) for p in (-1, 8)]
    + [("w", 3, p) for p in range(0, 8)]
    + [("g", 1, p) for p in (-1, 8)]
    + [("g", 2, p) for p in range(0, 8)]
)
PLANES = {
    ("w", -2): ("lo", 0, 0, 0), ("w", -1): ("lo", 0, 16, 0), ("g", -1): ("lo", 0, 32, 0),
    ("w", 8): ("hi", 0, 0, 0), ("w", 9): ("hi", 0, 16, 0), ("g", 8): ("hi", 0, 32, 0),
    ("w", -3): ("lo", 1, 0, 0), ("g", -2): ("lo", 1, 0, 512),
    ("w", 10): ("hi", 1, 0, 0), ("g", 9): ("hi", 1, 0, 512),
}
TALL = 24
TOP = 4


def shape(*dims):
    return jax.ShapeDtypeStruct(dims, jnp.float32)


def call(body, outs, scratch=(), mib=8, flops=0, **extra):
    return pl.pallas_call(
        body,
        out_shape=outs,
        scratch_shapes=list(scratch),
        compiler_params=pltpu.CompilerParams(vmem_limit_bytes=mib * 1024 * 1024),
        cost_estimate=pl.CostEstimate(flops=flops, bytes_accessed=flops // 2, transcendentals=0),
        **extra,
    )


class Pick:
    def __init__(self, flag, yes, no):
        self.flag, self.yes, self.no = flag, yes, no

    def __getitem__(self, at):
        return jnp.where(self.flag, self.yes[at], self.no[at])


class Post:
    def __init__(self, even, s0, s1):
        self.even, self.s0, self.s1 = even, s0, s1

    def put(self, at, up, down):
        self.s0[at] = jnp.where(self.even, up, down)
        self.s1[at] = jnp.where(self.even, down, up)

    def both(self, at, value):
        self.s0[at] = value
        self.s1[at] = value


def received(even, r0, r1):
    return Pick(even, r1, r0), Pick(even, r0, r1)


def k1(w, g, cshift, h, s1, s0):
    post = Post(lax.axis_index("core") == 0, s0, s1)
    h[...] = jnp.zeros((2, 8, 128), jnp.float32)
    for x in range(2):
        h[x, 2:6, :] = 1.0 / (6.0 + cshift[x])
    rows = lambda k: (slice(16 * k, 16 * k + 16), slice(None))
    post.put(rows(0), w[6], w[0])
    post.put(rows(1), w[7], w[1])
    post.put(rows(2), g[7], g[0])
    post.put((slice(48, 56), slice(0, 128)), h[1], h[0])
    post.both((slice(48, 56), slice(128, 512)), jnp.zeros((8, 384), jnp.float32))


def plane(own, sides, field, p):
    if 0 <= p < 8:
        return lambda a, b: own[field][p, a:b, :]
    side, which, base, lane = PLANES[field, p]
    ref = sides[side][which]
    return lambda a, b: ref[base + a:base + b, lane:lane + 512]


def pack_rows(rows, own, sides, post):
    for k, (field, d, p) in enumerate(rows):
        read = plane(own, sides, field, p)
        post.put((slice(k, k + 1), slice(None)), read(16 - d, 17 - d), read(d - 1, d))


def k2(w, g, x1, x0, h, inverse, s0, s1):
    lo, hi = received(lax.axis_index("core") == 0, x0, x1)
    post = Post(lax.rem(lax.axis_index("grp"), 2) == 0, s0, s1)
    pack_rows(NEAR, {"w": w, "g": g}, {"lo": (lo,), "hi": (hi,)}, post)
    post.both((slice(26, 32), slice(None)), jnp.zeros((6, 512), jnp.float32))
    for x in range(2):
        post.both((slice(26, 30), slice(128 * x, 128 * x + 128)), h[x, 2:6, :])
    for half in range(2):
        piece = inverse[32 * half:32 * half + 32, :]
        at = (slice(32, 64), slice(256 * half, 256 * half + 256))
        post.put(at, piece[:, 256:512], piece[:, 0:256])


def fine_sum(ref, p, first, last):
    c = ref[p]
    total = ref[p - 1] + ref[p + 1]
    total = total + pltpu.roll(c, 1, 0) + pltpu.roll(c, TALL - 1, 0)
    total = total + jnp.where(first, 0.0, pltpu.roll(c, 1, 1))
    return total + jnp.where(last, 0.0, pltpu.roll(c, 511, 1))


def edges(dims):
    lane = lax.broadcasted_iota(jnp.int32, dims, 1)
    return lane == 0, lane == dims[1] - 1


def line_sides(c, first, last):
    total = jnp.where(first, 0.0, pltpu.roll(c, 1, 1))
    return total + jnp.where(last, 0.0, pltpu.roll(c, 127, 1))


def column_sides(c):
    return pltpu.roll(c, 1, 0) + pltpu.roll(c, 7, 0)


def fill(wide, own, sides, messages):
    zero = jnp.zeros((TOP, 512), jnp.float32)
    for field in ("w", "g"):
        out = wide[field]
        for i in range(14):
            p = i - 3
            out[i, 0:TOP, :] = zero
            out[i, TOP + 16:TALL, :] = zero
            known = 0 <= p < 8 or ((field, p) in PLANES and PLANES[field, p][1] < len(sides["lo"]))
            out[i, TOP:TOP + 16, :] = plane(own, sides, field, p)(0, 16) if known else jnp.zeros((16, 512), jnp.float32)
    for rows, lo, hi in messages:
        for k, (field, d, p) in enumerate(rows):
            wide[field][p + 3, TOP - d:TOP + 1 - d, :] = lo[k:k + 1]
            wide[field][p + 3, TOP + 15 + d:TOP + 16 + d, :] = hi[k:k + 1]


def exact_dot(x, chosen):
    rest, parts = x, []
    for _ in range(3):
        part = rest.astype(jnp.bfloat16)
        parts.append(part)
        rest = rest - part.astype(jnp.float32)
    y = jnp.dot(
        jnp.concatenate(parts, axis=0), chosen.astype(jnp.float32).astype(jnp.bfloat16),
        preferred_element_type=jnp.float32,
    )
    n = x.shape[0]
    return y[0:n] + (y[n:2 * n] + y[2 * n:3 * n])


def k3(w, g, x1, x0, y0, y1, h, rhs, inverse, L, T, u, s1, W, G, V):
    even = lax.axis_index("core") == 0
    xlo, xhi = received(even, x0, x1)
    ylo, yhi = received(lax.rem(lax.axis_index("grp"), 2) == 0, y0, y1)
    own = {"w": w, "g": g}
    fill({"w": W, "g": G}, own, {"lo": (xlo,), "hi": (xhi,)}, [(NEAR, ylo, yhi)])
    first, last = edges((TALL, 512))
    for i in range(2, 12):
        V[i] = (alpha - beta) * W[i] + (beta * G[i]) * fine_sum(W, i, first, last)
    sums = []
    for x in range(2):
        total, right = jnp.zeros((TALL, 512), jnp.float32), rhs[4 * x]
        for p in range(4 * x, 4 * x + 4):
            total = total + jnp.where(G[p + 3] > 0.0, fine_sum(V, p + 3, first, last), 0.0)
            right = right if p == 4 * x else right + rhs[p]
        sums.append(total[TOP:TOP + 16] + (1.0 - alpha) * right)
    cell = lax.broadcasted_iota(jnp.int32, (512, 128), 0)
    agg = lax.broadcasted_iota(jnp.int32, (512, 128), 1)
    thin = exact_dot(jnp.concatenate(sums, axis=0), cell // 4 == agg)
    thin = thin + pltpu.roll(thin, 31, 0)
    thin = thin + pltpu.roll(thin, 30, 0)
    two = jnp.zeros((2, 128), jnp.float32)
    r = [
        jnp.concatenate([two] + [thin[k:k + 1] for k in range(16 * x, 16 * x + 16, 4)] + [two], axis=0)
        for x in range(2)
    ]
    four = lax.broadcasted_iota(jnp.int32, (8, 128), 0)
    first, last = edges((8, 128))
    lo, hi = xlo[48:56, 0:128], xhi[48:56, 0:128]
    hx = (lo + h[1], h[0] + hi)
    us, hs = [], []
    for x in range(2):
        us.append(r[x] * h[x])
        below = jnp.broadcast_to(ylo[29:30, 128 * x:128 * x + 128], (8, 128))
        above = jnp.broadcast_to(yhi[26:27, 128 * x:128 * x + 128], (8, 128))
        hs.append(jnp.where(four == 1, below, jnp.where(four == 6, above, h[x])))
        u[x] = us[x]
    q = jnp.zeros((8, 128), jnp.float32)
    flat = []
    for x in range(2):
        side = line_sides(us[x], first, last) + column_sides(us[x])
        q = q + (alpha - beta) * us[x] + beta * (hx[x] * us[x] + hs[x] * side)
        flat.append((alpha - beta) * us[x] + beta * hs[x] * (us[1 - x] + side))
    total = 2.0 * q + line_sides(q, first, last) + column_sides(q) + (1.0 - alpha) * (r[0] + r[1])
    total = total - jnp.where(jnp.broadcast_to(lo[2:3], (8, 128)) > 0.0, 0.0, flat[0])
    total = total - jnp.where(jnp.broadcast_to(hi[2:3], (8, 128)) > 0.0, 0.0, flat[1])
    for i in range(64):
        L[i] = total
    T[0:64, 256:768] = inverse[...]
    for half in range(2):
        rows, lanes = slice(32 * half, 32 * half + 32), slice(256 * half, 256 * half + 256)
        T[rows, 0:256] = ylo[32:64, lanes]
        T[rows, 768:1024] = yhi[32:64, lanes]
    post = Post(even, T.at[64:88], s1)
    post.put((slice(0, 16), slice(0, 512)), w[5], w[2])
    post.put((slice(0, 16), slice(512, 1024)), g[6], g[1])
    tiles = slice(16, 24)
    post.both((tiles, slice(0, 128)), us[0])
    post.both((tiles, slice(128, 256)), us[1])
    post.put((tiles, slice(256, 384)), h[1], h[0])
    post.both((tiles, slice(384, 1024)), jnp.zeros((8, 640), jnp.float32))


def k4(w, g, x1, x0, u, h, f1, mate, s0, s1):
    even = lax.axis_index("core") == 0
    lo, hi = received(even, x0, x1)
    flo, fhi = received(even, mate.at[64:88], f1)
    post = Post(lax.rem(lax.axis_index("grp"), 2) == 0, s0, s1)
    pack_rows(FAR, {"w": w, "g": g}, {"lo": (lo,), "hi": (hi,)}, post)
    post.both((slice(22, 24), slice(None)), jnp.zeros((2, 512), jnp.float32))
    tiles = [u[0], u[1], h[0], h[1]]
    for ref in (flo, fhi):
        tiles += [ref[16:24, 128 * k:128 * k + 128] for k in range(4)]
    for k, t in enumerate(tiles):
        row, lane = 24 + 8 * (k // 4), 128 * (k % 4)
        post.both((slice(row, row + 8), slice(lane, lane + 128)), t)


def k5(lines, own, mate, out):
    s = [lines[i] for i in range(8)]
    for i in range(8, 64):
        s[i % 8] = s[i % 8] + lines[i]
    while len(s) > 1:
        s = [a + b for a, b in zip(s[::2], s[1::2])]
    s = s[0]
    tables = []
    for ref in (own, mate):
        t = ref[0:64, 0:128] * s[0:1]
        for k in range(1, 8):
            t = t + ref[0:64, 128 * k:128 * k + 128] * s[k:k + 1]
        tables.append(t)
    even = lax.axis_index("core") == 0
    table = jnp.concatenate([jnp.where(even, *tables), jnp.where(even, *tables[::-1])], axis=0)
    y = jnp.broadcast_to(jnp.sum(table.T, axis=0, keepdims=True), (8, 128))
    for i in range(32):
        out[8 * i:8 * i + 8] = y


def spread(tiles):
    cell = lax.broadcasted_iota(jnp.int32, (128, 512), 1)
    agg = lax.broadcasted_iota(jnp.int32, (128, 512), 0)
    z = exact_dot(tiles, cell // 4 == agg)
    upper = lax.broadcasted_iota(jnp.int32, (8, 512), 0) < 4
    planes = []
    for k in range(0, tiles.shape[0], 8):
        parts = []
        for t in range(k + 1, k + 7, 2):
            a = jnp.broadcast_to(z[t:t + 1], (8, 512))
            b = jnp.broadcast_to(z[t + 1:t + 2], (8, 512))
            parts.append(jnp.where(upper, a, b))
        planes.append(jnp.concatenate(parts, axis=0))
    return planes


def k6(w, g, x0, x1, y0, y1, mate, f1, v0, v1, u, h, A, W, G):
    even, row_even = lax.axis_index("core") == 0, lax.rem(lax.axis_index("grp"), 2) == 0
    xlo, xhi = received(even, x0, x1)
    flo, fhi = received(even, mate.at[64:88], f1)
    ylo, yhi = received(row_even, y0, y1)
    vlo, vhi = received(row_even, v0, v1)
    own = {"w": w, "g": g}
    fill({"w": W, "g": G}, own, {"lo": (xlo, flo), "hi": (xhi, fhi)}, [(NEAR, ylo, yhi), (FAR, vlo, vhi)])
    four = lax.broadcasted_iota(jnp.int32, (8, 128), 0)
    first, last = edges((8, 128))

    def tile(mine, k):
        row, lane = 24 + 8 * (k // 4), 128 * (k % 4)
        below = pltpu.roll(vlo[row:row + 8, lane:lane + 128], 4, 0)
        above = pltpu.roll(vhi[row:row + 8, lane:lane + 128], 4, 0)
        return jnp.where(four < 2, below, jnp.where(four > 5, above, mine))

    far = [[ref[16:24, 128 * k:128 * k + 128] for k in range(3)] for ref in (flo, fhi)]
    us = [tile(far[0][0], 4), tile(far[0][1], 5), tile(u[0], 0), tile(u[1], 1), tile(far[1][0], 8), tile(far[1][1], 9)]
    hs = [tile(far[0][2], 6), tile(h[0], 2), tile(h[1], 3), tile(far[1][2], 10)]
    for x in range(4):
        c = us[x + 1]
        s = us[x] + us[x + 2] + line_sides(c, first, last) + column_sides(c)
        A[34, 0:8, 128 * x:128 * x + 128] = alpha * c + beta * hs[x] * s
    first, last = edges((TALL, 512))
    for i in range(1, 13):
        A[i + 21] = alpha * W[i] + (beta * G[i]) * fine_sum(W, i, first, last)
        A[i + 9] = G[i]
        if 2 <= i < 12:
            A[i - 2] = W[i]
    A[34, 8:TALL, :] = jnp.zeros((TALL - 8, 512), jnp.float32)


def k7(terms, A, rho, out, R, U0, U1, O, sems):
    fix = [jnp.zeros((1, 128), jnp.float32)]
    for j in range(-1, 5):
        k = jnp.clip(4 * lax.axis_index("grp") + j, 0, 31)
        fix.append(jnp.sum(terms[pl.ds(pl.multiple_of(8 * k, 8), 8), :], axis=0, keepdims=True))
    fix = jnp.concatenate(fix + [jnp.zeros((1, 128), jnp.float32)], axis=0)
    pro = spread(jnp.concatenate([A[34, 0:8, 128 * x:128 * x + 128] + fix for x in range(4)], axis=0))
    first, last = edges((TALL, 512))
    for p in range(8):
        R[p, 0:TOP, :] = jnp.zeros((TOP, 512), jnp.float32)
        R[p, TOP:TOP + 16, :] = rho[p]
        R[p, TOP + 16:TALL, :] = jnp.zeros((TOP, 512), jnp.float32)
    for i in range(1, 13):
        U0[i] = A[i + 21] + jnp.where(A[i + 9] > 0.0, pro[(i + 1) // 4], 0.0)
    for i in range(2, 12):
        U1[i] = (1.0 - c1) * U0[i] + c1 * (A[i - 2] + A[i + 9] * fine_sum(U0, i, first, last))
    copies = []
    for p in range(8):
        i = p + 3
        gp = A[i + 9]
        solid = ((1.0 - c1) * alpha + c1) * R[p] + (1.0 - c1) * pro[p // 4 + 1]
        mid = jnp.where(gp > 0.0, U1[i], solid)
        new = (1.0 - c2) * mid + c2 * (R[p] + gp * fine_sum(U1, i, first, last))
        O[p] = new[TOP:TOP + 16]
        copies.append(pltpu.make_async_copy(O.at[p], out.at[p], sems.at[p]))
        copies[-1].start()
    for c in copies:
        c.wait()


def swaps(s0, s1, axis, order):
    count, sent, got = lax.axis_size(axis), (s0, s1), [None, None]
    for parity in order:
        pairs = []
        for i in range(parity, count - 1, 2):
            pairs += [(i, i + 1), (i + 1, i)]
        got[parity] = lax.ppermute(sent[parity], axis, pairs)
    return got


def shards(rhs, shift, mask, cshift, inverse):
    field, coarse = shape(8, 16, 512), shape(2, 8, 128)
    wide = pltpu.VMEM((14, TALL, 512), jnp.float32)

    def kernel(name, body, outs, scratch, *args, flops=0, **extra):
        with jax.named_scope(name):
            return call(body, outs, scratch, flops=flops, **extra)(*args)

    inv = 1.0 / (6.0 + shift)
    fluid = mask.astype(jnp.float32)
    rho = rhs * inv
    g = fluid * inv
    w = fluid * rho
    h, s1, s0 = kernel("edges", k1, [coarse, shape(56, 512), shape(56, 512)], [], w, g, cshift)
    x0, x1 = swaps(s0, s1, AGG, (1, 0))
    s0, s1 = kernel("near_rows", k2, [shape(64, 512)] * 2, [], w, g, x1, x0, h, inverse)
    y0, y1 = swaps(s0, s1, "grp", (0, 1))
    lines, table, u, s1 = kernel(
        "residual", k3, [shape(64, 8, 128), shape(88, 1024), coarse, shape(24, 1024)],
        [wide] * 3, w, g, x1, x0, y0, y1, h, rhs, inverse,
    )
    lines = lax.all_to_all(lines, AGG, 0, 0)
    mate, f1 = swaps(table, s1, AGG, (1, 0))
    lines, mate, f1 = lax.optimization_barrier((lines, mate, f1))
    part = kernel("line_product", k5, shape(256, 128), [], lines, table, mate)
    terms = lax.all_to_all(part.reshape(256, 1, 128), ROW, 0, 0).reshape(256, 128)
    s0, s1 = kernel("far_rows", k4, [shape(48, 512)] * 2, [], w, g, x1, x0, u, h, f1, mate, flops=200000)
    v0, v1 = swaps(s0, s1, "grp", (0, 1))
    own = pltpu.VMEM((8, 16, 512), jnp.float32)
    known = kernel(
        "presmooth", k6, shape(35, TALL, 512), [wide, wide],
        w, g, x0, x1, y0, y1, mate, f1, v0, v1, u, h, flops=4000000,
    )
    return kernel(
        "postsmooth", k7, field,
        [pltpu.VMEM((8, TALL, 512), jnp.float32), wide, wide, own, pltpu.SemaphoreType.DMA((8,))],
        terms, known, rho, out_specs=pl.BlockSpec(memory_space=pl.ANY),
    )


def solution(mesh):
    finer = Mesh(mesh.devices.reshape(4, 2, 4, 2, 8), AGG + ("grp",))
    cells = P(AGG, "grp", None)
    return jax.shard_map(
        shards, mesh=finer, in_specs=(cells, cells, cells, cells, P(AGG, "grp")), out_specs=cells,
        check_vma=False,
    )
```

```python
import jax
import jax.numpy as jnp
from jax import lax
from jax.experimental import pallas as pl
from jax.experimental.pallas import tpu as pltpu
from jax.sharding import Mesh, PartitionSpec as P

c1 = 0.5735
c2 = 1.9751
alpha = c1 + c2 - c1 * c2
beta = c1 * c2
AGG = ("x", "zhi", "zlo", "core")
ROW = ("x", "zhi", "zlo", "grp")


NEAR = (
    [("w", 1, p) for p in range(-1, 9)]
    + [("w", 2, p) for p in range(0, 8)]
    + [("g", 1, p) for p in range(0, 8)]
)
FAR = (
    [("w", 1, p) for p in (-2, 9)]
    + [("w", 2, p) for p in (-1, 8)]
    + [("w", 3, p) for p in range(0, 8)]
    + [("g", 1, p) for p in (-1, 8)]
    + [("g", 2, p) for p in range(0, 8)]
)
PLANES = {
    ("w", -2): ("lo", 0, 0, 0), ("w", -1): ("lo", 0, 16, 0), ("g", -1): ("lo", 0, 32, 0),
    ("w", 8): ("hi", 0, 0, 0), ("w", 9): ("hi", 0, 16, 0), ("g", 8): ("hi", 0, 32, 0),
    ("w", -3): ("lo", 1, 0, 0), ("g", -2): ("lo", 1, 0, 512),
    ("w", 10): ("hi", 1, 0, 0), ("g", 9): ("hi", 1, 0, 512),
}
TALL = 24
TOP = 4


def shape(*dims):
    return jax.ShapeDtypeStruct(dims, jnp.float32)


def call(body, outs, scratch=(), mib=8, flops=0, **extra):
    return pl.pallas_call(
        body,
        out_shape=outs,
        scratch_shapes=list(scratch),
        compiler_params=pltpu.CompilerParams(vmem_limit_bytes=mib * 1024 * 1024),
        cost_estimate=pl.CostEstimate(flops=flops, bytes_accessed=flops // 2, transcendentals=0),
        **extra,
    )


class Pick:
    def __init__(self, flag, yes, no):
        self.flag, self.yes, self.no = flag, yes, no

    def __getitem__(self, at):
        return jnp.where(self.flag, self.yes[at], self.no[at])


class Post:
    def __init__(self, even, s0, s1):
        self.even, self.s0, self.s1 = even, s0, s1

    def put(self, at, up, down):
        self.s0[at] = jnp.where(self.even, up, down)
        self.s1[at] = jnp.where(self.even, down, up)

    def both(self, at, value):
        self.s0[at] = value
        self.s1[at] = value


def received(even, r0, r1):
    return Pick(even, r1, r0), Pick(even, r0, r1)


def k1(w, g, cshift, h, s1, s0):
    post = Post(lax.axis_index("core") == 0, s0, s1)
    h[...] = jnp.zeros((2, 8, 128), jnp.float32)
    for x in range(2):
        h[x, 2:6, :] = 1.0 / (6.0 + cshift[x])
    rows = lambda k: (slice(16 * k, 16 * k + 16), slice(None))
    post.put(rows(0), w[6], w[0])
    post.put(rows(1), w[7], w[1])
    post.put(rows(2), g[7], g[0])
    post.put((slice(48, 56), slice(0, 128)), h[1], h[0])
    post.both((slice(48, 56), slice(128, 512)), jnp.zeros((8, 384), jnp.float32))


def plane(own, sides, field, p):
    if 0 <= p < 8:
        return lambda a, b: own[field][p, a:b, :]
    side, which, base, lane = PLANES[field, p]
    ref = sides[side][which]
    return lambda a, b: ref[base + a:base + b, lane:lane + 512]


def pack_rows(rows, own, sides, post):
    for k, (field, d, p) in enumerate(rows):
        read = plane(own, sides, field, p)
        post.put((slice(k, k + 1), slice(None)), read(16 - d, 17 - d), read(d - 1, d))


def k2(w, g, x1, x0, h, inverse, s0, s1):
    lo, hi = received(lax.axis_index("core") == 0, x0, x1)
    post = Post(lax.rem(lax.axis_index("grp"), 2) == 0, s0, s1)
    pack_rows(NEAR, {"w": w, "g": g}, {"lo": (lo,), "hi": (hi,)}, post)
    post.both((slice(26, 32), slice(None)), jnp.zeros((6, 512), jnp.float32))
    for x in range(2):
        post.both((slice(26, 30), slice(128 * x, 128 * x + 128)), h[x, 2:6, :])
    for half in range(2):
        piece = inverse[32 * half:32 * half + 32, :]
        at = (slice(32, 64), slice(256 * half, 256 * half + 256))
        post.put(at, piece[:, 256:512], piece[:, 0:256])


def fine_sum(ref, p, first, last):
    c = ref[p]
    total = ref[p - 1] + ref[p + 1]
    total = total + pltpu.roll(c, 1, 0) + pltpu.roll(c, TALL - 1, 0)
    total = total + jnp.where(first, 0.0, pltpu.roll(c, 1, 1))
    return total + jnp.where(last, 0.0, pltpu.roll(c, 511, 1))


def edges(dims):
    lane = lax.broadcasted_iota(jnp.int32, dims, 1)
    return lane == 0, lane == dims[1] - 1


def line_sides(c, first, last):
    total = jnp.where(first, 0.0, pltpu.roll(c, 1, 1))
    return total + jnp.where(last, 0.0, pltpu.roll(c, 127, 1))


def column_sides(c):
    return pltpu.roll(c, 1, 0) + pltpu.roll(c, 7, 0)


def fill(wide, own, sides, messages):
    zero = jnp.zeros((TOP, 512), jnp.float32)
    for field in ("w", "g"):
        out = wide[field]
        for i in range(14):
            p = i - 3
            out[i, 0:TOP, :] = zero
            out[i, TOP + 16:TALL, :] = zero
            known = 0 <= p < 8 or ((field, p) in PLANES and PLANES[field, p][1] < len(sides["lo"]))
            out[i, TOP:TOP + 16, :] = plane(own, sides, field, p)(0, 16) if known else jnp.zeros((16, 512), jnp.float32)
    for rows, lo, hi in messages:
        for k, (field, d, p) in enumerate(rows):
            wide[field][p + 3, TOP - d:TOP + 1 - d, :] = lo[k:k + 1]
            wide[field][p + 3, TOP + 15 + d:TOP + 16 + d, :] = hi[k:k + 1]


def exact_dot(x, chosen):
    rest, parts = x, []
    for _ in range(3):
        part = rest.astype(jnp.bfloat16)
        parts.append(part)
        rest = rest - part.astype(jnp.float32)
    y = jnp.dot(
        jnp.concatenate(parts, axis=0), chosen.astype(jnp.float32).astype(jnp.bfloat16),
        preferred_element_type=jnp.float32,
    )
    n = x.shape[0]
    return y[0:n] + (y[n:2 * n] + y[2 * n:3 * n])


def k3(w, g, x1, x0, y0, y1, h, part, inverse, L, T, u, s1, W, G, V):
    even = lax.axis_index("core") == 0
    xlo, xhi = received(even, x0, x1)
    ylo, yhi = received(lax.rem(lax.axis_index("grp"), 2) == 0, y0, y1)
    own = {"w": w, "g": g}
    fill({"w": W, "g": G}, own, {"lo": (xlo,), "hi": (xhi,)}, [(NEAR, ylo, yhi)])
    first, last = edges((TALL, 512))
    for i in range(2, 12):
        V[i] = (alpha - beta) * W[i] + (beta * G[i]) * fine_sum(W, i, first, last)
    sums = []
    for x in range(2):
        total, right = jnp.zeros((TALL, 512), jnp.float32), part[4 * x]
        for p in range(4 * x, 4 * x + 4):
            total = total + jnp.where(G[p + 3] > 0.0, fine_sum(V, p + 3, first, last), 0.0)
            right = right if p == 4 * x else right + part[p]
        sums.append(total[TOP:TOP + 16] + right)
    cell = lax.broadcasted_iota(jnp.int32, (512, 128), 0)
    agg = lax.broadcasted_iota(jnp.int32, (512, 128), 1)
    thin = exact_dot(jnp.concatenate(sums, axis=0), cell // 4 == agg)
    thin = thin + pltpu.roll(thin, 31, 0)
    thin = thin + pltpu.roll(thin, 30, 0)
    two = jnp.zeros((2, 128), jnp.float32)
    r = [
        jnp.concatenate([two] + [thin[k:k + 1] for k in range(16 * x, 16 * x + 16, 4)] + [two], axis=0)
        for x in range(2)
    ]
    four = lax.broadcasted_iota(jnp.int32, (8, 128), 0)
    first, last = edges((8, 128))
    lo, hi = xlo[48:56, 0:128], xhi[48:56, 0:128]
    hx = (lo + h[1], h[0] + hi)
    us, hs = [], []
    for x in range(2):
        us.append(r[x] * h[x])
        below = jnp.broadcast_to(ylo[29:30, 128 * x:128 * x + 128], (8, 128))
        above = jnp.broadcast_to(yhi[26:27, 128 * x:128 * x + 128], (8, 128))
        hs.append(jnp.where(four == 1, below, jnp.where(four == 6, above, h[x])))
        u[x] = us[x]
    q = jnp.zeros((8, 128), jnp.float32)
    flat = []
    for x in range(2):
        side = line_sides(us[x], first, last) + column_sides(us[x])
        q = q + (alpha - beta) * us[x] + beta * (hx[x] * us[x] + hs[x] * side)
        flat.append((alpha - beta) * us[x] + beta * hs[x] * (us[1 - x] + side))
    total = 2.0 * q + line_sides(q, first, last) + column_sides(q) + (1.0 - alpha) * (r[0] + r[1])
    total = total - jnp.where(jnp.broadcast_to(lo[2:3], (8, 128)) > 0.0, 0.0, flat[0])
    total = total - jnp.where(jnp.broadcast_to(hi[2:3], (8, 128)) > 0.0, 0.0, flat[1])
    for i in range(64):
        L[i] = total
    T[0:64, 256:768] = inverse[...]
    for half in range(2):
        rows, lanes = slice(32 * half, 32 * half + 32), slice(256 * half, 256 * half + 256)
        T[rows, 0:256] = ylo[32:64, lanes]
        T[rows, 768:1024] = yhi[32:64, lanes]
    post = Post(even, T.at[64:88], s1)
    post.put((slice(0, 16), slice(0, 512)), w[5], w[2])
    post.put((slice(0, 16), slice(512, 1024)), g[6], g[1])
    tiles = slice(16, 24)
    post.both((tiles, slice(0, 128)), us[0])
    post.both((tiles, slice(128, 256)), us[1])
    post.put((tiles, slice(256, 384)), h[1], h[0])
    post.both((tiles, slice(384, 1024)), jnp.zeros((8, 640), jnp.float32))


def k4(w, g, x1, x0, u, h, f1, mate, s0, s1):
    even = lax.axis_index("core") == 0
    lo, hi = received(even, x0, x1)
    flo, fhi = received(even, mate.at[64:88], f1)
    post = Post(lax.rem(lax.axis_index("grp"), 2) == 0, s0, s1)
    pack_rows(FAR, {"w": w, "g": g}, {"lo": (lo,), "hi": (hi,)}, post)
    post.both((slice(22, 24), slice(None)), jnp.zeros((2, 512), jnp.float32))
    tiles = [u[0], u[1], h[0], h[1]]
    for ref in (flo, fhi):
        tiles += [ref[16:24, 128 * k:128 * k + 128] for k in range(4)]
    for k, t in enumerate(tiles):
        row, lane = 24 + 8 * (k // 4), 128 * (k % 4)
        post.both((slice(row, row + 8), slice(lane, lane + 128)), t)


def k5(lines, own, mate, out):
    s = [lines[i] for i in range(8)]
    for i in range(8, 64):
        s[i % 8] = s[i % 8] + lines[i]
    while len(s) > 1:
        s = [a + b for a, b in zip(s[::2], s[1::2])]
    s = s[0]
    tables = []
    for ref in (own, mate):
        t = ref[0:64, 0:128] * s[0:1]
        for k in range(1, 8):
            t = t + ref[0:64, 128 * k:128 * k + 128] * s[k:k + 1]
        tables.append(t)
    even = lax.axis_index("core") == 0
    table = jnp.concatenate([jnp.where(even, *tables), jnp.where(even, *tables[::-1])], axis=0)
    y = jnp.broadcast_to(jnp.sum(table.T, axis=0, keepdims=True), (8, 128))
    for i in range(32):
        out[8 * i:8 * i + 8] = y


def spread(tiles):
    cell = lax.broadcasted_iota(jnp.int32, (128, 512), 1)
    agg = lax.broadcasted_iota(jnp.int32, (128, 512), 0)
    z = exact_dot(tiles, cell // 4 == agg)
    upper = lax.broadcasted_iota(jnp.int32, (8, 512), 0) < 4
    planes = []
    for k in range(0, tiles.shape[0], 8):
        parts = []
        for t in range(k + 1, k + 7, 2):
            a = jnp.broadcast_to(z[t:t + 1], (8, 512))
            b = jnp.broadcast_to(z[t + 1:t + 2], (8, 512))
            parts.append(jnp.where(upper, a, b))
        planes.append(jnp.concatenate(parts, axis=0))
    return planes


def k6(w, g, x0, x1, y0, y1, mate, f1, v0, v1, u, h, A, W, G):
    even, row_even = lax.axis_index("core") == 0, lax.rem(lax.axis_index("grp"), 2) == 0
    xlo, xhi = received(even, x0, x1)
    flo, fhi = received(even, mate.at[64:88], f1)
    ylo, yhi = received(row_even, y0, y1)
    vlo, vhi = received(row_even, v0, v1)
    own = {"w": w, "g": g}
    fill({"w": W, "g": G}, own, {"lo": (xlo, flo), "hi": (xhi, fhi)}, [(NEAR, ylo, yhi), (FAR, vlo, vhi)])
    four = lax.broadcasted_iota(jnp.int32, (8, 128), 0)
    first, last = edges((8, 128))

    def tile(mine, k):
        row, lane = 24 + 8 * (k // 4), 128 * (k % 4)
        below = pltpu.roll(vlo[row:row + 8, lane:lane + 128], 4, 0)
        above = pltpu.roll(vhi[row:row + 8, lane:lane + 128], 4, 0)
        return jnp.where(four < 2, below, jnp.where(four > 5, above, mine))

    far = [[ref[16:24, 128 * k:128 * k + 128] for k in range(3)] for ref in (flo, fhi)]
    us = [tile(far[0][0], 4), tile(far[0][1], 5), tile(u[0], 0), tile(u[1], 1), tile(far[1][0], 8), tile(far[1][1], 9)]
    hs = [tile(far[0][2], 6), tile(h[0], 2), tile(h[1], 3), tile(far[1][2], 10)]
    for x in range(4):
        c = us[x + 1]
        s = us[x] + us[x + 2] + line_sides(c, first, last) + column_sides(c)
        A[34, 0:8, 128 * x:128 * x + 128] = alpha * c + beta * hs[x] * s
    first, last = edges((TALL, 512))
    for i in range(1, 13):
        A[i + 21] = alpha * W[i] + (beta * G[i]) * fine_sum(W, i, first, last)
        A[i + 9] = G[i]
        if 2 <= i < 12:
            A[i - 2] = W[i]
    A[34, 8:TALL, :] = jnp.zeros((TALL - 8, 512), jnp.float32)


def k7(terms, A, rho, out, R, U0, U1, O, sems):
    fix = [jnp.zeros((1, 128), jnp.float32)]
    for j in range(-1, 5):
        k = jnp.clip(4 * lax.axis_index("grp") + j, 0, 31)
        fix.append(jnp.sum(terms[pl.ds(pl.multiple_of(8 * k, 8), 8), :], axis=0, keepdims=True))
    fix = jnp.concatenate(fix + [jnp.zeros((1, 128), jnp.float32)], axis=0)
    pro = spread(jnp.concatenate([A[34, 0:8, 128 * x:128 * x + 128] + fix for x in range(4)], axis=0))
    first, last = edges((TALL, 512))
    for p in range(8):
        R[p, 0:TOP, :] = jnp.zeros((TOP, 512), jnp.float32)
        R[p, TOP:TOP + 16, :] = rho[p]
        R[p, TOP + 16:TALL, :] = jnp.zeros((TOP, 512), jnp.float32)
    for i in range(1, 13):
        U0[i] = A[i + 21] + jnp.where(A[i + 9] > 0.0, pro[(i + 1) // 4], 0.0)
    for i in range(2, 12):
        U1[i] = (1.0 - c1) * U0[i] + c1 * (A[i - 2] + A[i + 9] * fine_sum(U0, i, first, last))
    copies = []
    for p in range(8):
        i = p + 3
        gp = A[i + 9]
        solid = ((1.0 - c1) * alpha + c1) * R[p] + (1.0 - c1) * pro[p // 4 + 1]
        mid = jnp.where(gp > 0.0, U1[i], solid)
        new = (1.0 - c2) * mid + c2 * (R[p] + gp * fine_sum(U1, i, first, last))
        O[p] = new[TOP:TOP + 16]
        copies.append(pltpu.make_async_copy(O.at[p], out.at[p], sems.at[p]))
        copies[-1].start()
    for c in copies:
        c.wait()


def swaps(s0, s1, axis, order):
    count, sent, got = lax.axis_size(axis), (s0, s1), [None, None]
    for parity in order:
        pairs = []
        for i in range(parity, count - 1, 2):
            pairs += [(i, i + 1), (i + 1, i)]
        got[parity] = lax.ppermute(sent[parity], axis, pairs)
    return got


def shards(rhs, shift, mask, cshift, inverse):
    field, coarse = shape(8, 16, 512), shape(2, 8, 128)
    wide = pltpu.VMEM((14, TALL, 512), jnp.float32)

    def kernel(name, body, outs, scratch, *args, flops=0, **extra):
        with jax.named_scope(name):
            return call(body, outs, scratch, flops=flops, **extra)(*args)

    inv = 1.0 / (6.0 + shift)
    fluid = mask.astype(jnp.float32)
    rho = rhs * inv
    g = fluid * inv
    w = fluid * rho
    part = (1.0 - alpha) * rhs
    h, s1, s0 = kernel("edges", k1, [coarse, shape(56, 512), shape(56, 512)], [], w, g, cshift)
    x0, x1 = swaps(s0, s1, AGG, (1, 0))
    s0, s1 = kernel("near_rows", k2, [shape(64, 512)] * 2, [], w, g, x1, x0, h, inverse)
    y0, y1 = swaps(s0, s1, "grp", (0, 1))
    lines, table, u, s1 = kernel(
        "residual", k3, [shape(64, 8, 128), shape(88, 1024), coarse, shape(24, 1024)],
        [wide] * 3, w, g, x1, x0, y0, y1, h, part, inverse,
    )
    lines = lax.all_to_all(lines, AGG, 0, 0)
    mate, f1 = swaps(table, s1, AGG, (1, 0))
    lines, mate, f1 = lax.optimization_barrier((lines, mate, f1))
    part = kernel("line_product", k5, shape(256, 128), [], lines, table, mate)
    terms = lax.all_to_all(part.reshape(256, 1, 128), ROW, 0, 0).reshape(256, 128)
    s0, s1 = kernel("far_rows", k4, [shape(48, 512)] * 2, [], w, g, x1, x0, u, h, f1, mate, flops=200000)
    v0, v1 = swaps(s0, s1, "grp", (0, 1))
    own = pltpu.VMEM((8, 16, 512), jnp.float32)
    known = kernel(
        "presmooth", k6, shape(35, TALL, 512), [wide, wide],
        w, g, x0, x1, y0, y1, mate, f1, v0, v1, u, h, flops=4000000,
    )
    return kernel(
        "postsmooth", k7, field,
        [pltpu.VMEM((8, TALL, 512), jnp.float32), wide, wide, own, pltpu.SemaphoreType.DMA((8,))],
        terms, known, rho, out_specs=pl.BlockSpec(memory_space=pl.ANY),
    )


def solution(mesh):
    finer = Mesh(mesh.devices.reshape(4, 2, 4, 2, 8), AGG + ("grp",))
    cells = P(AGG, "grp", None)
    return jax.shard_map(
        shards, mesh=finer, in_specs=(cells, cells, cells, cells, P(AGG, "grp")), out_specs=cells,
        check_vma=False,
    )
```

```python
import jax
import jax.numpy as jnp
from jax import lax
from jax.experimental import pallas as pl
from jax.experimental.pallas import tpu as pltpu
from jax.sharding import Mesh, PartitionSpec as P

c1 = 0.5735
c2 = 1.9751
alpha = c1 + c2 - c1 * c2
beta = c1 * c2
AGG = ("x", "zhi", "zlo", "core")
ROW = ("x", "zhi", "zlo", "grp")


NEAR = (
    [("w", 1, p) for p in range(-1, 9)]
    + [("w", 2, p) for p in range(0, 8)]
    + [("g", 1, p) for p in range(0, 8)]
)
FAR = (
    [("w", 1, p) for p in (-2, 9)]
    + [("w", 2, p) for p in (-1, 8)]
    + [("w", 3, p) for p in range(0, 8)]
    + [("g", 1, p) for p in (-1, 8)]
    + [("g", 2, p) for p in range(0, 8)]
)
PLANES = {
    ("w", -2): ("lo", 0, 0, 0), ("w", -1): ("lo", 0, 16, 0), ("g", -1): ("lo", 0, 32, 0),
    ("w", 8): ("hi", 0, 0, 0), ("w", 9): ("hi", 0, 16, 0), ("g", 8): ("hi", 0, 32, 0),
    ("w", -3): ("lo", 1, 0, 0), ("g", -2): ("lo", 1, 0, 512),
    ("w", 10): ("hi", 1, 0, 0), ("g", 9): ("hi", 1, 0, 512),
}
TALL = 24
TOP = 4


def shape(*dims):
    return jax.ShapeDtypeStruct(dims, jnp.float32)


def call(body, outs, scratch=(), mib=8, flops=0, **extra):
    return pl.pallas_call(
        body,
        out_shape=outs,
        scratch_shapes=list(scratch),
        compiler_params=pltpu.CompilerParams(vmem_limit_bytes=mib * 1024 * 1024),
        cost_estimate=pl.CostEstimate(flops=flops, bytes_accessed=flops // 2, transcendentals=0),
        **extra,
    )


class Pick:
    def __init__(self, flag, yes, no):
        self.flag, self.yes, self.no = flag, yes, no

    def __getitem__(self, at):
        return jnp.where(self.flag, self.yes[at], self.no[at])


class Post:
    def __init__(self, even, s0, s1):
        self.even, self.s0, self.s1 = even, s0, s1

    def put(self, at, up, down):
        self.s0[at] = jnp.where(self.even, up, down)
        self.s1[at] = jnp.where(self.even, down, up)

    def both(self, at, value):
        self.s0[at] = value
        self.s1[at] = value


def received(even, r0, r1):
    return Pick(even, r1, r0), Pick(even, r0, r1)


def k1(w, g, cshift, h, s1, s0):
    post = Post(lax.axis_index("core") == 0, s0, s1)
    h[...] = jnp.zeros((2, 8, 128), jnp.float32)
    for x in range(2):
        h[x, 2:6, :] = 1.0 / (6.0 + cshift[x])
    rows = lambda k: (slice(16 * k, 16 * k + 16), slice(None))
    post.put(rows(0), w[6], w[0])
    post.put(rows(1), w[7], w[1])
    post.put(rows(2), g[7], g[0])
    post.put((slice(48, 56), slice(0, 128)), h[1], h[0])
    post.both((slice(48, 56), slice(128, 512)), jnp.zeros((8, 384), jnp.float32))


def plane(own, sides, field, p):
    if 0 <= p < 8:
        return lambda a, b: own[field][p, a:b, :]
    side, which, base, lane = PLANES[field, p]
    ref = sides[side][which]
    return lambda a, b: ref[base + a:base + b, lane:lane + 512]


def pack_rows(rows, own, sides, post):
    for k, (field, d, p) in enumerate(rows):
        read = plane(own, sides, field, p)
        post.put((slice(k, k + 1), slice(None)), read(16 - d, 17 - d), read(d - 1, d))


def k2(w, g, x1, x0, h, inverse, s0, s1):
    lo, hi = received(lax.axis_index("core") == 0, x0, x1)
    post = Post(lax.rem(lax.axis_index("grp"), 2) == 0, s0, s1)
    pack_rows(NEAR, {"w": w, "g": g}, {"lo": (lo,), "hi": (hi,)}, post)
    post.both((slice(26, 32), slice(None)), jnp.zeros((6, 512), jnp.float32))
    for x in range(2):
        post.both((slice(26, 30), slice(128 * x, 128 * x + 128)), h[x, 2:6, :])
    for half in range(2):
        piece = inverse[32 * half:32 * half + 32, :]
        at = (slice(32, 64), slice(256 * half, 256 * half + 256))
        post.put(at, piece[:, 256:512], piece[:, 0:256])


def fine_sum(ref, p, first, last):
    c = ref[p]
    total = ref[p - 1] + ref[p + 1]
    total = total + pltpu.roll(c, 1, 0) + pltpu.roll(c, TALL - 1, 0)
    total = total + jnp.where(first, 0.0, pltpu.roll(c, 1, 1))
    return total + jnp.where(last, 0.0, pltpu.roll(c, 511, 1))


def edges(dims):
    lane = lax.broadcasted_iota(jnp.int32, dims, 1)
    return lane == 0, lane == dims[1] - 1


def line_sides(c, first, last):
    total = jnp.where(first, 0.0, pltpu.roll(c, 1, 1))
    return total + jnp.where(last, 0.0, pltpu.roll(c, 127, 1))


def column_sides(c):
    return pltpu.roll(c, 1, 0) + pltpu.roll(c, 7, 0)


def fill(wide, own, sides, messages):
    zero = jnp.zeros((TOP, 512), jnp.float32)
    for field in ("w", "g"):
        out = wide[field]
        for i in range(14):
            p = i - 3
            out[i, 0:TOP, :] = zero
            out[i, TOP + 16:TALL, :] = zero
            known = 0 <= p < 8 or ((field, p) in PLANES and PLANES[field, p][1] < len(sides["lo"]))
            out[i, TOP:TOP + 16, :] = plane(own, sides, field, p)(0, 16) if known else jnp.zeros((16, 512), jnp.float32)
    for rows, lo, hi in messages:
        for k, (field, d, p) in enumerate(rows):
            wide[field][p + 3, TOP - d:TOP + 1 - d, :] = lo[k:k + 1]
            wide[field][p + 3, TOP + 15 + d:TOP + 16 + d, :] = hi[k:k + 1]


def exact_dot(x, chosen):
    rest, parts = x, []
    for _ in range(3):
        part = rest.astype(jnp.bfloat16)
        parts.append(part)
        rest = rest - part.astype(jnp.float32)
    y = jnp.dot(
        jnp.concatenate(parts, axis=0), chosen.astype(jnp.float32).astype(jnp.bfloat16),
        preferred_element_type=jnp.float32,
    )
    n = x.shape[0]
    return y[0:n] + (y[n:2 * n] + y[2 * n:3 * n])


def restricted(sums):
    cell = lax.broadcasted_iota(jnp.int32, (512, 128), 0)
    agg = lax.broadcasted_iota(jnp.int32, (512, 128), 1)
    return exact_dot(sums, cell // 4 == agg)


def row_sum(planes, p, first, last, top, bottom):
    c = planes(p)
    total = planes(p - 1) + planes(p + 1)
    total = total + jnp.where(top, 0.0, pltpu.roll(c, 1, 0)) + jnp.where(bottom, 0.0, pltpu.roll(c, 15, 0))
    total = total + jnp.where(first, 0.0, pltpu.roll(c, 1, 1))
    return total + jnp.where(last, 0.0, pltpu.roll(c, 511, 1))


def k2b(w, g, x1, x0, part, r, rim, V):
    lo, hi = received(lax.axis_index("core") == 0, x0, x1)
    own, sides = {"w": w, "g": g}, {"lo": (lo,), "hi": (hi,)}
    ws = lambda p: plane(own, sides, "w", p)(0, 16)
    gs = lambda p: plane(own, sides, "g", p)(0, 16)
    first, last = edges((16, 512))
    row = lax.broadcasted_iota(jnp.int32, (16, 512), 0)
    top, bottom = row == 0, row == 15
    for p in range(-1, 9):
        V[p + 1] = (alpha - beta) * ws(p) + (beta * gs(p)) * row_sum(ws, p, first, last, top, bottom)
    vs = lambda p: V[p + 1]
    sums = []
    for x in range(2):
        total = None
        for p in range(4 * x, 4 * x + 4):
            s = jnp.where(g[p] > 0.0, row_sum(vs, p, first, last, top, bottom), 0.0) + part[p]
            total = s if total is None else total + s
        sums.append(total)
    thin = restricted(jnp.concatenate(sums, axis=0))
    thin = thin + pltpu.roll(thin, 31, 0)
    thin = thin + pltpu.roll(thin, 30, 0)
    two = jnp.zeros((2, 128), jnp.float32)
    for x in range(2):
        rows = [thin[k:k + 1] for k in range(16 * x, 16 * x + 16, 4)]
        r[x] = jnp.concatenate([two] + rows + [two], axis=0)
    for side, at, inner in ((0, 0, 1), (1, 15, 14)):
        base = 40 * side
        rim[base + 34:base + 40] = jnp.zeros((6, 512), jnp.float32)
        for p in range(8):
            rim[base + p:base + p + 1] = w[p, at:at + 1, :]
            rim[base + 8 + p:base + 9 + p] = g[p, inner:inner + 1, :]
            rim[base + 16 + p:base + 17 + p] = g[p, at:at + 1, :]
        for k, p in enumerate(range(-1, 9)):
            rim[base + 24 + k:base + 25 + k] = plane(own, sides, "g", p)(at, at + 1)


def k3(w, g, x1, x0, y0, y1, h, r0, rim, inverse, L, T, u, s1, D):
    even = lax.axis_index("core") == 0
    xlo, xhi = received(even, x0, x1)
    ylo, yhi = received(lax.rem(lax.axis_index("grp"), 2) == 0, y0, y1)
    first, last = edges((8, 512))
    sums = []
    for side, ref in ((0, ylo), (1, yhi)):
        base = 40 * side
        D[side, 0:10, :] = beta * rim[base + 24:base + 34] * ref[0:10]
        w1, w2, g1 = ref[1:9], ref[10:18], ref[18:26]
        near = w2 + rim[base:base + 8] + ref[0:8] + ref[2:10]
        near = near + jnp.where(first, 0.0, pltpu.roll(w1, 1, 1)) + jnp.where(last, 0.0, pltpu.roll(w1, 511, 1))
        d = D[side, 1:9, :]
        s = (alpha - beta) * w1 + (beta * g1) * near + D[side, 0:8, :] + D[side, 2:10, :]
        s = s + jnp.where(first, 0.0, pltpu.roll(d, 1, 1)) + jnp.where(last, 0.0, pltpu.roll(d, 511, 1))
        inner = jnp.where(rim[base + 8:base + 16] > 0.0, d, 0.0)
        sums.append(jnp.where(rim[base + 16:base + 24] > 0.0, s, 0.0) + inner)
    thin = restricted(jnp.concatenate(sums, axis=0))
    thin = thin + pltpu.roll(thin, 15, 0)
    thin = thin + pltpu.roll(thin, 14, 0)
    four = lax.broadcasted_iota(jnp.int32, (8, 128), 0)
    r = []
    for x in range(2):
        below = jnp.broadcast_to(thin[4 * x:4 * x + 1], (8, 128))
        above = jnp.broadcast_to(thin[8 + 4 * x:9 + 4 * x], (8, 128))
        r.append(r0[x] + jnp.where(four == 2, below, jnp.where(four == 5, above, 0.0)))
    first, last = edges((8, 128))
    lo, hi = xlo[48:56, 0:128], xhi[48:56, 0:128]
    hx = (lo + h[1], h[0] + hi)
    us, hs = [], []
    for x in range(2):
        us.append(r[x] * h[x])
        below = jnp.broadcast_to(ylo[29:30, 128 * x:128 * x + 128], (8, 128))
        above = jnp.broadcast_to(yhi[26:27, 128 * x:128 * x + 128], (8, 128))
        hs.append(jnp.where(four == 1, below, jnp.where(four == 6, above, h[x])))
        u[x] = us[x]
    q = jnp.zeros((8, 128), jnp.float32)
    flat = []
    for x in range(2):
        side = line_sides(us[x], first, last) + column_sides(us[x])
        q = q + (alpha - beta) * us[x] + beta * (hx[x] * us[x] + hs[x] * side)
        flat.append((alpha - beta) * us[x] + beta * hs[x] * (us[1 - x] + side))
    total = 2.0 * q + line_sides(q, first, last) + column_sides(q) + (1.0 - alpha) * (r[0] + r[1])
    total = total - jnp.where(jnp.broadcast_to(lo[2:3], (8, 128)) > 0.0, 0.0, flat[0])
    total = total - jnp.where(jnp.broadcast_to(hi[2:3], (8, 128)) > 0.0, 0.0, flat[1])
    for i in range(64):
        L[i] = total
    T[0:64, 256:768] = inverse[...]
    for half in range(2):
        rows, lanes = slice(32 * half, 32 * half + 32), slice(256 * half, 256 * half + 256)
        T[rows, 0:256] = ylo[32:64, lanes]
        T[rows, 768:1024] = yhi[32:64, lanes]
    post = Post(even, T.at[64:88], s1)
    post.put((slice(0, 16), slice(0, 512)), w[5], w[2])
    post.put((slice(0, 16), slice(512, 1024)), g[6], g[1])
    tiles = slice(16, 24)
    post.both((tiles, slice(0, 128)), us[0])
    post.both((tiles, slice(128, 256)), us[1])
    post.put((tiles, slice(256, 384)), h[1], h[0])
    post.both((tiles, slice(384, 1024)), jnp.zeros((8, 640), jnp.float32))


def k4(w, g, x1, x0, u, h, f1, mate, s0, s1):
    even = lax.axis_index("core") == 0
    lo, hi = received(even, x0, x1)
    flo, fhi = received(even, mate.at[64:88], f1)
    post = Post(lax.rem(lax.axis_index("grp"), 2) == 0, s0, s1)
    pack_rows(FAR, {"w": w, "g": g}, {"lo": (lo,), "hi": (hi,)}, post)
    post.both((slice(22, 24), slice(None)), jnp.zeros((2, 512), jnp.float32))
    tiles = [u[0], u[1], h[0], h[1]]
    for ref in (flo, fhi):
        tiles += [ref[16:24, 128 * k:128 * k + 128] for k in range(4)]
    for k, t in enumerate(tiles):
        row, lane = 24 + 8 * (k // 4), 128 * (k % 4)
        post.both((slice(row, row + 8), slice(lane, lane + 128)), t)


def k5(lines, own, mate, out):
    s = [lines[i] for i in range(8)]
    for i in range(8, 64):
        s[i % 8] = s[i % 8] + lines[i]
    while len(s) > 1:
        s = [a + b for a, b in zip(s[::2], s[1::2])]
    s = s[0]
    tables = []
    for ref in (own, mate):
        t = ref[0:64, 0:128] * s[0:1]
        for k in range(1, 8):
            t = t + ref[0:64, 128 * k:128 * k + 128] * s[k:k + 1]
        tables.append(t)
    even = lax.axis_index("core") == 0
    table = jnp.concatenate([jnp.where(even, *tables), jnp.where(even, *tables[::-1])], axis=0)
    y = jnp.broadcast_to(jnp.sum(table.T, axis=0, keepdims=True), (8, 128))
    for i in range(32):
        out[8 * i:8 * i + 8] = y


def spread(tiles):
    cell = lax.broadcasted_iota(jnp.int32, (128, 512), 1)
    agg = lax.broadcasted_iota(jnp.int32, (128, 512), 0)
    z = exact_dot(tiles, cell // 4 == agg)
    upper = lax.broadcasted_iota(jnp.int32, (8, 512), 0) < 4
    planes = []
    for k in range(0, tiles.shape[0], 8):
        parts = []
        for t in range(k + 1, k + 7, 2):
            a = jnp.broadcast_to(z[t:t + 1], (8, 512))
            b = jnp.broadcast_to(z[t + 1:t + 2], (8, 512))
            parts.append(jnp.where(upper, a, b))
        planes.append(jnp.concatenate(parts, axis=0))
    return planes


def k6(w, g, x0, x1, y0, y1, mate, f1, v0, v1, u, h, A, W, G):
    even, row_even = lax.axis_index("core") == 0, lax.rem(lax.axis_index("grp"), 2) == 0
    xlo, xhi = received(even, x0, x1)
    flo, fhi = received(even, mate.at[64:88], f1)
    ylo, yhi = received(row_even, y0, y1)
    vlo, vhi = received(row_even, v0, v1)
    own = {"w": w, "g": g}
    fill({"w": W, "g": G}, own, {"lo": (xlo, flo), "hi": (xhi, fhi)}, [(NEAR, ylo, yhi), (FAR, vlo, vhi)])
    four = lax.broadcasted_iota(jnp.int32, (8, 128), 0)
    first, last = edges((8, 128))

    def tile(mine, k):
        row, lane = 24 + 8 * (k // 4), 128 * (k % 4)
        below = pltpu.roll(vlo[row:row + 8, lane:lane + 128], 4, 0)
        above = pltpu.roll(vhi[row:row + 8, lane:lane + 128], 4, 0)
        return jnp.where(four < 2, below, jnp.where(four > 5, above, mine))

    far = [[ref[16:24, 128 * k:128 * k + 128] for k in range(3)] for ref in (flo, fhi)]
    us = [tile(far[0][0], 4), tile(far[0][1], 5), tile(u[0], 0), tile(u[1], 1), tile(far[1][0], 8), tile(far[1][1], 9)]
    hs = [tile(far[0][2], 6), tile(h[0], 2), tile(h[1], 3), tile(far[1][2], 10)]
    for x in range(4):
        c = us[x + 1]
        s = us[x] + us[x + 2] + line_sides(c, first, last) + column_sides(c)
        A[34, 0:8, 128 * x:128 * x + 128] = alpha * c + beta * hs[x] * s
    first, last = edges((TALL, 512))
    for i in range(1, 13):
        A[i + 21] = alpha * W[i] + (beta * G[i]) * fine_sum(W, i, first, last)
        A[i + 9] = G[i]
        if 2 <= i < 12:
            A[i - 2] = W[i]
    A[34, 8:TALL, :] = jnp.zeros((TALL - 8, 512), jnp.float32)


def k7(terms, A, rho, out, R, U0, U1, O, sems):
    fix = [jnp.zeros((1, 128), jnp.float32)]
    for j in range(-1, 5):
        k = jnp.clip(4 * lax.axis_index("grp") + j, 0, 31)
        fix.append(jnp.sum(terms[pl.ds(pl.multiple_of(8 * k, 8), 8), :], axis=0, keepdims=True))
    fix = jnp.concatenate(fix + [jnp.zeros((1, 128), jnp.float32)], axis=0)
    pro = spread(jnp.concatenate([A[34, 0:8, 128 * x:128 * x + 128] + fix for x in range(4)], axis=0))
    first, last = edges((TALL, 512))
    for p in range(8):
        R[p, 0:TOP, :] = jnp.zeros((TOP, 512), jnp.float32)
        R[p, TOP:TOP + 16, :] = rho[p]
        R[p, TOP + 16:TALL, :] = jnp.zeros((TOP, 512), jnp.float32)
    for i in range(1, 13):
        U0[i] = A[i + 21] + jnp.where(A[i + 9] > 0.0, pro[(i + 1) // 4], 0.0)
    for i in range(2, 12):
        U1[i] = (1.0 - c1) * U0[i] + c1 * (A[i - 2] + A[i + 9] * fine_sum(U0, i, first, last))
    copies = []
    for p in range(8):
        i = p + 3
        gp = A[i + 9]
        solid = ((1.0 - c1) * alpha + c1) * R[p] + (1.0 - c1) * pro[p // 4 + 1]
        mid = jnp.where(gp > 0.0, U1[i], solid)
        new = (1.0 - c2) * mid + c2 * (R[p] + gp * fine_sum(U1, i, first, last))
        O[p] = new[TOP:TOP + 16]
        copies.append(pltpu.make_async_copy(O.at[p], out.at[p], sems.at[p]))
        copies[-1].start()
    for c in copies:
        c.wait()


def swaps(s0, s1, axis, order):
    count, sent, got = lax.axis_size(axis), (s0, s1), [None, None]
    for parity in order:
        pairs = []
        for i in range(parity, count - 1, 2):
            pairs += [(i, i + 1), (i + 1, i)]
        got[parity] = lax.ppermute(sent[parity], axis, pairs)
    return got


def shards(rhs, shift, mask, cshift, inverse):
    field, coarse = shape(8, 16, 512), shape(2, 8, 128)
    wide = pltpu.VMEM((14, TALL, 512), jnp.float32)

    def kernel(name, body, outs, scratch, *args, flops=0, **extra):
        with jax.named_scope(name):
            return call(body, outs, scratch, flops=flops, **extra)(*args)

    inv = 1.0 / (6.0 + shift)
    fluid = mask.astype(jnp.float32)
    rho = rhs * inv
    g = fluid * inv
    w = fluid * rho
    part = (1.0 - alpha) * rhs
    h, s1, s0 = kernel("edges", k1, [coarse, shape(56, 512), shape(56, 512)], [], w, g, cshift)
    x0, x1 = swaps(s0, s1, AGG, (1, 0))
    s0, s1 = kernel("near_rows", k2, [shape(64, 512)] * 2, [], w, g, x1, x0, h, inverse)
    y0, y1 = swaps(s0, s1, "grp", (0, 1))
    r0, rim = kernel(
        "own_residual", k2b, [coarse, shape(80, 512)], [pltpu.VMEM((10, 16, 512), jnp.float32)],
        w, g, x1, x0, part, flops=3000000,
    )
    lines, table, u, s1 = kernel(
        "residual", k3, [shape(64, 8, 128), shape(88, 1024), coarse, shape(24, 1024)],
        [pltpu.VMEM((2, 16, 512), jnp.float32)], w, g, x1, x0, y0, y1, h, r0, rim, inverse,
    )
    lines = lax.all_to_all(lines, AGG, 0, 0)
    mate, f1 = swaps(table, s1, AGG, (1, 0))
    lines, mate, f1 = lax.optimization_barrier((lines, mate, f1))
    part = kernel("line_product", k5, shape(256, 128), [], lines, table, mate)
    terms = lax.all_to_all(part.reshape(256, 1, 128), ROW, 0, 0).reshape(256, 128)
    s0, s1 = kernel("far_rows", k4, [shape(48, 512)] * 2, [], w, g, x1, x0, u, h, f1, mate, flops=200000)
    v0, v1 = swaps(s0, s1, "grp", (0, 1))
    own = pltpu.VMEM((8, 16, 512), jnp.float32)
    known = kernel(
        "presmooth", k6, shape(35, TALL, 512), [wide, wide],
        w, g, x0, x1, y0, y1, mate, f1, v0, v1, u, h, flops=4000000,
    )
    return kernel(
        "postsmooth", k7, field,
        [pltpu.VMEM((8, TALL, 512), jnp.float32), wide, wide, own, pltpu.SemaphoreType.DMA((8,))],
        terms, known, rho, out_specs=pl.BlockSpec(memory_space=pl.ANY),
    )


def solution(mesh):
    finer = Mesh(mesh.devices.reshape(4, 2, 4, 2, 8), AGG + ("grp",))
    cells = P(AGG, "grp", None)
    return jax.shard_map(
        shards, mesh=finer, in_specs=(cells, cells, cells, cells, P(AGG, "grp")), out_specs=cells,
        check_vma=False,
    )
```

```python
import jax
import jax.numpy as jnp
from jax import lax
from jax.experimental import pallas as pl
from jax.experimental.pallas import tpu as pltpu
from jax.sharding import Mesh, PartitionSpec as P

c1 = 0.5735
c2 = 1.9751
alpha = c1 + c2 - c1 * c2
beta = c1 * c2
AGG = ("x", "zhi", "zlo", "core")
ROW = ("x", "zhi", "zlo", "grp")


NEAR = (
    [("w", 1, p) for p in range(-1, 9)]
    + [("w", 2, p) for p in range(0, 8)]
    + [("g", 1, p) for p in range(0, 8)]
)
FAR = (
    [("w", 1, p) for p in (-2, 9)]
    + [("w", 2, p) for p in (-1, 8)]
    + [("w", 3, p) for p in range(0, 8)]
    + [("g", 1, p) for p in (-1, 8)]
    + [("g", 2, p) for p in range(0, 8)]
)
PLANES = {
    ("w", -2): ("lo", 0, 0, 0), ("w", -1): ("lo", 0, 16, 0), ("g", -1): ("lo", 0, 32, 0),
    ("w", 8): ("hi", 0, 0, 0), ("w", 9): ("hi", 0, 16, 0), ("g", 8): ("hi", 0, 32, 0),
    ("w", -3): ("lo", 1, 0, 0), ("g", -2): ("lo", 1, 0, 512),
    ("w", 10): ("hi", 1, 0, 0), ("g", 9): ("hi", 1, 0, 512),
}
TALL = 24
TOP = 4


def shape(*dims):
    return jax.ShapeDtypeStruct(dims, jnp.float32)


def call(body, outs, scratch=(), mib=8, flops=0, **extra):
    return pl.pallas_call(
        body,
        out_shape=outs,
        scratch_shapes=list(scratch),
        compiler_params=pltpu.CompilerParams(vmem_limit_bytes=mib * 1024 * 1024),
        cost_estimate=pl.CostEstimate(flops=flops, bytes_accessed=flops // 2, transcendentals=0),
        **extra,
    )


class Pick:
    def __init__(self, flag, yes, no):
        self.flag, self.yes, self.no = flag, yes, no

    def __getitem__(self, at):
        return jnp.where(self.flag, self.yes[at], self.no[at])


class Post:
    def __init__(self, even, s0, s1):
        self.even, self.s0, self.s1 = even, s0, s1

    def put(self, at, up, down):
        self.s0[at] = jnp.where(self.even, up, down)
        self.s1[at] = jnp.where(self.even, down, up)

    def both(self, at, value):
        self.s0[at] = value
        self.s1[at] = value


def received(even, r0, r1):
    return Pick(even, r1, r0), Pick(even, r0, r1)


def k1(w, g, cshift, h, s1, s0):
    post = Post(lax.axis_index("core") == 0, s0, s1)
    h[...] = jnp.zeros((2, 8, 128), jnp.float32)
    for x in range(2):
        h[x, 2:6, :] = 1.0 / (6.0 + cshift[x])
    rows = lambda k: (slice(16 * k, 16 * k + 16), slice(None))
    post.put(rows(0), w[6], w[0])
    post.put(rows(1), w[7], w[1])
    post.put(rows(2), g[7], g[0])
    post.put((slice(48, 56), slice(0, 128)), h[1], h[0])
    post.both((slice(48, 56), slice(128, 512)), jnp.zeros((8, 384), jnp.float32))


def plane(own, sides, field, p):
    if 0 <= p < 8:
        return lambda a, b: own[field][p, a:b, :]
    side, which, base, lane = PLANES[field, p]
    ref = sides[side][which]
    return lambda a, b: ref[base + a:base + b, lane:lane + 512]


def pack_rows(rows, own, sides, post):
    for k, (field, d, p) in enumerate(rows):
        read = plane(own, sides, field, p)
        post.put((slice(k, k + 1), slice(None)), read(16 - d, 17 - d), read(d - 1, d))


def k2(w, g, x1, x0, h, inverse, s0, s1):
    lo, hi = received(lax.axis_index("core") == 0, x0, x1)
    post = Post(lax.rem(lax.axis_index("grp"), 2) == 0, s0, s1)
    pack_rows(NEAR, {"w": w, "g": g}, {"lo": (lo,), "hi": (hi,)}, post)
    post.both((slice(26, 32), slice(None)), jnp.zeros((6, 512), jnp.float32))
    for x in range(2):
        post.both((slice(26, 30), slice(128 * x, 128 * x + 128)), h[x, 2:6, :])
    for half in range(2):
        piece = inverse[32 * half:32 * half + 32, :]
        at = (slice(32, 64), slice(256 * half, 256 * half + 256))
        post.put(at, piece[:, 256:512], piece[:, 0:256])


def fine_sum(ref, p, first, last):
    c = ref[p]
    total = ref[p - 1] + ref[p + 1]
    total = total + pltpu.roll(c, 1, 0) + pltpu.roll(c, TALL - 1, 0)
    total = total + jnp.where(first, 0.0, pltpu.roll(c, 1, 1))
    return total + jnp.where(last, 0.0, pltpu.roll(c, 511, 1))


def edges(dims):
    lane = lax.broadcasted_iota(jnp.int32, dims, 1)
    return lane == 0, lane == dims[1] - 1


def line_sides(c, first, last):
    total = jnp.where(first, 0.0, pltpu.roll(c, 1, 1))
    return total + jnp.where(last, 0.0, pltpu.roll(c, 127, 1))


def column_sides(c):
    return pltpu.roll(c, 1, 0) + pltpu.roll(c, 7, 0)


def fill(wide, own, sides, messages):
    zero = jnp.zeros((TOP, 512), jnp.float32)
    for field in ("w", "g"):
        out = wide[field]
        for i in range(14):
            p = i - 3
            out[i, 0:TOP, :] = zero
            out[i, TOP + 16:TALL, :] = zero
            known = 0 <= p < 8 or ((field, p) in PLANES and PLANES[field, p][1] < len(sides["lo"]))
            out[i, TOP:TOP + 16, :] = plane(own, sides, field, p)(0, 16) if known else jnp.zeros((16, 512), jnp.float32)
    for rows, lo, hi in messages:
        for k, (field, d, p) in enumerate(rows):
            wide[field][p + 3, TOP - d:TOP + 1 - d, :] = lo[k:k + 1]
            wide[field][p + 3, TOP + 15 + d:TOP + 16 + d, :] = hi[k:k + 1]


def exact_dot(x, chosen):
    rest, parts = x, []
    for _ in range(3):
        part = rest.astype(jnp.bfloat16)
        parts.append(part)
        rest = rest - part.astype(jnp.float32)
    y = jnp.dot(
        jnp.concatenate(parts, axis=0), chosen.astype(jnp.float32).astype(jnp.bfloat16),
        preferred_element_type=jnp.float32,
    )
    n = x.shape[0]
    return y[0:n] + (y[n:2 * n] + y[2 * n:3 * n])


def restricted(sums):
    cell = lax.broadcasted_iota(jnp.int32, (512, 128), 0)
    agg = lax.broadcasted_iota(jnp.int32, (512, 128), 1)
    return exact_dot(sums, cell // 4 == agg)


def row_sum(planes, p, first, last, top, bottom):
    c = planes(p)
    total = planes(p - 1) + planes(p + 1)
    total = total + jnp.where(top, 0.0, pltpu.roll(c, 1, 0)) + jnp.where(bottom, 0.0, pltpu.roll(c, 15, 0))
    total = total + jnp.where(first, 0.0, pltpu.roll(c, 1, 1))
    return total + jnp.where(last, 0.0, pltpu.roll(c, 511, 1))


def k2b(w, g, x1, x0, part, r, rim, V):
    lo, hi = received(lax.axis_index("core") == 0, x0, x1)
    own, sides = {"w": w, "g": g}, {"lo": (lo,), "hi": (hi,)}
    ws = lambda p: plane(own, sides, "w", p)(0, 16)
    gs = lambda p: plane(own, sides, "g", p)(0, 16)
    first, last = edges((16, 512))
    row = lax.broadcasted_iota(jnp.int32, (16, 512), 0)
    top, bottom = row == 0, row == 15
    for p in range(-1, 9):
        V[p + 1] = (alpha - beta) * ws(p) + (beta * gs(p)) * row_sum(ws, p, first, last, top, bottom)
    vs = lambda p: V[p + 1]
    sums = []
    for x in range(2):
        total = None
        for p in range(4 * x, 4 * x + 4):
            s = jnp.where(g[p] > 0.0, row_sum(vs, p, first, last, top, bottom), 0.0) + part[p]
            total = s if total is None else total + s
        sums.append(total)
    thin = restricted(jnp.concatenate(sums, axis=0))
    thin = thin + pltpu.roll(thin, 31, 0)
    thin = thin + pltpu.roll(thin, 30, 0)
    two = jnp.zeros((2, 128), jnp.float32)
    for x in range(2):
        rows = [thin[k:k + 1] for k in range(16 * x, 16 * x + 16, 4)]
        r[x] = jnp.concatenate([two] + rows + [two], axis=0)
    for side, at, inner in ((0, 0, 1), (1, 15, 14)):
        base = 40 * side
        rim[base + 34:base + 40] = jnp.zeros((6, 512), jnp.float32)
        for p in range(8):
            rim[base + p:base + p + 1] = w[p, at:at + 1, :]
            rim[base + 8 + p:base + 9 + p] = g[p, inner:inner + 1, :]
            rim[base + 16 + p:base + 17 + p] = g[p, at:at + 1, :]
        for k, p in enumerate(range(-1, 9)):
            rim[base + 24 + k:base + 25 + k] = plane(own, sides, "g", p)(at, at + 1)


def k3(w, g, x1, x0, y0, y1, h, r0, rim, L, u, s1, D):
    even = lax.axis_index("core") == 0
    xlo, xhi = received(even, x0, x1)
    ylo, yhi = received(lax.rem(lax.axis_index("grp"), 2) == 0, y0, y1)
    first, last = edges((8, 512))
    sums = []
    for side, ref in ((0, ylo), (1, yhi)):
        base = 40 * side
        D[side, 0:10, :] = beta * rim[base + 24:base + 34] * ref[0:10]
        w1, w2, g1 = ref[1:9], ref[10:18], ref[18:26]
        near = w2 + rim[base:base + 8] + ref[0:8] + ref[2:10]
        near = near + jnp.where(first, 0.0, pltpu.roll(w1, 1, 1)) + jnp.where(last, 0.0, pltpu.roll(w1, 511, 1))
        d = D[side, 1:9, :]
        s = (alpha - beta) * w1 + (beta * g1) * near + D[side, 0:8, :] + D[side, 2:10, :]
        s = s + jnp.where(first, 0.0, pltpu.roll(d, 1, 1)) + jnp.where(last, 0.0, pltpu.roll(d, 511, 1))
        inner = jnp.where(rim[base + 8:base + 16] > 0.0, d, 0.0)
        sums.append(jnp.where(rim[base + 16:base + 24] > 0.0, s, 0.0) + inner)
    thin = restricted(jnp.concatenate(sums, axis=0))
    thin = thin + pltpu.roll(thin, 15, 0)
    thin = thin + pltpu.roll(thin, 14, 0)
    four = lax.broadcasted_iota(jnp.int32, (8, 128), 0)
    r = []
    for x in range(2):
        below = jnp.broadcast_to(thin[4 * x:4 * x + 1], (8, 128))
        above = jnp.broadcast_to(thin[8 + 4 * x:9 + 4 * x], (8, 128))
        r.append(r0[x] + jnp.where(four == 2, below, jnp.where(four == 5, above, 0.0)))
    first, last = edges((8, 128))
    lo, hi = xlo[48:56, 0:128], xhi[48:56, 0:128]
    hx = (lo + h[1], h[0] + hi)
    us, hs = [], []
    for x in range(2):
        us.append(r[x] * h[x])
        below = jnp.broadcast_to(ylo[29:30, 128 * x:128 * x + 128], (8, 128))
        above = jnp.broadcast_to(yhi[26:27, 128 * x:128 * x + 128], (8, 128))
        hs.append(jnp.where(four == 1, below, jnp.where(four == 6, above, h[x])))
        u[x] = us[x]
    q = jnp.zeros((8, 128), jnp.float32)
    flat = []
    for x in range(2):
        side = line_sides(us[x], first, last) + column_sides(us[x])
        q = q + (alpha - beta) * us[x] + beta * (hx[x] * us[x] + hs[x] * side)
        flat.append((alpha - beta) * us[x] + beta * hs[x] * (us[1 - x] + side))
    total = 2.0 * q + line_sides(q, first, last) + column_sides(q) + (1.0 - alpha) * (r[0] + r[1])
    total = total - jnp.where(jnp.broadcast_to(lo[2:3], (8, 128)) > 0.0, 0.0, flat[0])
    total = total - jnp.where(jnp.broadcast_to(hi[2:3], (8, 128)) > 0.0, 0.0, flat[1])
    for i in range(64):
        L[i] = total
    far_message(even, w, g, us, h, None, s1)


def far_message(even, w, g, us, h, s0, s1):
    up_first = even if s1 is None else jnp.logical_not(even)
    out = s0 if s1 is None else s1
    out[0:16, 0:512] = jnp.where(up_first, w[5], w[2])
    out[0:16, 512:1024] = jnp.where(up_first, g[6], g[1])
    out[16:24, 0:128] = us[0]
    out[16:24, 128:256] = us[1]
    out[16:24, 256:384] = jnp.where(up_first, h[1], h[0])
    out[16:24, 384:1024] = jnp.zeros((8, 640), jnp.float32)


def k3b(w, g, y0, y1, h, u, inverse, T):
    ylo, yhi = received(lax.rem(lax.axis_index("grp"), 2) == 0, y0, y1)
    T[0:64, 256:768] = inverse[...]
    for half in range(2):
        rows, lanes = slice(32 * half, 32 * half + 32), slice(256 * half, 256 * half + 256)
        T[rows, 0:256] = ylo[32:64, lanes]
        T[rows, 768:1024] = yhi[32:64, lanes]
    far_message(lax.axis_index("core") == 0, w, g, (u[0], u[1]), h, T.at[64:88], None)


def k4(w, g, x1, x0, u, h, f1, mate, s0, s1):
    even = lax.axis_index("core") == 0
    lo, hi = received(even, x0, x1)
    flo, fhi = received(even, mate.at[64:88], f1)
    post = Post(lax.rem(lax.axis_index("grp"), 2) == 0, s0, s1)
    pack_rows(FAR, {"w": w, "g": g}, {"lo": (lo,), "hi": (hi,)}, post)
    post.both((slice(22, 24), slice(None)), jnp.zeros((2, 512), jnp.float32))
    tiles = [u[0], u[1], h[0], h[1]]
    for ref in (flo, fhi):
        tiles += [ref[16:24, 128 * k:128 * k + 128] for k in range(4)]
    for k, t in enumerate(tiles):
        row, lane = 24 + 8 * (k // 4), 128 * (k % 4)
        post.both((slice(row, row + 8), slice(lane, lane + 128)), t)


def k5(lines, own, mate, out):
    s = [lines[i] for i in range(8)]
    for i in range(8, 64):
        s[i % 8] = s[i % 8] + lines[i]
    while len(s) > 1:
        s = [a + b for a, b in zip(s[::2], s[1::2])]
    s = s[0]
    tables = []
    for ref in (own, mate):
        t = ref[0:64, 0:128] * s[0:1]
        for k in range(1, 8):
            t = t + ref[0:64, 128 * k:128 * k + 128] * s[k:k + 1]
        tables.append(t)
    even = lax.axis_index("core") == 0
    table = jnp.concatenate([jnp.where(even, *tables), jnp.where(even, *tables[::-1])], axis=0)
    y = jnp.broadcast_to(jnp.sum(table.T, axis=0, keepdims=True), (8, 128))
    for i in range(32):
        out[8 * i:8 * i + 8] = y


def spread(tiles):
    cell = lax.broadcasted_iota(jnp.int32, (128, 512), 1)
    agg = lax.broadcasted_iota(jnp.int32, (128, 512), 0)
    z = exact_dot(tiles, cell // 4 == agg)
    upper = lax.broadcasted_iota(jnp.int32, (8, 512), 0) < 4
    planes = []
    for k in range(0, tiles.shape[0], 8):
        parts = []
        for t in range(k + 1, k + 7, 2):
            a = jnp.broadcast_to(z[t:t + 1], (8, 512))
            b = jnp.broadcast_to(z[t + 1:t + 2], (8, 512))
            parts.append(jnp.where(upper, a, b))
        planes.append(jnp.concatenate(parts, axis=0))
    return planes


def k6(w, g, x0, x1, y0, y1, mate, f1, v0, v1, u, h, A, W, G):
    even, row_even = lax.axis_index("core") == 0, lax.rem(lax.axis_index("grp"), 2) == 0
    xlo, xhi = received(even, x0, x1)
    flo, fhi = received(even, mate.at[64:88], f1)
    ylo, yhi = received(row_even, y0, y1)
    vlo, vhi = received(row_even, v0, v1)
    own = {"w": w, "g": g}
    fill({"w": W, "g": G}, own, {"lo": (xlo, flo), "hi": (xhi, fhi)}, [(NEAR, ylo, yhi), (FAR, vlo, vhi)])
    four = lax.broadcasted_iota(jnp.int32, (8, 128), 0)
    first, last = edges((8, 128))

    def tile(mine, k):
        row, lane = 24 + 8 * (k // 4), 128 * (k % 4)
        below = pltpu.roll(vlo[row:row + 8, lane:lane + 128], 4, 0)
        above = pltpu.roll(vhi[row:row + 8, lane:lane + 128], 4, 0)
        return jnp.where(four < 2, below, jnp.where(four > 5, above, mine))

    far = [[ref[16:24, 128 * k:128 * k + 128] for k in range(3)] for ref in (flo, fhi)]
    us = [tile(far[0][0], 4), tile(far[0][1], 5), tile(u[0], 0), tile(u[1], 1), tile(far[1][0], 8), tile(far[1][1], 9)]
    hs = [tile(far[0][2], 6), tile(h[0], 2), tile(h[1], 3), tile(far[1][2], 10)]
    for x in range(4):
        c = us[x + 1]
        s = us[x] + us[x + 2] + line_sides(c, first, last) + column_sides(c)
        A[34, 0:8, 128 * x:128 * x + 128] = alpha * c + beta * hs[x] * s
    first, last = edges((TALL, 512))
    for i in range(1, 13):
        A[i + 21] = alpha * W[i] + (beta * G[i]) * fine_sum(W, i, first, last)
        A[i + 9] = G[i]
        if 2 <= i < 12:
            A[i - 2] = W[i]
    A[34, 8:TALL, :] = jnp.zeros((TALL - 8, 512), jnp.float32)


def k7(terms, A, rho, out, R, U0, U1, O, sems):
    fix = [jnp.zeros((1, 128), jnp.float32)]
    for j in range(-1, 5):
        k = jnp.clip(4 * lax.axis_index("grp") + j, 0, 31)
        fix.append(jnp.sum(terms[pl.ds(pl.multiple_of(8 * k, 8), 8), :], axis=0, keepdims=True))
    fix = jnp.concatenate(fix + [jnp.zeros((1, 128), jnp.float32)], axis=0)
    pro = spread(jnp.concatenate([A[34, 0:8, 128 * x:128 * x + 128] + fix for x in range(4)], axis=0))
    first, last = edges((TALL, 512))
    for p in range(8):
        R[p, 0:TOP, :] = jnp.zeros((TOP, 512), jnp.float32)
        R[p, TOP:TOP + 16, :] = rho[p]
        R[p, TOP + 16:TALL, :] = jnp.zeros((TOP, 512), jnp.float32)
    for i in range(1, 13):
        U0[i] = A[i + 21] + jnp.where(A[i + 9] > 0.0, pro[(i + 1) // 4], 0.0)
    for i in range(2, 12):
        U1[i] = (1.0 - c1) * U0[i] + c1 * (A[i - 2] + A[i + 9] * fine_sum(U0, i, first, last))
    copies = []
    for p in range(8):
        i = p + 3
        gp = A[i + 9]
        solid = ((1.0 - c1) * alpha + c1) * R[p] + (1.0 - c1) * pro[p // 4 + 1]
        mid = jnp.where(gp > 0.0, U1[i], solid)
        new = (1.0 - c2) * mid + c2 * (R[p] + gp * fine_sum(U1, i, first, last))
        O[p] = new[TOP:TOP + 16]
        copies.append(pltpu.make_async_copy(O.at[p], out.at[p], sems.at[p]))
        copies[-1].start()
    for c in copies:
        c.wait()


def swaps(s0, s1, axis, order):
    count, sent, got = lax.axis_size(axis), (s0, s1), [None, None]
    for parity in order:
        pairs = []
        for i in range(parity, count - 1, 2):
            pairs += [(i, i + 1), (i + 1, i)]
        got[parity] = lax.ppermute(sent[parity], axis, pairs)
    return got


def shards(rhs, shift, mask, cshift, inverse):
    field, coarse = shape(8, 16, 512), shape(2, 8, 128)
    wide = pltpu.VMEM((14, TALL, 512), jnp.float32)

    def kernel(name, body, outs, scratch, *args, flops=0, **extra):
        with jax.named_scope(name):
            return call(body, outs, scratch, flops=flops, **extra)(*args)

    inv = 1.0 / (6.0 + shift)
    fluid = mask.astype(jnp.float32)
    rho = rhs * inv
    g = fluid * inv
    w = fluid * rho
    part = (1.0 - alpha) * rhs
    h, s1, s0 = kernel("edges", k1, [coarse, shape(56, 512), shape(56, 512)], [], w, g, cshift)
    x0, x1 = swaps(s0, s1, AGG, (1, 0))
    s0, s1 = kernel("near_rows", k2, [shape(64, 512)] * 2, [], w, g, x1, x0, h, inverse)
    y0, y1 = swaps(s0, s1, "grp", (0, 1))
    r0, rim = kernel(
        "own_residual", k2b, [coarse, shape(80, 512)], [pltpu.VMEM((10, 16, 512), jnp.float32)],
        w, g, x1, x0, part, flops=3000000,
    )
    lines, u, s1 = kernel(
        "residual", k3, [shape(64, 8, 128), coarse, shape(24, 1024)],
        [pltpu.VMEM((2, 16, 512), jnp.float32)], w, g, x1, x0, y0, y1, h, r0, rim,
    )
    table = kernel("line_table", k3b, shape(88, 1024), [], w, g, y0, y1, h, u, inverse, flops=400000)
    lines = lax.all_to_all(lines, AGG, 0, 0)
    mate, f1 = swaps(table, s1, AGG, (1, 0))
    lines, mate, f1 = lax.optimization_barrier((lines, mate, f1))
    part = kernel("line_product", k5, shape(256, 128), [], lines, table, mate)
    terms = lax.all_to_all(part.reshape(256, 1, 128), ROW, 0, 0).reshape(256, 128)
    s0, s1 = kernel("far_rows", k4, [shape(48, 512)] * 2, [], w, g, x1, x0, u, h, f1, mate, flops=200000)
    v0, v1 = swaps(s0, s1, "grp", (0, 1))
    own = pltpu.VMEM((8, 16, 512), jnp.float32)
    known = kernel(
        "presmooth", k6, shape(35, TALL, 512), [wide, wide],
        w, g, x0, x1, y0, y1, mate, f1, v0, v1, u, h, flops=4000000,
    )
    return kernel(
        "postsmooth", k7, field,
        [pltpu.VMEM((8, TALL, 512), jnp.float32), wide, wide, own, pltpu.SemaphoreType.DMA((8,))],
        terms, known, rho, out_specs=pl.BlockSpec(memory_space=pl.ANY),
    )


def solution(mesh):
    finer = Mesh(mesh.devices.reshape(4, 2, 4, 2, 8), AGG + ("grp",))
    cells = P(AGG, "grp", None)
    return jax.shard_map(
        shards, mesh=finer, in_specs=(cells, cells, cells, cells, P(AGG, "grp")), out_specs=cells,
        check_vma=False,
    )
```

```python
import jax
import jax.numpy as jnp
from jax import lax
from jax.experimental import pallas as pl
from jax.experimental.pallas import tpu as pltpu
from jax.sharding import Mesh, PartitionSpec as P

c1 = 0.5735
c2 = 1.9751
alpha = c1 + c2 - c1 * c2
beta = c1 * c2
AGG = ("x", "zhi", "zlo", "core")
ROW = ("x", "zhi", "zlo", "grp")


NEAR = (
    [("w", 1, p) for p in range(-1, 9)]
    + [("w", 2, p) for p in range(0, 8)]
    + [("g", 1, p) for p in range(0, 8)]
)
FAR = (
    [("w", 1, p) for p in (-2, 9)]
    + [("w", 2, p) for p in (-1, 8)]
    + [("w", 3, p) for p in range(0, 8)]
    + [("g", 1, p) for p in (-1, 8)]
    + [("g", 2, p) for p in range(0, 8)]
)
PLANES = {
    ("w", -2): ("lo", 0, 0, 0), ("w", -1): ("lo", 0, 16, 0), ("g", -1): ("lo", 0, 32, 0),
    ("w", 8): ("hi", 0, 0, 0), ("w", 9): ("hi", 0, 16, 0), ("g", 8): ("hi", 0, 32, 0),
    ("w", -3): ("lo", 1, 0, 0), ("g", -2): ("lo", 1, 0, 512),
    ("w", 10): ("hi", 1, 0, 0), ("g", 9): ("hi", 1, 0, 512),
}
TALL = 24
TOP = 4


def shape(*dims):
    return jax.ShapeDtypeStruct(dims, jnp.float32)


def call(body, outs, scratch=(), mib=8, flops=0, **extra):
    return pl.pallas_call(
        body,
        out_shape=outs,
        scratch_shapes=list(scratch),
        compiler_params=pltpu.CompilerParams(vmem_limit_bytes=mib * 1024 * 1024),
        cost_estimate=pl.CostEstimate(flops=flops, bytes_accessed=flops // 2, transcendentals=0),
        **extra,
    )


class Pick:
    def __init__(self, flag, yes, no):
        self.flag, self.yes, self.no = flag, yes, no

    def __getitem__(self, at):
        return jnp.where(self.flag, self.yes[at], self.no[at])


class Post:
    def __init__(self, even, s0, s1):
        self.even, self.s0, self.s1 = even, s0, s1

    def put(self, at, up, down):
        self.s0[at] = jnp.where(self.even, up, down)
        self.s1[at] = jnp.where(self.even, down, up)

    def both(self, at, value):
        self.s0[at] = value
        self.s1[at] = value


def received(even, r0, r1):
    return Pick(even, r1, r0), Pick(even, r0, r1)


def k1(w, g, cshift, h, s1, s0):
    post = Post(lax.axis_index("core") == 0, s0, s1)
    h[...] = jnp.zeros((2, 8, 128), jnp.float32)
    for x in range(2):
        h[x, 2:6, :] = 1.0 / (6.0 + cshift[x])
    rows = lambda k: (slice(16 * k, 16 * k + 16), slice(None))
    post.put(rows(0), w[6], w[0])
    post.put(rows(1), w[7], w[1])
    post.put(rows(2), g[7], g[0])
    post.put((slice(48, 56), slice(0, 128)), h[1], h[0])
    post.both((slice(48, 56), slice(128, 512)), jnp.zeros((8, 384), jnp.float32))


def plane(own, sides, field, p):
    if 0 <= p < 8:
        return lambda a, b: own[field][p, a:b, :]
    side, which, base, lane = PLANES[field, p]
    ref = sides[side][which]
    return lambda a, b: ref[base + a:base + b, lane:lane + 512]


def pack_rows(rows, own, sides, post):
    for k, (field, d, p) in enumerate(rows):
        read = plane(own, sides, field, p)
        post.put((slice(k, k + 1), slice(None)), read(16 - d, 17 - d), read(d - 1, d))


def k2(w, g, x1, x0, h, inverse, s0, s1):
    lo, hi = received(lax.axis_index("core") == 0, x0, x1)
    post = Post(lax.rem(lax.axis_index("grp"), 2) == 0, s0, s1)
    pack_rows(NEAR, {"w": w, "g": g}, {"lo": (lo,), "hi": (hi,)}, post)
    post.both((slice(26, 32), slice(None)), jnp.zeros((6, 512), jnp.float32))
    for x in range(2):
        post.both((slice(26, 30), slice(128 * x, 128 * x + 128)), h[x, 2:6, :])
    for half in range(2):
        piece = inverse[32 * half:32 * half + 32, :]
        at = (slice(32, 64), slice(256 * half, 256 * half + 256))
        post.put(at, piece[:, 256:512], piece[:, 0:256])


def fine_sum(ref, p, first, last):
    c = ref[p]
    total = ref[p - 1] + ref[p + 1]
    total = total + pltpu.roll(c, 1, 0) + pltpu.roll(c, TALL - 1, 0)
    total = total + jnp.where(first, 0.0, pltpu.roll(c, 1, 1))
    return total + jnp.where(last, 0.0, pltpu.roll(c, 511, 1))


def edges(dims):
    lane = lax.broadcasted_iota(jnp.int32, dims, 1)
    return lane == 0, lane == dims[1] - 1


def line_sides(c, first, last):
    total = jnp.where(first, 0.0, pltpu.roll(c, 1, 1))
    return total + jnp.where(last, 0.0, pltpu.roll(c, 127, 1))


def column_sides(c):
    return pltpu.roll(c, 1, 0) + pltpu.roll(c, 7, 0)


def fill(wide, own, sides, messages):
    zero = jnp.zeros((TOP, 512), jnp.float32)
    for field in ("w", "g"):
        out = wide[field]
        for i in range(14):
            p = i - 3
            out[i, 0:TOP, :] = zero
            out[i, TOP + 16:TALL, :] = zero
            known = 0 <= p < 8 or ((field, p) in PLANES and PLANES[field, p][1] < len(sides["lo"]))
            out[i, TOP:TOP + 16, :] = plane(own, sides, field, p)(0, 16) if known else jnp.zeros((16, 512), jnp.float32)
    for rows, lo, hi in messages:
        for k, (field, d, p) in enumerate(rows):
            wide[field][p + 3, TOP - d:TOP + 1 - d, :] = lo[k:k + 1]
            wide[field][p + 3, TOP + 15 + d:TOP + 16 + d, :] = hi[k:k + 1]


def exact_dot(x, chosen):
    rest, parts = x, []
    for _ in range(3):
        part = rest.astype(jnp.bfloat16)
        parts.append(part)
        rest = rest - part.astype(jnp.float32)
    y = jnp.dot(
        jnp.concatenate(parts, axis=0), chosen.astype(jnp.float32).astype(jnp.bfloat16),
        preferred_element_type=jnp.float32,
    )
    n = x.shape[0]
    return y[0:n] + (y[n:2 * n] + y[2 * n:3 * n])


def restricted(sums):
    cell = lax.broadcasted_iota(jnp.int32, (512, 128), 0)
    agg = lax.broadcasted_iota(jnp.int32, (512, 128), 1)
    return exact_dot(sums, cell // 4 == agg)


def row_sum(planes, p, first, last, top, bottom):
    c = planes(p)
    total = planes(p - 1) + planes(p + 1)
    total = total + jnp.where(top, 0.0, pltpu.roll(c, 1, 0)) + jnp.where(bottom, 0.0, pltpu.roll(c, 15, 0))
    total = total + jnp.where(first, 0.0, pltpu.roll(c, 1, 1))
    return total + jnp.where(last, 0.0, pltpu.roll(c, 511, 1))


def k2b(w, g, x1, x0, part, r, rim, V):
    lo, hi = received(lax.axis_index("core") == 0, x0, x1)
    own, sides = {"w": w, "g": g}, {"lo": (lo,), "hi": (hi,)}
    ws = lambda p: plane(own, sides, "w", p)(0, 16)
    gs = lambda p: plane(own, sides, "g", p)(0, 16)
    first, last = edges((16, 512))
    row = lax.broadcasted_iota(jnp.int32, (16, 512), 0)
    top, bottom = row == 0, row == 15
    for p in range(-1, 9):
        V[p + 1] = (alpha - beta) * ws(p) + (beta * gs(p)) * row_sum(ws, p, first, last, top, bottom)
    vs = lambda p: V[p + 1]
    sums = []
    for x in range(2):
        total = None
        for p in range(4 * x, 4 * x + 4):
            s = jnp.where(g[p] > 0.0, row_sum(vs, p, first, last, top, bottom), 0.0) + part[p]
            total = s if total is None else total + s
        sums.append(total)
    thin = restricted(jnp.concatenate(sums, axis=0))
    thin = thin + pltpu.roll(thin, 31, 0)
    thin = thin + pltpu.roll(thin, 30, 0)
    two = jnp.zeros((2, 128), jnp.float32)
    for x in range(2):
        rows = [thin[k:k + 1] for k in range(16 * x, 16 * x + 16, 4)]
        r[x] = jnp.concatenate([two] + rows + [two], axis=0)
    for side, at, inner in ((0, 0, 1), (1, 15, 14)):
        base = 40 * side
        rim[base + 34:base + 40] = jnp.zeros((6, 512), jnp.float32)
        for p in range(8):
            rim[base + p:base + p + 1] = w[p, at:at + 1, :]
            rim[base + 8 + p:base + 9 + p] = g[p, inner:inner + 1, :]
            rim[base + 16 + p:base + 17 + p] = g[p, at:at + 1, :]
        for k, p in enumerate(range(-1, 9)):
            rim[base + 24 + k:base + 25 + k] = plane(own, sides, "g", p)(at, at + 1)


def k3(w, g, x1, x0, y1, y0, h, r0, rim, inverse, L, T, u, s1, D):
    even = lax.axis_index("core") == 0
    xlo, xhi = received(even, x0, x1)
    ylo, yhi = received(lax.rem(lax.axis_index("grp"), 2) == 0, y0, y1)
    first, last = edges((8, 512))
    sums = []
    for side, ref in ((0, ylo), (1, yhi)):
        base = 40 * side
        D[side, 0:10, :] = beta * rim[base + 24:base + 34] * ref[0:10]
        w1, w2, g1 = ref[1:9], ref[10:18], ref[18:26]
        near = w2 + rim[base:base + 8] + ref[0:8] + ref[2:10]
        near = near + jnp.where(first, 0.0, pltpu.roll(w1, 1, 1)) + jnp.where(last, 0.0, pltpu.roll(w1, 511, 1))
        d = D[side, 1:9, :]
        s = (alpha - beta) * w1 + (beta * g1) * near + D[side, 0:8, :] + D[side, 2:10, :]
        s = s + jnp.where(first, 0.0, pltpu.roll(d, 1, 1)) + jnp.where(last, 0.0, pltpu.roll(d, 511, 1))
        inner = jnp.where(rim[base + 8:base + 16] > 0.0, d, 0.0)
        sums.append(jnp.where(rim[base + 16:base + 24] > 0.0, s, 0.0) + inner)
    thin = restricted(jnp.concatenate(sums, axis=0))
    thin = thin + pltpu.roll(thin, 15, 0)
    thin = thin + pltpu.roll(thin, 14, 0)
    four = lax.broadcasted_iota(jnp.int32, (8, 128), 0)
    r = []
    for x in range(2):
        below = jnp.broadcast_to(thin[4 * x:4 * x + 1], (8, 128))
        above = jnp.broadcast_to(thin[8 + 4 * x:9 + 4 * x], (8, 128))
        r.append(r0[x] + jnp.where(four == 2, below, jnp.where(four == 5, above, 0.0)))
    first, last = edges((8, 128))
    lo, hi = xlo[48:56, 0:128], xhi[48:56, 0:128]
    hx = (lo + h[1], h[0] + hi)
    us, hs = [], []
    for x in range(2):
        us.append(r[x] * h[x])
        below = jnp.broadcast_to(ylo[29:30, 128 * x:128 * x + 128], (8, 128))
        above = jnp.broadcast_to(yhi[26:27, 128 * x:128 * x + 128], (8, 128))
        hs.append(jnp.where(four == 1, below, jnp.where(four == 6, above, h[x])))
        u[x] = us[x]
    q = jnp.zeros((8, 128), jnp.float32)
    flat = []
    for x in range(2):
        side = line_sides(us[x], first, last) + column_sides(us[x])
        q = q + (alpha - beta) * us[x] + beta * (hx[x] * us[x] + hs[x] * side)
        flat.append((alpha - beta) * us[x] + beta * hs[x] * (us[1 - x] + side))
    total = 2.0 * q + line_sides(q, first, last) + column_sides(q) + (1.0 - alpha) * (r[0] + r[1])
    total = total - jnp.where(jnp.broadcast_to(lo[2:3], (8, 128)) > 0.0, 0.0, flat[0])
    total = total - jnp.where(jnp.broadcast_to(hi[2:3], (8, 128)) > 0.0, 0.0, flat[1])
    for i in range(64):
        L[i] = total
    T[0:64, 256:768] = inverse[...]
    for half in range(2):
        rows, lanes = slice(32 * half, 32 * half + 32), slice(256 * half, 256 * half + 256)
        T[rows, 0:256] = ylo[32:64, lanes]
        T[rows, 768:1024] = yhi[32:64, lanes]
    post = Post(even, T.at[64:88], s1)
    post.put((slice(0, 16), slice(0, 512)), w[5], w[2])
    post.put((slice(0, 16), slice(512, 1024)), g[6], g[1])
    tiles = slice(16, 24)
    post.both((tiles, slice(0, 128)), us[0])
    post.both((tiles, slice(128, 256)), us[1])
    post.put((tiles, slice(256, 384)), h[1], h[0])
    post.both((tiles, slice(384, 1024)), jnp.zeros((8, 640), jnp.float32))


def k4(w, g, x1, x0, u, h, f1, mate, s0, s1):
    even = lax.axis_index("core") == 0
    lo, hi = received(even, x0, x1)
    flo, fhi = received(even, mate.at[64:88], f1)
    post = Post(lax.rem(lax.axis_index("grp"), 2) == 0, s0, s1)
    pack_rows(FAR, {"w": w, "g": g}, {"lo": (lo,), "hi": (hi,)}, post)
    post.both((slice(22, 24), slice(None)), jnp.zeros((2, 512), jnp.float32))
    tiles = [u[0], u[1], h[0], h[1]]
    for ref in (flo, fhi):
        tiles += [ref[16:24, 128 * k:128 * k + 128] for k in range(4)]
    for k, t in enumerate(tiles):
        row, lane = 24 + 8 * (k // 4), 128 * (k % 4)
        post.both((slice(row, row + 8), slice(lane, lane + 128)), t)


def k5(lines, own, mate, out):
    s = [lines[i] for i in range(8)]
    for i in range(8, 64):
        s[i % 8] = s[i % 8] + lines[i]
    while len(s) > 1:
        s = [a + b for a, b in zip(s[::2], s[1::2])]
    s = s[0]
    tables = []
    for ref in (own, mate):
        t = ref[0:64, 0:128] * s[0:1]
        for k in range(1, 8):
            t = t + ref[0:64, 128 * k:128 * k + 128] * s[k:k + 1]
        tables.append(t)
    even = lax.axis_index("core") == 0
    table = jnp.concatenate([jnp.where(even, *tables), jnp.where(even, *tables[::-1])], axis=0)
    y = jnp.broadcast_to(jnp.sum(table.T, axis=0, keepdims=True), (8, 128))
    for i in range(32):
        out[8 * i:8 * i + 8] = y


def spread(tiles):
    cell = lax.broadcasted_iota(jnp.int32, (128, 512), 1)
    agg = lax.broadcasted_iota(jnp.int32, (128, 512), 0)
    z = exact_dot(tiles, cell // 4 == agg)
    upper = lax.broadcasted_iota(jnp.int32, (8, 512), 0) < 4
    planes = []
    for k in range(0, tiles.shape[0], 8):
        parts = []
        for t in range(k + 1, k + 7, 2):
            a = jnp.broadcast_to(z[t:t + 1], (8, 512))
            b = jnp.broadcast_to(z[t + 1:t + 2], (8, 512))
            parts.append(jnp.where(upper, a, b))
        planes.append(jnp.concatenate(parts, axis=0))
    return planes


def k6(w, g, x0, x1, y0, y1, mate, f1, v0, v1, u, h, A, W, G):
    even, row_even = lax.axis_index("core") == 0, lax.rem(lax.axis_index("grp"), 2) == 0
    xlo, xhi = received(even, x0, x1)
    flo, fhi = received(even, mate.at[64:88], f1)
    ylo, yhi = received(row_even, y0, y1)
    vlo, vhi = received(row_even, v0, v1)
    own = {"w": w, "g": g}
    fill({"w": W, "g": G}, own, {"lo": (xlo, flo), "hi": (xhi, fhi)}, [(NEAR, ylo, yhi), (FAR, vlo, vhi)])
    four = lax.broadcasted_iota(jnp.int32, (8, 128), 0)
    first, last = edges((8, 128))

    def tile(mine, k):
        row, lane = 24 + 8 * (k // 4), 128 * (k % 4)
        below = pltpu.roll(vlo[row:row + 8, lane:lane + 128], 4, 0)
        above = pltpu.roll(vhi[row:row + 8, lane:lane + 128], 4, 0)
        return jnp.where(four < 2, below, jnp.where(four > 5, above, mine))

    far = [[ref[16:24, 128 * k:128 * k + 128] for k in range(3)] for ref in (flo, fhi)]
    us = [tile(far[0][0], 4), tile(far[0][1], 5), tile(u[0], 0), tile(u[1], 1), tile(far[1][0], 8), tile(far[1][1], 9)]
    hs = [tile(far[0][2], 6), tile(h[0], 2), tile(h[1], 3), tile(far[1][2], 10)]
    for x in range(4):
        c = us[x + 1]
        s = us[x] + us[x + 2] + line_sides(c, first, last) + column_sides(c)
        A[34, 0:8, 128 * x:128 * x + 128] = alpha * c + beta * hs[x] * s
    first, last = edges((TALL, 512))
    for i in range(1, 13):
        A[i + 21] = alpha * W[i] + (beta * G[i]) * fine_sum(W, i, first, last)
        A[i + 9] = G[i]
        if 2 <= i < 12:
            A[i - 2] = W[i]
    A[34, 8:TALL, :] = jnp.zeros((TALL - 8, 512), jnp.float32)


def k7(terms, A, rho, out, R, U0, U1, O, sems):
    fix = [jnp.zeros((1, 128), jnp.float32)]
    for j in range(-1, 5):
        k = jnp.clip(4 * lax.axis_index("grp") + j, 0, 31)
        fix.append(jnp.sum(terms[pl.ds(pl.multiple_of(8 * k, 8), 8), :], axis=0, keepdims=True))
    fix = jnp.concatenate(fix + [jnp.zeros((1, 128), jnp.float32)], axis=0)
    pro = spread(jnp.concatenate([A[34, 0:8, 128 * x:128 * x + 128] + fix for x in range(4)], axis=0))
    first, last = edges((TALL, 512))
    for p in range(8):
        R[p, 0:TOP, :] = jnp.zeros((TOP, 512), jnp.float32)
        R[p, TOP:TOP + 16, :] = rho[p]
        R[p, TOP + 16:TALL, :] = jnp.zeros((TOP, 512), jnp.float32)
    for i in range(1, 13):
        U0[i] = A[i + 21] + jnp.where(A[i + 9] > 0.0, pro[(i + 1) // 4], 0.0)
    for i in range(2, 12):
        U1[i] = (1.0 - c1) * U0[i] + c1 * (A[i - 2] + A[i + 9] * fine_sum(U0, i, first, last))
    copies = []
    for p in range(8):
        i = p + 3
        gp = A[i + 9]
        solid = ((1.0 - c1) * alpha + c1) * R[p] + (1.0 - c1) * pro[p // 4 + 1]
        mid = jnp.where(gp > 0.0, U1[i], solid)
        new = (1.0 - c2) * mid + c2 * (R[p] + gp * fine_sum(U1, i, first, last))
        O[p] = new[TOP:TOP + 16]
        copies.append(pltpu.make_async_copy(O.at[p], out.at[p], sems.at[p]))
        copies[-1].start()
    for c in copies:
        c.wait()


def swaps(s0, s1, axis, order):
    count, sent, got = lax.axis_size(axis), (s0, s1), [None, None]
    for parity in order:
        pairs = []
        for i in range(parity, count - 1, 2):
            pairs += [(i, i + 1), (i + 1, i)]
        got[parity] = lax.ppermute(sent[parity], axis, pairs)
    return got


def shards(rhs, shift, mask, cshift, inverse):
    field, coarse = shape(8, 16, 512), shape(2, 8, 128)
    wide = pltpu.VMEM((14, TALL, 512), jnp.float32)

    def kernel(name, body, outs, scratch, *args, flops=0, **extra):
        with jax.named_scope(name):
            return call(body, outs, scratch, flops=flops, **extra)(*args)

    inv = 1.0 / (6.0 + shift)
    fluid = mask.astype(jnp.float32)
    rho = rhs * inv
    g = fluid * inv
    w = fluid * rho
    part = (1.0 - alpha) * rhs
    h, s1, s0 = kernel("edges", k1, [coarse, shape(56, 512), shape(56, 512)], [], w, g, cshift)
    x0, x1 = swaps(s0, s1, AGG, (1, 0))
    s0, s1 = kernel("near_rows", k2, [shape(64, 512)] * 2, [], w, g, x1, x0, h, inverse)
    y0, y1 = swaps(s0, s1, "grp", (1, 0))
    r0, rim = kernel(
        "own_residual", k2b, [coarse, shape(80, 512)], [pltpu.VMEM((10, 16, 512), jnp.float32)],
        w, g, x1, x0, part, flops=3000000,
    )
    lines, table, u, s1 = kernel(
        "residual", k3, [shape(64, 8, 128), shape(88, 1024), coarse, shape(24, 1024)],
        [pltpu.VMEM((2, 16, 512), jnp.float32)], w, g, x1, x0, y1, y0, h, r0, rim, inverse,
    )
    lines = lax.all_to_all(lines, AGG, 0, 0)
    mate, f1 = swaps(table, s1, AGG, (1, 0))
    lines, mate, f1 = lax.optimization_barrier((lines, mate, f1))
    part = kernel("line_product", k5, shape(256, 128), [], lines, table, mate)
    terms = lax.all_to_all(part.reshape(256, 1, 128), ROW, 0, 0).reshape(256, 128)
    s0, s1 = kernel("far_rows", k4, [shape(48, 512)] * 2, [], w, g, x1, x0, u, h, f1, mate, flops=200000)
    v0, v1 = swaps(s0, s1, "grp", (0, 1))
    own = pltpu.VMEM((8, 16, 512), jnp.float32)
    known = kernel(
        "presmooth", k6, shape(35, TALL, 512), [wide, wide],
        w, g, x0, x1, y0, y1, mate, f1, v0, v1, u, h, flops=4000000,
    )
    return kernel(
        "postsmooth", k7, field,
        [pltpu.VMEM((8, TALL, 512), jnp.float32), wide, wide, own, pltpu.SemaphoreType.DMA((8,))],
        terms, known, rho, out_specs=pl.BlockSpec(memory_space=pl.ANY),
    )


def solution(mesh):
    finer = Mesh(mesh.devices.reshape(4, 2, 4, 2, 8), AGG + ("grp",))
    cells = P(AGG, "grp", None)
    return jax.shard_map(
        shards, mesh=finer, in_specs=(cells, cells, cells, cells, P(AGG, "grp")), out_specs=cells,
        check_vma=False,
    )
```

```python
import jax
import jax.numpy as jnp
from jax import lax
from jax.experimental import pallas as pl
from jax.experimental.pallas import tpu as pltpu
from jax.sharding import Mesh, PartitionSpec as P

c1 = 0.5735
c2 = 1.9751
alpha = c1 + c2 - c1 * c2
beta = c1 * c2
AGG = ("x", "zhi", "zlo", "core")
ROW = ("x", "zhi", "zlo", "grp")


NEAR = (
    [("w", 1, p) for p in range(-1, 9)]
    + [("w", 2, p) for p in range(0, 8)]
    + [("g", 1, p) for p in range(0, 8)]
)
FAR = (
    [("w", 1, p) for p in (-2, 9)]
    + [("w", 2, p) for p in (-1, 8)]
    + [("w", 3, p) for p in range(0, 8)]
    + [("g", 1, p) for p in (-1, 8)]
    + [("g", 2, p) for p in range(0, 8)]
)
PLANES = {
    ("w", -2): ("lo", 0, 0, 0), ("w", -1): ("lo", 0, 16, 0), ("g", -1): ("lo", 0, 32, 0),
    ("w", 8): ("hi", 0, 0, 0), ("w", 9): ("hi", 0, 16, 0), ("g", 8): ("hi", 0, 32, 0),
    ("w", -3): ("lo", 1, 0, 0), ("g", -2): ("lo", 1, 0, 512),
    ("w", 10): ("hi", 1, 0, 0), ("g", 9): ("hi", 1, 0, 512),
}
TALL = 24
TOP = 4


def shape(*dims):
    return jax.ShapeDtypeStruct(dims, jnp.float32)


def call(body, outs, scratch=(), mib=8, flops=0, **extra):
    return pl.pallas_call(
        body,
        out_shape=outs,
        scratch_shapes=list(scratch),
        compiler_params=pltpu.CompilerParams(vmem_limit_bytes=mib * 1024 * 1024),
        cost_estimate=pl.CostEstimate(flops=flops, bytes_accessed=flops // 2, transcendentals=0),
        **extra,
    )


class Pick:
    def __init__(self, flag, yes, no):
        self.flag, self.yes, self.no = flag, yes, no

    def __getitem__(self, at):
        return jnp.where(self.flag, self.yes[at], self.no[at])


class Post:
    def __init__(self, even, s0, s1):
        self.even, self.s0, self.s1 = even, s0, s1

    def put(self, at, up, down):
        self.s0[at] = jnp.where(self.even, up, down)
        self.s1[at] = jnp.where(self.even, down, up)

    def both(self, at, value):
        self.s0[at] = value
        self.s1[at] = value


def received(even, r0, r1):
    return Pick(even, r1, r0), Pick(even, r0, r1)


def k1(w, g, cshift, h, s1, s0):
    post = Post(lax.axis_index("core") == 0, s0, s1)
    h[...] = jnp.zeros((2, 8, 128), jnp.float32)
    for x in range(2):
        h[x, 2:6, :] = 1.0 / (6.0 + cshift[x])
    rows = lambda k: (slice(16 * k, 16 * k + 16), slice(None))
    post.put(rows(0), w[6], w[0])
    post.put(rows(1), w[7], w[1])
    post.put(rows(2), g[7], g[0])
    post.put((slice(48, 56), slice(0, 128)), h[1], h[0])
    post.both((slice(48, 56), slice(128, 512)), jnp.zeros((8, 384), jnp.float32))


def plane(own, sides, field, p):
    if 0 <= p < 8:
        return lambda a, b: own[field][p, a:b, :]
    side, which, base, lane = PLANES[field, p]
    ref = sides[side][which]
    return lambda a, b: ref[base + a:base + b, lane:lane + 512]


def pack_rows(rows, own, sides, post):
    for k, (field, d, p) in enumerate(rows):
        read = plane(own, sides, field, p)
        post.put((slice(k, k + 1), slice(None)), read(16 - d, 17 - d), read(d - 1, d))


def k2(w, g, x1, x0, h, inverse, s0, s1):
    lo, hi = received(lax.axis_index("core") == 0, x0, x1)
    post = Post(lax.rem(lax.axis_index("grp"), 2) == 0, s0, s1)
    pack_rows(NEAR, {"w": w, "g": g}, {"lo": (lo,), "hi": (hi,)}, post)
    post.both((slice(26, 32), slice(None)), jnp.zeros((6, 512), jnp.float32))
    for x in range(2):
        post.both((slice(26, 30), slice(128 * x, 128 * x + 128)), h[x, 2:6, :])
    for half in range(2):
        piece = inverse[32 * half:32 * half + 32, :]
        at = (slice(32, 64), slice(256 * half, 256 * half + 256))
        post.put(at, piece[:, 256:512], piece[:, 0:256])


def fine_sum(ref, p, first, last):
    c = ref[p]
    total = ref[p - 1] + ref[p + 1]
    total = total + pltpu.roll(c, 1, 0) + pltpu.roll(c, TALL - 1, 0)
    total = total + jnp.where(first, 0.0, pltpu.roll(c, 1, 1))
    return total + jnp.where(last, 0.0, pltpu.roll(c, 511, 1))


def edges(dims):
    lane = lax.broadcasted_iota(jnp.int32, dims, 1)
    return lane == 0, lane == dims[1] - 1


def line_sides(c, first, last):
    total = jnp.where(first, 0.0, pltpu.roll(c, 1, 1))
    return total + jnp.where(last, 0.0, pltpu.roll(c, 127, 1))


def column_sides(c):
    return pltpu.roll(c, 1, 0) + pltpu.roll(c, 7, 0)


def fill(wide, own, sides, messages):
    zero = jnp.zeros((TOP, 512), jnp.float32)
    for field in ("w", "g"):
        out = wide[field]
        for i in range(14):
            p = i - 3
            out[i, 0:TOP, :] = zero
            out[i, TOP + 16:TALL, :] = zero
            known = 0 <= p < 8 or ((field, p) in PLANES and PLANES[field, p][1] < len(sides["lo"]))
            out[i, TOP:TOP + 16, :] = plane(own, sides, field, p)(0, 16) if known else jnp.zeros((16, 512), jnp.float32)
    for rows, lo, hi in messages:
        for k, (field, d, p) in enumerate(rows):
            wide[field][p + 3, TOP - d:TOP + 1 - d, :] = lo[k:k + 1]
            wide[field][p + 3, TOP + 15 + d:TOP + 16 + d, :] = hi[k:k + 1]


def exact_dot(x, chosen):
    rest, parts = x, []
    for _ in range(3):
        part = rest.astype(jnp.bfloat16)
        parts.append(part)
        rest = rest - part.astype(jnp.float32)
    y = jnp.dot(
        jnp.concatenate(parts, axis=0), chosen.astype(jnp.float32).astype(jnp.bfloat16),
        preferred_element_type=jnp.float32,
    )
    n = x.shape[0]
    return y[0:n] + (y[n:2 * n] + y[2 * n:3 * n])


def restricted(sums):
    cell = lax.broadcasted_iota(jnp.int32, (512, 128), 0)
    agg = lax.broadcasted_iota(jnp.int32, (512, 128), 1)
    return exact_dot(sums, cell // 4 == agg)


def row_sum(planes, p, first, last, top, bottom):
    c = planes(p)
    total = planes(p - 1) + planes(p + 1)
    total = total + jnp.where(top, 0.0, pltpu.roll(c, 1, 0)) + jnp.where(bottom, 0.0, pltpu.roll(c, 15, 0))
    total = total + jnp.where(first, 0.0, pltpu.roll(c, 1, 1))
    return total + jnp.where(last, 0.0, pltpu.roll(c, 511, 1))


def k2b(w, g, x1, x0, part, r, rim, V):
    lo, hi = received(lax.axis_index("core") == 0, x0, x1)
    own, sides = {"w": w, "g": g}, {"lo": (lo,), "hi": (hi,)}
    ws = lambda p: plane(own, sides, "w", p)(0, 16)
    gs = lambda p: plane(own, sides, "g", p)(0, 16)
    first, last = edges((16, 512))
    row = lax.broadcasted_iota(jnp.int32, (16, 512), 0)
    top, bottom = row == 0, row == 15
    for p in range(-1, 9):
        V[p + 1] = (alpha - beta) * ws(p) + (beta * gs(p)) * row_sum(ws, p, first, last, top, bottom)
    vs = lambda p: V[p + 1]
    sums = []
    for x in range(2):
        total = None
        for p in range(4 * x, 4 * x + 4):
            s = jnp.where(g[p] > 0.0, row_sum(vs, p, first, last, top, bottom), 0.0) + part[p]
            total = s if total is None else total + s
        sums.append(total)
    thin = restricted(jnp.concatenate(sums, axis=0))
    thin = thin + pltpu.roll(thin, 31, 0)
    thin = thin + pltpu.roll(thin, 30, 0)
    two = jnp.zeros((2, 128), jnp.float32)
    for x in range(2):
        rows = [thin[k:k + 1] for k in range(16 * x, 16 * x + 16, 4)]
        r[x] = jnp.concatenate([two] + rows + [two], axis=0)
    for side, at, inner in ((0, 0, 1), (1, 15, 14)):
        base = 40 * side
        rim[base + 34:base + 40] = jnp.zeros((6, 512), jnp.float32)
        for p in range(8):
            rim[base + p:base + p + 1] = w[p, at:at + 1, :]
            rim[base + 8 + p:base + 9 + p] = g[p, inner:inner + 1, :]
            rim[base + 16 + p:base + 17 + p] = g[p, at:at + 1, :]
        for k, p in enumerate(range(-1, 9)):
            rim[base + 24 + k:base + 25 + k] = plane(own, sides, "g", p)(at, at + 1)


def k3(w, g, x1, x0, y1, y0, h, r0, rim, inverse, L, T, u, s1, D):
    even = lax.axis_index("core") == 0
    xlo, xhi = received(even, x0, x1)
    ylo, yhi = received(lax.rem(lax.axis_index("grp"), 2) == 0, y0, y1)
    first, last = edges((8, 512))
    sums = []
    for side, ref in ((0, ylo), (1, yhi)):
        base = 40 * side
        D[side, 0:10, :] = beta * rim[base + 24:base + 34] * ref[0:10]
        w1, w2, g1 = ref[1:9], ref[10:18], ref[18:26]
        near = w2 + rim[base:base + 8] + ref[0:8] + ref[2:10]
        near = near + jnp.where(first, 0.0, pltpu.roll(w1, 1, 1)) + jnp.where(last, 0.0, pltpu.roll(w1, 511, 1))
        d = D[side, 1:9, :]
        s = (alpha - beta) * w1 + (beta * g1) * near + D[side, 0:8, :] + D[side, 2:10, :]
        s = s + jnp.where(first, 0.0, pltpu.roll(d, 1, 1)) + jnp.where(last, 0.0, pltpu.roll(d, 511, 1))
        inner = jnp.where(rim[base + 8:base + 16] > 0.0, d, 0.0)
        sums.append(jnp.where(rim[base + 16:base + 24] > 0.0, s, 0.0) + inner)
    thin = restricted(jnp.concatenate(sums, axis=0))
    thin = thin + pltpu.roll(thin, 15, 0)
    thin = thin + pltpu.roll(thin, 14, 0)
    four = lax.broadcasted_iota(jnp.int32, (8, 128), 0)
    r = []
    for x in range(2):
        below = jnp.broadcast_to(thin[4 * x:4 * x + 1], (8, 128))
        above = jnp.broadcast_to(thin[8 + 4 * x:9 + 4 * x], (8, 128))
        r.append(r0[x] + jnp.where(four == 2, below, jnp.where(four == 5, above, 0.0)))
    first, last = edges((8, 128))
    lo, hi = xlo[48:56, 0:128], xhi[48:56, 0:128]
    hx = (lo + h[1], h[0] + hi)
    us, hs = [], []
    for x in range(2):
        us.append(r[x] * h[x])
        below = jnp.broadcast_to(ylo[29:30, 128 * x:128 * x + 128], (8, 128))
        above = jnp.broadcast_to(yhi[26:27, 128 * x:128 * x + 128], (8, 128))
        hs.append(jnp.where(four == 1, below, jnp.where(four == 6, above, h[x])))
        u[x] = us[x]
    q = jnp.zeros((8, 128), jnp.float32)
    flat = []
    for x in range(2):
        side = line_sides(us[x], first, last) + column_sides(us[x])
        q = q + (alpha - beta) * us[x] + beta * (hx[x] * us[x] + hs[x] * side)
        flat.append((alpha - beta) * us[x] + beta * hs[x] * (us[1 - x] + side))
    total = 2.0 * q + line_sides(q, first, last) + column_sides(q) + (1.0 - alpha) * (r[0] + r[1])
    total = total - jnp.where(jnp.broadcast_to(lo[2:3], (8, 128)) > 0.0, 0.0, flat[0])
    total = total - jnp.where(jnp.broadcast_to(hi[2:3], (8, 128)) > 0.0, 0.0, flat[1])
    for i in range(64):
        L[i] = total
    T[0:64, 256:768] = inverse[...]
    for half in range(2):
        rows, lanes = slice(32 * half, 32 * half + 32), slice(256 * half, 256 * half + 256)
        T[rows, 0:256] = ylo[32:64, lanes]
        T[rows, 768:1024] = yhi[32:64, lanes]
    post = Post(even, T.at[64:88], s1)
    post.put((slice(0, 16), slice(0, 512)), w[5], w[2])
    post.put((slice(0, 16), slice(512, 1024)), g[6], g[1])
    tiles = slice(16, 24)
    post.both((tiles, slice(0, 128)), us[0])
    post.both((tiles, slice(128, 256)), us[1])
    post.put((tiles, slice(256, 384)), h[1], h[0])
    post.both((tiles, slice(384, 1024)), jnp.zeros((8, 640), jnp.float32))


def k4(w, g, x1, x0, u, h, f1, mate, s0, s1):
    even = lax.axis_index("core") == 0
    lo, hi = received(even, x0, x1)
    flo, fhi = received(even, mate.at[64:88], f1)
    post = Post(lax.rem(lax.axis_index("grp"), 2) == 0, s0, s1)
    pack_rows(FAR, {"w": w, "g": g}, {"lo": (lo,), "hi": (hi,)}, post)
    post.both((slice(22, 24), slice(None)), jnp.zeros((2, 512), jnp.float32))
    tiles = [u[0], u[1], h[0], h[1]]
    for ref in (flo, fhi):
        tiles += [ref[16:24, 128 * k:128 * k + 128] for k in range(4)]
    for k, t in enumerate(tiles):
        row, lane = 24 + 8 * (k // 4), 128 * (k % 4)
        post.both((slice(row, row + 8), slice(lane, lane + 128)), t)


def k5(lines, own, mate, out):
    s = [lines[i] for i in range(8)]
    for i in range(8, 64):
        s[i % 8] = s[i % 8] + lines[i]
    while len(s) > 1:
        s = [a + b for a, b in zip(s[::2], s[1::2])]
    s = s[0]
    tables = []
    for ref in (own, mate):
        t = ref[0:64, 0:128] * s[0:1]
        for k in range(1, 8):
            t = t + ref[0:64, 128 * k:128 * k + 128] * s[k:k + 1]
        tables.append(t)
    even = lax.axis_index("core") == 0
    table = jnp.concatenate([jnp.where(even, *tables), jnp.where(even, *tables[::-1])], axis=0)
    y = jnp.broadcast_to(jnp.sum(table.T, axis=0, keepdims=True), (8, 128))
    for i in range(32):
        out[8 * i:8 * i + 8] = y


def spread(tiles):
    cell = lax.broadcasted_iota(jnp.int32, (128, 512), 1)
    agg = lax.broadcasted_iota(jnp.int32, (128, 512), 0)
    z = exact_dot(tiles, cell // 4 == agg)
    upper = lax.broadcasted_iota(jnp.int32, (8, 512), 0) < 4
    planes = []
    for k in range(0, tiles.shape[0], 8):
        parts = []
        for t in range(k + 1, k + 7, 2):
            a = jnp.broadcast_to(z[t:t + 1], (8, 512))
            b = jnp.broadcast_to(z[t + 1:t + 2], (8, 512))
            parts.append(jnp.where(upper, a, b))
        planes.append(jnp.concatenate(parts, axis=0))
    return planes


def k6(w, g, x0, x1, y0, y1, mate, f1, v1, v0, u, h, A, W, G):
    even, row_even = lax.axis_index("core") == 0, lax.rem(lax.axis_index("grp"), 2) == 0
    xlo, xhi = received(even, x0, x1)
    flo, fhi = received(even, mate.at[64:88], f1)
    ylo, yhi = received(row_even, y0, y1)
    vlo, vhi = received(row_even, v0, v1)
    own = {"w": w, "g": g}
    fill({"w": W, "g": G}, own, {"lo": (xlo, flo), "hi": (xhi, fhi)}, [(NEAR, ylo, yhi), (FAR, vlo, vhi)])
    four = lax.broadcasted_iota(jnp.int32, (8, 128), 0)
    first, last = edges((8, 128))

    def tile(mine, k):
        row, lane = 24 + 8 * (k // 4), 128 * (k % 4)
        below = pltpu.roll(vlo[row:row + 8, lane:lane + 128], 4, 0)
        above = pltpu.roll(vhi[row:row + 8, lane:lane + 128], 4, 0)
        return jnp.where(four < 2, below, jnp.where(four > 5, above, mine))

    far = [[ref[16:24, 128 * k:128 * k + 128] for k in range(3)] for ref in (flo, fhi)]
    us = [tile(far[0][0], 4), tile(far[0][1], 5), tile(u[0], 0), tile(u[1], 1), tile(far[1][0], 8), tile(far[1][1], 9)]
    hs = [tile(far[0][2], 6), tile(h[0], 2), tile(h[1], 3), tile(far[1][2], 10)]
    for x in range(4):
        c = us[x + 1]
        s = us[x] + us[x + 2] + line_sides(c, first, last) + column_sides(c)
        A[34, 0:8, 128 * x:128 * x + 128] = alpha * c + beta * hs[x] * s
    first, last = edges((TALL, 512))
    for i in range(1, 13):
        A[i + 21] = alpha * W[i] + (beta * G[i]) * fine_sum(W, i, first, last)
        A[i + 9] = G[i]
        if 2 <= i < 12:
            A[i - 2] = W[i]
    A[34, 8:TALL, :] = jnp.zeros((TALL - 8, 512), jnp.float32)


def k7(terms, A, rho, out, R, U0, U1, O, sems):
    fix = [jnp.zeros((1, 128), jnp.float32)]
    for j in range(-1, 5):
        k = jnp.clip(4 * lax.axis_index("grp") + j, 0, 31)
        fix.append(jnp.sum(terms[pl.ds(pl.multiple_of(8 * k, 8), 8), :], axis=0, keepdims=True))
    fix = jnp.concatenate(fix + [jnp.zeros((1, 128), jnp.float32)], axis=0)
    pro = spread(jnp.concatenate([A[34, 0:8, 128 * x:128 * x + 128] + fix for x in range(4)], axis=0))
    first, last = edges((TALL, 512))
    for p in range(8):
        R[p, 0:TOP, :] = jnp.zeros((TOP, 512), jnp.float32)
        R[p, TOP:TOP + 16, :] = rho[p]
        R[p, TOP + 16:TALL, :] = jnp.zeros((TOP, 512), jnp.float32)
    for i in range(1, 13):
        U0[i] = A[i + 21] + jnp.where(A[i + 9] > 0.0, pro[(i + 1) // 4], 0.0)
    for i in range(2, 12):
        U1[i] = (1.0 - c1) * U0[i] + c1 * (A[i - 2] + A[i + 9] * fine_sum(U0, i, first, last))
    copies = []
    for p in range(8):
        i = p + 3
        gp = A[i + 9]
        solid = ((1.0 - c1) * alpha + c1) * R[p] + (1.0 - c1) * pro[p // 4 + 1]
        mid = jnp.where(gp > 0.0, U1[i], solid)
        new = (1.0 - c2) * mid + c2 * (R[p] + gp * fine_sum(U1, i, first, last))
        O[p] = new[TOP:TOP + 16]
        copies.append(pltpu.make_async_copy(O.at[p], out.at[p], sems.at[p]))
        copies[-1].start()
    for c in copies:
        c.wait()


def swaps(s0, s1, axis, order):
    count, sent, got = lax.axis_size(axis), (s0, s1), [None, None]
    for parity in order:
        pairs = []
        for i in range(parity, count - 1, 2):
            pairs += [(i, i + 1), (i + 1, i)]
        got[parity] = lax.ppermute(sent[parity], axis, pairs)
    return got


def shards(rhs, shift, mask, cshift, inverse):
    field, coarse = shape(8, 16, 512), shape(2, 8, 128)
    wide = pltpu.VMEM((14, TALL, 512), jnp.float32)

    def kernel(name, body, outs, scratch, *args, flops=0, **extra):
        with jax.named_scope(name):
            return call(body, outs, scratch, flops=flops, **extra)(*args)

    inv = 1.0 / (6.0 + shift)
    fluid = mask.astype(jnp.float32)
    rho = rhs * inv
    g = fluid * inv
    w = fluid * rho
    part = (1.0 - alpha) * rhs
    h, s1, s0 = kernel("edges", k1, [coarse, shape(56, 512), shape(56, 512)], [], w, g, cshift)
    x0, x1 = swaps(s0, s1, AGG, (1, 0))
    s0, s1 = kernel("near_rows", k2, [shape(64, 512)] * 2, [], w, g, x1, x0, h, inverse)
    y0, y1 = swaps(s0, s1, "grp", (1, 0))
    r0, rim = kernel(
        "own_residual", k2b, [coarse, shape(80, 512)], [pltpu.VMEM((10, 16, 512), jnp.float32)],
        w, g, x1, x0, part, flops=3000000,
    )
    lines, table, u, s1 = kernel(
        "residual", k3, [shape(64, 8, 128), shape(88, 1024), coarse, shape(24, 1024)],
        [pltpu.VMEM((2, 16, 512), jnp.float32)], w, g, x1, x0, y1, y0, h, r0, rim, inverse,
    )
    lines = lax.all_to_all(lines, AGG, 0, 0)
    mate, f1 = swaps(table, s1, AGG, (1, 0))
    lines, mate, f1 = lax.optimization_barrier((lines, mate, f1))
    part = kernel("line_product", k5, shape(256, 128), [], lines, table, mate)
    terms = lax.all_to_all(part.reshape(256, 1, 128), ROW, 0, 0).reshape(256, 128)
    s0, s1 = kernel("far_rows", k4, [shape(48, 512)] * 2, [], w, g, x1, x0, u, h, f1, mate, flops=200000)
    v0, v1 = swaps(s0, s1, "grp", (1, 0))
    own = pltpu.VMEM((8, 16, 512), jnp.float32)
    known = kernel(
        "presmooth", k6, shape(35, TALL, 512), [wide, wide],
        w, g, x0, x1, y0, y1, mate, f1, v1, v0, u, h, flops=4000000,
    )
    return kernel(
        "postsmooth", k7, field,
        [pltpu.VMEM((8, TALL, 512), jnp.float32), wide, wide, own, pltpu.SemaphoreType.DMA((8,))],
        terms, known, rho, out_specs=pl.BlockSpec(memory_space=pl.ANY),
    )


def solution(mesh):
    finer = Mesh(mesh.devices.reshape(4, 2, 4, 2, 8), AGG + ("grp",))
    cells = P(AGG, "grp", None)
    return jax.shard_map(
        shards, mesh=finer, in_specs=(cells, cells, cells, cells, P(AGG, "grp")), out_specs=cells,
        check_vma=False,
    )
```
